32 devices in a mesh: row: 32 (over z, y, x, core).
Axes of the slice: x: 2, y: 2, z: 4, core: 2. Of those that a mesh axis runs over, the one named last changes fastest.
Arguments:
- row_ids: int32 [4096, 26, 30], P('row'), may hold values from 0 to 16383, as said below
- hot_counts: int32 [4096, 26], P('row'), may hold values from 1 to 30, as said below
- dense_feats: float32 [4096, 13], P('row'), may hold values from -6 to 6
- click_labels: int32 [4096], P('row'), may hold values 0 or 1
- block_owners: int32 [240], replicated, may hold values from 0 to 383, as said below
- embed_table: float32 [26, 16384, 128], P(None, 'row'), may hold values from -1.5 to 1.5
- table_moment: float32 [26, 16384, 128], P(None, 'row'), may hold values from -2.3834774e-09 to 2.3834774e-09
- table_square: float32 [26, 16384, 128], P(None, 'row'), may hold values from 2.9343825e-20 to 1.173753e-19
- dense_slots: float32 [384, 128, 512], P('row'), may hold values from -0.13258252 to 0.13258252
- dense_moment: float32 [384, 128, 512], P('row'), may hold values from -1.1094483e-07 to 1.1094483e-07
- dense_square: float32 [384, 128, 512], P('row'), may hold values from 6.3578286e-17 to 2.5431315e-16
- dense_proj: float32 [13, 128], replicated, may hold values from -1.75 to 1.75
- proj_moment: float32 [13, 128], replicated, may hold values from -2.2188966e-07 to 2.2188966e-07
- proj_square: float32 [13, 128], replicated, may hold values from 2.5431316e-17 to 1.0172526e-16
- head_weight: float32 [512], replicated, may hold values from -0.25 to 0.25
- head_moment: float32 [512], replicated, may hold values from -3.328345e-06 to 3.328345e-06
- head_square: float32 [512], replicated, may hold values from 5.722046e-14 to 2.2888183e-13
- biases: float32 [13057], replicated, may hold values from -1.8 to 1.8
- bias_moment: float32 [13057], replicated, may hold values from -2.2188966e-07 to 2.2188966e-07
- bias_square: float32 [13057], replicated, may hold values from 2.5431315e-16 to 1.0172526e-15
Outputs:
- loss_total: float32 [], replicated
- grad_norm: float32 [], replicated
- table_out: float32 [26, 16384, 128], P(None, 'row')
- table_moment_out: float32 [26, 16384, 128], P(None, 'row')
- table_square_out: float32 [26, 16384, 128], P(None, 'row')
- dense_out: float32 [384, 128, 512], P('row')
- dense_moment_out: float32 [384, 128, 512], P('row')
- dense_square_out: float32 [384, 128, 512], P('row')
- proj_out: float32 [13, 128], replicated
- proj_moment_out: float32 [13, 128], replicated
- proj_square_out: float32 [13, 128], replicated
- head_out: float32 [512], replicated
- head_moment_out: float32 [512], replicated
- head_square_out: float32 [512], replicated
- bias_out: float32 [13057], replicated
- bias_moment_out: float32 [13057], replicated
- bias_square_out: float32 [13057], replicated
The draws below stay inside these ranges and needn't reach their ends.
Inputs may be any that keep to these rules, and one draw needn't show every extreme that they name: `hot_counts`: each sample's counts over its 26 features sum to 403. `row_ids`: ids index rows of their feature's table. Of the live slots (j below the count) of the 128 samples of each device, exactly 1612 have ids in the rows [d * 512, (d + 1) * 512) of each device d. `block_owners`: distinct values; value p names slot p % 12 of device p // 12; some device owns 12 blocks.
All inputs are finite; a program needn't handle non-finite values. No bound on the sum of `click_labels` on one device may be relied on, other than what follows from the above.
Results may differ from the reference program's by a relative error of at most 0.013.
Values may be sent and summed in bfloat16 or wider, within the bound.
A program may use at most 384 MiB of HBM per device.

```python
import math
import jax
import jax.numpy as jnp
from jax import lax

F = 26
NDENSE = 13
HOT = 30
EMB = 128
RANK = 512
LAYERS = 3
H1 = 1024
H2 = 1024
H3 = 512
SAMP_DEV = 128
ROWS_DEV = 512
BR = 128
STEP = 10
WIDTH = 3456
TOTAL = 403
BATCH = 4096
ROWS = 16384
NBLK = 240
SLOTS = 12
NBIAS = 13057
N_ROW = 32


def shared_counts(key):
    halves = jax.random.randint(jax.random.fold_in(key, 11), (BATCH, F // 2), 1, HOT + 1)
    halves = halves.at[0, 0].set(HOT)
    paired = jnp.concatenate([halves, HOT + 1 - halves], axis=1)
    scores = jax.random.randint(jax.random.fold_in(key, 12), (BATCH, F), 0, 1 << 20) * F
    scores = scores + jnp.arange(F, dtype=jnp.int32)[None, :]
    ordering = jnp.argsort(scores, axis=1)
    return jnp.take_along_axis(paired, ordering, axis=1).astype(jnp.int32)


def draw_hot_counts(key, part):
    counts = shared_counts(key)
    return counts


def draw_row_ids(key, part):
    counts = shared_counts(key)
    key = jax.random.fold_in(key, 2)
    live_mask = lax.broadcasted_iota(jnp.int32, (BATCH, F, HOT), 2) < counts[:, :, None]
    live_mask = live_mask.reshape(N_ROW, SAMP_DEV * F * HOT)
    live_rank = jnp.cumsum(live_mask.astype(jnp.int32), axis=1) - 1
    live_rank = jnp.clip(live_rank, 0, SAMP_DEV * TOTAL - 1)
    subkeys = jax.random.split(jax.random.fold_in(key, 21), N_ROW)
    spread = jax.vmap(lambda subkey: jax.random.permutation(subkey, SAMP_DEV * TOTAL))(subkeys)
    live_owner = jnp.take_along_axis(spread.astype(jnp.int32), live_rank, axis=1) % N_ROW
    spare_owner = jax.random.randint(jax.random.fold_in(key, 22), live_mask.shape, 0, N_ROW)
    owner_dev = jnp.where(live_mask, live_owner, spare_owner)
    offset = jax.random.randint(jax.random.fold_in(key, 23), live_mask.shape, 0, ROWS_DEV)
    return (owner_dev * ROWS_DEV + offset).reshape(BATCH, F, HOT).astype(jnp.int32)


def draw_block_owners(key, part):
    key = jax.random.fold_in(key, 3)
    levels = jax.random.randint(jax.random.fold_in(key, 31), (N_ROW,), 0, 4)
    levels = levels.at[jax.random.randint(jax.random.fold_in(key, 32), (), 0, N_ROW)].set(0)
    places = jnp.arange(N_ROW * SLOTS, dtype=jnp.int32)
    device = places // SLOTS
    device_rank = jax.random.permutation(jax.random.fold_in(key, 33), N_ROW).astype(jnp.int32)
    priority = levels[device] * (N_ROW * SLOTS) + device_rank[device] * SLOTS + places % SLOTS
    chosen = places[jnp.argsort(priority)][:NBLK]
    return chosen[jax.random.permutation(jax.random.fold_in(key, 34), NBLK)].astype(jnp.int32)


def plant(entries, own_key, least, high):
    longest = entries.shape.index(max(entries.shape))
    spots = []
    for shift in (0, 1):
        where = [jax.random.randint(jax.random.fold_in(own_key, axis), (), 0, length) for axis, length in enumerate(entries.shape)]
        where[longest] = (where[longest] + shift) % entries.shape[longest]
        spots.append(tuple(where))
    return entries.at[spots[0]].set(least).at[spots[1]].set(high)


def steps_of(key, extent, pieces, least, largest):
    level = 1.0
    for dim, parts in pieces:
        steps = jax.random.uniform(jax.random.fold_in(jax.random.fold_in(key, 6), dim), (parts,), jnp.float32, least / len(pieces), largest / len(pieces))
        level = level * jnp.repeat(jnp.exp(steps), extent[dim] // parts).reshape((-1,) + (1,) * (len(extent) - 1 - dim))
    return level


def bell_draw(stream_key, shape, width, most, cuts=(), kind=jnp.bfloat16):
    drawn = width * jax.random.normal(stream_key, shape, jnp.float32)
    if cuts:
        drawn = drawn * steps_of(stream_key, shape, cuts, -0.22, 0.18)
    return jnp.clip(drawn, -most, most).astype(kind)


def setup_inputs(seed: int = 0) -> dict:
    key_list = jax.random.split(jax.random.key(seed), 21)
    return {
        "row_ids": draw_row_ids(jax.random.fold_in(key_list[20], 71), 0),
        "hot_counts": draw_hot_counts(jax.random.fold_in(key_list[20], 71), 0),
        "dense_feats": bell_draw(key_list[2], (BATCH, NDENSE), 1.0, 6.0, ((0, 32),), jnp.float32),
        "click_labels": plant((jax.random.randint(key_list[3], (BATCH,), 0, 2) < 1).astype(jnp.int32), jax.random.fold_in(key_list[3], 1), 0, 1),
        "block_owners": draw_block_owners(jax.random.fold_in(key_list[20], 71), 0),
        "embed_table": bell_draw(key_list[5], (F, ROWS, EMB), 0.25, 1.5, ((1, 32),), jnp.float32),
        "table_moment": bell_draw(key_list[6], (F, ROWS, EMB), (0.0000044 * (F * ROWS * EMB) ** -0.5), 2.383477415435209e-09, ((1, 32),), jnp.float32),
        "table_square": jnp.clip(jnp.exp(math.log(1.1737530040944366e-19) - 1.3862944 * jax.random.uniform(key_list[7], (F, ROWS, EMB), jnp.float32) ** steps_of(key_list[7], (F, ROWS, EMB), ((1, 32),), -0.2, 0.2)), 2.9343825102360916e-20, 1.1737530040944366e-19),
        "dense_slots": bell_draw(key_list[8], (N_ROW * SLOTS, BR, RANK), ((4 * RANK) ** -0.5), 0.13258252, ((0, 32),), jnp.float32),
        "dense_moment": bell_draw(key_list[9], (N_ROW * SLOTS, BR, RANK), (0.00011 * (NBLK * BR * RANK) ** -0.5), 1.1094483198803573e-07, ((0, 32),), jnp.float32),
        "dense_square": jnp.clip(jnp.exp(math.log(2.5431314561385153e-16) - 1.3862944 * jax.random.uniform(key_list[10], (N_ROW * SLOTS, BR, RANK), jnp.float32) ** steps_of(key_list[10], (N_ROW * SLOTS, BR, RANK), ((0, 32),), -0.2, 0.2)), 6.357828640346288e-17, 2.5431314561385153e-16),
        "dense_proj": bell_draw(key_list[11], (NDENSE, EMB), NDENSE ** -0.5, 1.75, (), jnp.float32),
        "proj_moment": bell_draw(key_list[12], (NDENSE, EMB), (0.00022 * (NBLK * BR * RANK) ** -0.5), 2.2188966397607146e-07, (), jnp.float32),
        "proj_square": jnp.clip(jnp.exp(jax.random.uniform(key_list[13], (NDENSE, EMB), jnp.float32, math.log(2.5431315554001888e-17), math.log(1.0172526221600755e-16))), 2.5431315554001888e-17, 1.0172526221600755e-16),
        "head_weight": bell_draw(key_list[14], (H3,), H3 ** -0.5, 0.25, (), jnp.float32),
        "head_moment": bell_draw(key_list[15], (H3,), (0.0033 * (NBLK * BR * RANK) ** -0.5), 3.3283449738519266e-06, (), jnp.float32),
        "head_square": jnp.clip(jnp.exp(jax.random.uniform(key_list[16], (H3,), jnp.float32, math.log(5.722045694255343e-14), math.log(2.288818277702137e-13))), 5.722045694255343e-14, 2.288818277702137e-13),
        "biases": bell_draw(key_list[17], (NBIAS,), 0.3, 1.8, (), jnp.float32),
        "bias_moment": bell_draw(key_list[18], (NBIAS,), (0.00022 * (NBLK * BR * RANK) ** -0.5), 2.2188966397607146e-07, (), jnp.float32),
        "bias_square": jnp.clip(jnp.exp(jax.random.uniform(key_list[19], (NBIAS,), jnp.float32, math.log(2.5431314561385153e-16), math.log(1.0172525824554061e-15))), 2.5431314561385153e-16, 1.0172525824554061e-15),
    }


@jax.custom_vjp
def low(v):
    return lax.optimization_barrier(v.astype(jnp.bfloat16)).astype(jnp.float32)

@jax.custom_vjp
def low_back(v):
    return v

def low_keep(v):
    return (low(v), None)

def low_pass(kept, grad):
    return (grad,)

def back_keep(v):
    return (v, None)

def back_low(kept, grad):
    return (low(grad),)
low.defvjp(low_keep, low_pass)
low_back.defvjp(back_keep, back_low)
beta_one = 0.9
beta_two = 0.999
adam_eps = 1e-12
decay_rate = 0.01
clip_norm = 0.001
rate_table = 0.3
rate_dense = 0.03
rate_small = 0.1

def product(left, right):
    return jnp.dot(left, right, precision=lax.Precision.HIGHEST, preferred_element_type=jnp.float32)

def split_dense(flat):
    cross_rows = LAYERS * WIDTH
    first = 2 * cross_rows + WIDTH * H1 // RANK
    second = first + H1 * H2 // RANK
    return (flat[:cross_rows].reshape(LAYERS, WIDTH, RANK), flat[cross_rows:2 * cross_rows].reshape(LAYERS, WIDTH, RANK), flat[2 * cross_rows:first].reshape(WIDTH, H1), flat[first:second].reshape(H1, H2), flat[second:second + H2 * H3 // RANK].reshape(H2, H3))

def split_bias(biases):
    start = EMB + LAYERS * WIDTH
    return (biases[:EMB], biases[EMB:start].reshape(LAYERS, WIDTH), biases[start:start + H1], biases[start + H1:start + H1 + H2], biases[start + H1 + H2:start + H1 + H2 + H3], biases[NBIAS - 1])

def forward(params, row_ids, hot_counts, dense_feats, click_labels, block_owners):
    embed_table, dense_slots, dense_proj, head_weight, biases = params
    rounded = low(embed_table)
    features = jnp.arange(F, dtype=jnp.int32)[None, :, None]

    def pool_block(inputs):
        block_ids, block_counts = inputs
        live_mask = (lax.broadcasted_iota(jnp.int32, block_ids.shape, 2) < block_counts[:, :, None]).astype(jnp.float32)
        gathered = rounded[features, block_ids]
        return lax.optimization_barrier(jnp.sum(gathered * live_mask[..., None], axis=2))
    pooled = lax.map(jax.checkpoint(pool_block), (row_ids.reshape(N_ROW, SAMP_DEV, F, HOT), hot_counts.reshape(N_ROW, SAMP_DEV, F)))
    pooled = low(low_back(pooled.reshape(BATCH, F * EMB)))
    bias_dense, bias_cross, bias_one, bias_two, bias_three, bias_last = split_bias(biases)
    anchor = jnp.concatenate([product(dense_feats, dense_proj) + bias_dense, pooled], axis=1)
    cross_down, cross_up, first_matrix, middle, third_matrix = split_dense(low(dense_slots[block_owners]).reshape(NBLK * BR, RANK))
    current = anchor
    for depth in range(LAYERS):
        reduced = low(low_back(product(low(current), cross_down[depth])))
        mixing = low_back(product(reduced, cross_up[depth].T)) + bias_cross[depth]
        current = anchor * mixing + current
    hidden = jax.nn.gelu(low_back(product(low(current), first_matrix)) + bias_one)
    hidden = jax.nn.gelu(low_back(product(low(hidden), middle)) + bias_two)
    hidden = jax.nn.gelu(low_back(product(low(hidden), third_matrix)) + bias_three)
    logits = product(hidden, head_weight) + bias_last
    labels = click_labels.astype(jnp.float32)
    loss_total = jnp.sum(jax.nn.softplus(logits) - labels * logits)
    return (loss_total / BATCH, loss_total)

def adamw(weight, moment, square, gradient, step_rate):
    moment = beta_one * moment + (1 - beta_one) * gradient
    square = beta_two * square + (1 - beta_two) * gradient * gradient
    corrected = moment / (1 - beta_one ** STEP)
    scaled = square / (1 - beta_two ** STEP)
    weight = weight - step_rate * (corrected / (jnp.sqrt(scaled) + adam_eps) + decay_rate * weight)
    return (weight, moment, square)

def reference(row_ids, hot_counts, dense_feats, click_labels, block_owners, embed_table, table_moment, table_square, dense_slots, dense_moment, dense_square, dense_proj, proj_moment, proj_square, head_weight, head_moment, head_square, biases, bias_moment, bias_square):

    def objective(*params):
        return forward(params, row_ids, hot_counts, dense_feats, click_labels, block_owners)
    params = (embed_table, dense_slots, dense_proj, head_weight, biases)
    mean_loss, pullback, loss_total = jax.vjp(objective, *params, has_aux=True)
    gradients = pullback(jnp.ones_like(mean_loss))
    squares = jnp.float32(0.0)
    for gradient in gradients:
        squares = squares + jnp.sum(gradient * gradient)
    grad_norm = jnp.sqrt(squares)
    clip_scale = clip_norm / jnp.maximum(grad_norm, clip_norm)
    table_new = adamw(embed_table, table_moment, table_square, clip_scale * gradients[0], rate_table)
    dense_new = adamw(dense_slots, dense_moment, dense_square, clip_scale * gradients[1], rate_dense)
    proj_new = adamw(dense_proj, proj_moment, proj_square, clip_scale * gradients[2], rate_small)
    head_new = adamw(head_weight, head_moment, head_square, clip_scale * gradients[3], rate_small)
    bias_new = adamw(biases, bias_moment, bias_square, clip_scale * gradients[4], rate_small)
    return (loss_total, grad_norm, table_new[0], table_new[1], table_new[2], dense_new[0], dense_new[1], dense_new[2], proj_new[0], proj_new[1], proj_new[2], head_new[0], head_new[1], head_new[2], bias_new[0], bias_new[1], bias_new[2])
```

```python
import functools

import jax
import jax.numpy as jnp
from jax import lax
from jax.experimental import pallas as pl
from jax.experimental.pallas import tpu as pltpu
from jax.sharding import PartitionSpec as P

F = 26
HOT = 30
EMB = 128
RANK = 512
LAYERS = 3
H1 = 1024
H2 = 1024
H3 = 512
BR = 128
STEP = 10
WIDTH = 3456
TOTAL = 403
NBIAS = 13057


beta_one = 0.9
beta_two = 0.999
adam_eps = 1e-12
decay_rate = 0.01
clip_norm = 0.001
rate_table = 0.3
rate_dense = 0.03
rate_small = 0.1
highest = lax.Precision.HIGHEST


def split_dense(flat):
    cross_rows = LAYERS * WIDTH
    first = 2 * cross_rows + WIDTH * H1 // RANK
    second = first + H1 * H2 // RANK
    return (
        flat[:cross_rows].reshape(LAYERS, WIDTH, RANK),
        flat[cross_rows : 2 * cross_rows].reshape(LAYERS, WIDTH, RANK),
        flat[2 * cross_rows : first].reshape(WIDTH, H1),
        flat[first:second].reshape(H1, H2),
        flat[second : second + H2 * H3 // RANK],
    )


def split_bias(biases):
    start = EMB + LAYERS * WIDTH
    return (
        biases[:EMB],
        biases[EMB:start].reshape(LAYERS, WIDTH),
        biases[start : start + H1],
        biases[start + H1 : start + H1 + H2],
        biases[start + H1 + H2 : start + H1 + H2 + H3],
        biases[NBIAS - 1],
    )


def cross_forward(anchor, current, weight_down, weight_up, bias_term):
    current_low = current.astype(jnp.bfloat16)
    reduced = jnp.dot(current_low, weight_down, preferred_element_type=jnp.float32).astype(
        jnp.bfloat16
    )
    mixing = (
        jnp.einsum("sr,wr->sw", reduced, weight_up, preferred_element_type=jnp.float32) + bias_term
    )
    return ((current_low, reduced, mixing), anchor * mixing + current)


def cross_backward(anchor, stored, weight_down, weight_up, grad_current):
    current_low, reduced, mixing = stored
    grad_mixing = anchor * grad_current
    grad_mixing_low = grad_mixing.astype(jnp.bfloat16)
    grad_up = jnp.einsum("sw,sr->wr", grad_mixing_low, reduced, preferred_element_type=jnp.float32)
    grad_reduced = jnp.dot(grad_mixing_low, weight_up, preferred_element_type=jnp.float32).astype(
        jnp.bfloat16
    )
    grad_down = jnp.einsum(
        "sw,sr->wr", current_low, grad_reduced, preferred_element_type=jnp.float32
    )
    grad_prev = grad_current + jnp.einsum(
        "sr,wr->sw", grad_reduced, weight_down, preferred_element_type=jnp.float32
    )
    return (grad_prev, grad_current * mixing, grad_down, grad_up, jnp.sum(grad_mixing, axis=0))


def dense_forward(inputs, weight, bias_term):
    inputs_low = inputs.astype(jnp.bfloat16)
    before = jnp.dot(inputs_low, weight, preferred_element_type=jnp.float32) + bias_term
    return ((inputs_low, before), jax.nn.gelu(before))


def dense_backward(stored, weight, grad_out):
    inputs_low, before = stored
    unused, gelu_back = jax.vjp(jax.nn.gelu, before)
    grad_before = gelu_back(grad_out)[0]
    grad_low = grad_before.astype(jnp.bfloat16)
    grad_weight = jnp.einsum("sa,sb->ab", inputs_low, grad_low, preferred_element_type=jnp.float32)
    grad_inputs = jnp.einsum("sb,ab->sa", grad_low, weight, preferred_element_type=jnp.float32)
    return (grad_inputs, grad_weight, jnp.sum(grad_before, axis=0))


def table_gradient(arrived, served, table_rows):
    received = served.shape[0]
    window = min(512, received)
    order_back = jnp.argsort(served, stable=True)
    sorted_ids = jnp.take(served, order_back)
    edges = jnp.arange(F + 1, dtype=jnp.int32) * table_rows
    bounds = jnp.sum((sorted_ids[None, :] < edges[:, None]).astype(jnp.int32), axis=1)
    starts = bounds[:-1]
    finish = bounds[1:]
    windows = (finish - starts + window - 1) // window
    ends_cum = jnp.cumsum(windows)
    begins_cum = ends_cum - windows
    step_count = F + received // window + 1
    turns = jnp.arange(step_count, dtype=jnp.int32)
    feature_of = jnp.sum((ends_cum[None, :] <= turns[:, None]).astype(jnp.int32), axis=1)
    feature_safe = jnp.minimum(feature_of, F - 1)
    first_row = (
        jnp.take(starts, feature_safe) + (turns - jnp.take(begins_cum, feature_safe)) * window
    )
    row_index = first_row[:, None] + jnp.arange(window, dtype=jnp.int32)[None, :]
    row_valid = (feature_of < F)[:, None] & (row_index < jnp.take(finish, feature_safe)[:, None])
    row_safe = jnp.minimum(row_index, received - 1)
    window_grads = jnp.take(arrived, jnp.take(order_back, row_safe), axis=0)
    local_row = jnp.take(sorted_ids, row_safe) - feature_safe[:, None] * table_rows
    local_row = jnp.where(row_valid, local_row, -1)
    selector = (
        local_row[:, :, None] == jnp.arange(table_rows, dtype=jnp.int32)[None, None, :]
    ).astype(jnp.bfloat16)
    partial_sums = jnp.einsum(
        "swr,swe->sre", selector, window_grads, preferred_element_type=jnp.float32
    )
    feature_pick = (feature_of[:, None] == jnp.arange(F, dtype=jnp.int32)[None, :]).astype(
        jnp.float32
    )
    return jnp.einsum(
        "sf,sre->fre",
        feature_pick,
        partial_sums,
        precision=highest,
        preferred_element_type=jnp.float32,
    )


def adamw(weight, moment, square, gradient, step_rate):
    moment = beta_one * moment + (1 - beta_one) * gradient
    square = beta_two * square + (1 - beta_two) * gradient * gradient
    corrected = moment / (1 - beta_one**STEP)
    scaled = square / (1 - beta_two**STEP)
    weight = weight - step_rate * (corrected / (jnp.sqrt(scaled) + adam_eps) + decay_rate * weight)
    return (weight, moment, square)


def count_kernel(devices, samples, table_rows, off_ref, keys_ref, table_ref, counts_ref, partial_ref):
    feature = pl.program_id(0)
    low_table = table_ref[0].T.astype(jnp.bfloat16)
    lane = lax.broadcasted_iota(jnp.int32, (1, samples), 1)
    row_iota = lax.broadcasted_iota(jnp.int32, (table_rows, 2 * samples), 0)
    sample_iota = lax.broadcasted_iota(jnp.int32, (2 * samples, 2 * samples), 0)

    def window(source, turn):
        start = off_ref[source * (F + 1) + feature] + turn * samples
        stop = off_ref[source * (F + 1) + feature + 1]
        tile = start // samples
        base = pl.multiple_of(tile * samples, samples)
        piece = keys_ref[pl.ds(source, 1), pl.ds(base, 2 * samples)]
        turned = pltpu.roll(piece, 2 * samples - (start - base), 1)[:, :samples]
        valid = lane < stop - start
        row = jnp.where(valid, (turned >> 7) & (table_rows - 1), -1)
        return row, turned & (samples - 1)

    def counted(first, turn):
        row_a, sample_a = window(first, turn)
        row_b, sample_b = window(first + 1, turn)
        row = jnp.concatenate([row_a, row_b], axis=1)
        sample = jnp.concatenate([sample_a, sample_b + samples], axis=1)
        row_hot = (row_iota == row).astype(jnp.float32).astype(jnp.bfloat16)
        sample_hot = (sample_iota == sample).astype(jnp.float32).astype(jnp.bfloat16)
        return lax.dot_general(
            row_hot, sample_hot, (((1,), (1,)), ((), ())), preferred_element_type=jnp.float32
        )

    def pair(step, carry):
        first = step * 2
        total = counted(first, 0)
        spans = [
            off_ref[(first + i) * (F + 1) + feature + 1] - off_ref[(first + i) * (F + 1) + feature]
            for i in (0, 1)
        ]
        turns = (jnp.maximum(spans[0], spans[1]) + samples - 1) // samples
        total = lax.fori_loop(1, turns, lambda turn, acc: acc + counted(first, turn), total)
        low = total.astype(jnp.bfloat16)
        counts_ref[0, :, pl.ds(pl.multiple_of(first * samples, 2 * samples), 2 * samples)] = low
        part = jnp.dot(low_table, low, preferred_element_type=jnp.float32).astype(jnp.bfloat16)
        partial_ref[first, 0] = part[:, :samples]
        partial_ref[first + 1, 0] = part[:, samples:]
        return carry

    lax.fori_loop(0, devices // 2, pair, 0, unroll=2)


def count_tables(offsets, keys, embed_table, devices, samples):
    table_rows = embed_table.shape[1]
    return pl.pallas_call(
        functools.partial(count_kernel, devices, samples, table_rows),
        grid_spec=pltpu.PrefetchScalarGridSpec(
            num_scalar_prefetch=1,
            grid=(F,),
            in_specs=[
                pl.BlockSpec(keys.shape, lambda f, off: (0, 0)),
                pl.BlockSpec((1, table_rows, EMB), lambda f, off: (f, 0, 0)),
            ],
            out_specs=[
                pl.BlockSpec((1, table_rows, devices * samples), lambda f, off: (f, 0, 0)),
                pl.BlockSpec((devices, 1, EMB, samples), lambda f, off: (0, f, 0, 0)),
            ],
        ),
        out_shape=[
            jax.ShapeDtypeStruct((F, table_rows, devices * samples), jnp.bfloat16),
            jax.ShapeDtypeStruct((devices, F, EMB, samples), jnp.bfloat16),
        ],
        compiler_params=pltpu.CompilerParams(vmem_limit_bytes=48 << 20),
        name="count_tables",
    )(offsets, keys, embed_table)


def row_grad_kernel(counts_ref, grads_ref, out_ref, square_ref):
    @pl.when(pl.program_id(0) == 0)
    def start():
        square_ref[...] = jnp.zeros_like(square_ref)

    total = jnp.dot(counts_ref[0], grads_ref[...], preferred_element_type=jnp.float32)
    out_ref[0] = total
    square_ref[...] += jnp.sum((total * total).reshape(-1, 8, EMB), axis=0)


def row_grads(counts, grads):
    table_rows, batch = counts.shape[1:]
    return pl.pallas_call(
        row_grad_kernel,
        grid=(F,),
        in_specs=[
            pl.BlockSpec((1, table_rows, batch), lambda f: (f, 0, 0)),
            pl.BlockSpec((batch, EMB), lambda f: (0, f)),
        ],
        out_specs=[
            pl.BlockSpec((1, table_rows, EMB), lambda f: (f, 0, 0)),
            pl.BlockSpec((8, EMB), lambda f: (0, 0)),
        ],
        out_shape=[
            jax.ShapeDtypeStruct((F, table_rows, EMB), jnp.float32),
            jax.ShapeDtypeStruct((8, EMB), jnp.float32),
        ],
        compiler_params=pltpu.CompilerParams(vmem_limit_bytes=48 << 20),
        name="row_grads",
    )(counts, grads)


MESH = pl.DeviceIdType.MESH


def place():
    me = lax.axis_index("row")
    return me // 8, (me // 4) % 2, (me // 2) % 2, me % 2


def device_at(z, y, x, core):
    return (((z * 2 + y) * 2 + x) * 2 + core,)


def greet(z, y, x, core):
    barrier = pltpu.get_barrier_semaphore()

    def hail(*where):
        pl.semaphore_signal(barrier, inc=1, device_id=device_at(*where), device_id_type=MESH)

    hail(z, y, x, 1 - core)
    hail(z, y, 1 - x, core)
    hail(z, 1 - y, x, core)

    @pl.when(z > 0)
    def below():
        hail(z - 1, y, x, core)

    @pl.when(z < 3)
    def above():
        hail(z + 1, y, x, core)

    @pl.when(jnp.logical_and(z > 0, z < 3))
    def inside():
        pl.semaphore_wait(barrier, 5)

    @pl.when(jnp.logical_or(z == 0, z == 3))
    def edge():
        pl.semaphore_wait(barrier, 4)


def remote(source, target, send_sem, recv_sem, where):
    return pltpu.make_async_remote_copy(
        src_ref=source,
        dst_ref=target,
        send_sem=send_sem,
        recv_sem=recv_sem,
        device_id=device_at(*where),
        device_id_type=MESH,
    )


def add_into(target, source, count):
    @pl.loop(0, count)
    def step(i):
        target[i] = target[i] + source[i]


def scatter_kernel(
    base, slices, lags, x_ref, out_ref, own, got_core, got_one, got_two, got_up, got_down,
    local_sem, send_core, recv_core, send_one, recv_one, send_two, recv_two,
    send_up, recv_up, send_down, recv_down,
):
    z, y, x, core = place()
    rows = own.shape[4]

    def span(q):
        return pl.ds(base + q * rows, rows)

    def kept(q):
        return pl.ds(q * rows, rows)

    def to_core(q):
        return remote(x_ref.at[:, :, :, 1 - core, span(q)], got_core.at[q], send_core.at[q], recv_core.at[q], (z, y, x, 1 - core))

    def to_one(q):
        if q % 2 == 0:
            source, where = own.at[q, :, :, 1 - x], (z, y, 1 - x, core)
        else:
            source, where = own.at[q, :, 1 - y], (z, 1 - y, x, core)
        return remote(source, got_one.at[q], send_one.at[q], recv_one.at[q], where)

    def to_two(q):
        if q % 2 == 0:
            source, where = own.at[q, :, 1 - y, x], (z, 1 - y, x, core)
        else:
            source, where = own.at[q, :, y, 1 - x], (z, y, 1 - x, core)
        return remote(source, got_two.at[q], send_two.at[q], recv_two.at[q], where)

    def to_up(q, level):
        count = 3 - level
        source = own.at[q, 1:4, y, x] if level == 0 else got_up.at[q, 1 : count + 1]
        return remote(source, got_up.at[q, 0:count], send_up.at[q], recv_up.at[q], (z + 1, y, x, core))

    def to_down(q, level):
        count = level
        source = own.at[q, 0:3, y, x] if level == 3 else got_down.at[q, 0:count]
        return remote(source, got_down.at[q, 0:count], send_down.at[q], recv_down.at[q], (z - 1, y, x, core))

    def local(q):
        return pltpu.make_async_copy(x_ref.at[:, :, :, core, span(q)], own.at[q], local_sem.at[q])

    def stage_zero(q):
        local(q).wait()
        to_core(q).wait_recv()

        @pl.loop(0, 16)
        def step(i):
            a, b, c = i // 4, (i // 2) % 2, i % 2
            own[q, a, b, c] = own[q, a, b, c] + got_core[q, a, b, c]

        to_one(q).start()

    def stage_one(q):
        to_one(q).wait_recv()

        @pl.loop(0, 8)
        def step(i):
            a, b = i // 2, i % 2
            if q % 2 == 0:
                own[q, a, b, x] = own[q, a, b, x] + got_one[q, a, b]
            else:
                own[q, a, y, b] = own[q, a, y, b] + got_one[q, a, b]

        to_two(q).start()

    def stage_two(q):
        to_two(q).wait_recv()

        @pl.loop(0, 4)
        def step(a):
            own[q, a, y, x] = own[q, a, y, x] + got_two[q, a]

        @pl.when(z == 0)
        def rise():
            to_up(q, 0).start()

        @pl.when(z == 3)
        def fall():
            to_down(q, 3).start()

    def stage_chain(q, hop):
        @pl.when(z == hop)
        def rise():
            to_up(q, hop - 1).wait_recv()
            for t in range(hop + 1, 4):
                got_up[q, t - hop] = got_up[q, t - hop] + own[q, t, y, x]
            if hop < 3:
                to_up(q, hop).start()

        @pl.when(z == 3 - hop)
        def fall():
            to_down(q, 4 - hop).wait_recv()
            for t in range(0, 3 - hop):
                got_down[q, t] = got_down[q, t] + own[q, t, y, x]
            if hop < 3:
                to_down(q, 3 - hop).start()

    def stage_end(q):
        @pl.when(z == 0)
        def bottom():
            total = own[q, 0, y, x].astype(jnp.float32) + got_down[q, 0].astype(jnp.float32)
            out_ref[kept(q)] = total.astype(out_ref.dtype)

        @pl.when(z == 3)
        def top():
            total = own[q, 3, y, x].astype(jnp.float32) + got_up[q, 0].astype(jnp.float32)
            out_ref[kept(q)] = total.astype(out_ref.dtype)

        for level in (1, 2):

            @pl.when(z == level)
            def middle():
                total = own[q, level, y, x].astype(jnp.float32) + got_up[q, 0].astype(jnp.float32)
                total = total + got_down[q, level].astype(jnp.float32)
                out_ref[kept(q)] = total.astype(out_ref.dtype)

    for q in range(slices):
        local(q).start()
    greet(z, y, x, core)
    for q in range(slices):
        to_core(q).start()
    stages = (
        stage_zero,
        stage_one,
        stage_two,
        lambda q: stage_chain(q, 1),
        lambda q: stage_chain(q, 2),
        lambda q: (stage_chain(q, 3), stage_end(q)),
    )
    for tick in range(slices + lags[-1]):
        for lag, stage in zip((0,) + lags, stages):
            if 0 <= tick - lag < slices:
                stage(tick - lag)
    for q in range(slices):
        to_core(q).wait_send()
        to_one(q).wait_send()
        to_two(q).wait_send()
        for level in range(4):

            @pl.when(z == level)
            def sent():
                if level < 3:
                    to_up(q, level).wait_send()
                if level > 0:
                    to_down(q, level).wait_send()


def scatter_sum(array, base, chunk, out_dtype, slices, lags, collective_id, name):
    lanes = array.shape[-1]
    rows = chunk // slices
    low = array.dtype
    dma = pltpu.SemaphoreType.DMA
    return pl.pallas_call(
        functools.partial(scatter_kernel, base, slices, lags),
        out_shape=jax.ShapeDtypeStruct((chunk, lanes), out_dtype),
        in_specs=[pl.BlockSpec(memory_space=pl.ANY)],
        out_specs=pl.BlockSpec(memory_space=pltpu.VMEM),
        scratch_shapes=[
            pltpu.VMEM((slices, 4, 2, 2, rows, lanes), low),
            pltpu.VMEM((slices, 4, 2, 2, rows, lanes), low),
            pltpu.VMEM((slices, 4, 2, rows, lanes), low),
            pltpu.VMEM((slices, 4, rows, lanes), low),
            pltpu.VMEM((slices, 3, rows, lanes), low),
            pltpu.VMEM((slices, 3, rows, lanes), low),
            dma((slices,)),
            dma((slices,)), dma((slices,)),
            dma((slices,)), dma((slices,)),
            dma((slices,)), dma((slices,)),
            dma((slices,)), dma((slices,)),
            dma((slices,)), dma((slices,)),
        ],
        compiler_params=pltpu.CompilerParams(
            collective_id=collective_id, has_side_effects=True, vmem_limit_bytes=60 << 20
        ),
        name=name,
    )(array.reshape(4, 2, 2, 2, -1, lanes))


def spread_kernel(slices, lags, x_ref, out_ref, local_sem, send_up, recv_up, send_down, recv_down,
    send_one, recv_one, send_two, recv_two, send_core, recv_core):
    z, y, x, core = place()
    rows = x_ref.shape[0] // slices

    def span(q):
        return pl.ds(q * rows, rows)

    def local(q):
        return pltpu.make_async_copy(x_ref.at[span(q)], out_ref.at[z, y, x, core, span(q)], local_sem.at[q])

    def to_up(q, k):
        block = z - k
        target = out_ref.at[block, y, x, core, span(q)]
        source = x_ref.at[span(q)] if k == 0 else target
        return remote(source, target, send_up.at[q, k], recv_up.at[q, k], (z + 1, y, x, core))

    def to_down(q, k):
        block = z + k
        target = out_ref.at[block, y, x, core, span(q)]
        source = x_ref.at[span(q)] if k == 0 else target
        return remote(source, target, send_down.at[q, k], recv_down.at[q, k], (z - 1, y, x, core))

    def to_one(q):
        block = out_ref.at[:, y, x, core, span(q)]
        where = (z, y, 1 - x, core) if q % 2 == 0 else (z, 1 - y, x, core)
        return remote(block, block, send_one.at[q], recv_one.at[q], where)

    def to_two(q):
        if q % 2 == 0:
            block, where = out_ref.at[:, y, :, core, span(q)], (z, 1 - y, x, core)
        else:
            block, where = out_ref.at[:, :, x, core, span(q)], (z, y, 1 - x, core)
        return remote(block, block, send_two.at[q], recv_two.at[q], where)

    def to_core(q):
        block = out_ref.at[:, :, :, core, span(q)]
        return remote(block, block, send_core.at[q], recv_core.at[q], (z, y, x, 1 - core))

    def stage_start(q):
        @pl.when(z < 3)
        def rise():
            to_up(q, 0).start()

        @pl.when(z > 0)
        def fall():
            to_down(q, 0).start()

    def stage_chain(q):
        for k in range(3):

            @pl.when(z - 1 - k >= 0)
            def rise():
                to_up(q, k).wait_recv()
                if k < 2:

                    @pl.when(z < 3)
                    def go_on():
                        to_up(q, k + 1).start()

            @pl.when(z + 1 + k <= 3)
            def fall():
                to_down(q, k).wait_recv()
                if k < 2:

                    @pl.when(z > 0)
                    def go_on():
                        to_down(q, k + 1).start()

        local(q).wait()
        to_one(q).start()

    def stage_one(q):
        to_one(q).wait_recv()
        to_two(q).start()

    def stage_two(q):
        to_two(q).wait_recv()
        to_core(q).start()

    def stage_core(q):
        to_core(q).wait_recv()

    for q in range(slices):
        local(q).start()
    greet(z, y, x, core)
    for q in range(slices):
        stage_start(q)
    for tick in range(slices + lags[2]):
        for lag, stage in zip((0,) + lags, (stage_chain, stage_one, stage_two, stage_core)):
            if 0 <= tick - lag < slices:
                stage(tick - lag)
    for q in range(slices):
        for k in range(3):

            @pl.when(jnp.logical_and(z < 3, z - k >= 0))
            def rise():
                to_up(q, k).wait_send()

            @pl.when(jnp.logical_and(z > 0, z + k <= 3))
            def fall():
                to_down(q, k).wait_send()

        to_one(q).wait_send()
        to_two(q).wait_send()
        to_core(q).wait_send()


def spread(array, slices, lags, collective_id, name):
    chunk, lanes = array.shape
    dma = pltpu.SemaphoreType.DMA
    gathered = pl.pallas_call(
        functools.partial(spread_kernel, slices, lags),
        out_shape=jax.ShapeDtypeStruct((4, 2, 2, 2, chunk, lanes), array.dtype),
        in_specs=[pl.BlockSpec(memory_space=pl.ANY)],
        out_specs=pl.BlockSpec(memory_space=pl.ANY),
        scratch_shapes=[
            dma((slices,)),
            dma((slices, 3)), dma((slices, 3)),
            dma((slices, 3)), dma((slices, 3)),
            dma((slices,)), dma((slices,)),
            dma((slices,)), dma((slices,)),
            dma((slices,)), dma((slices,)),
        ],
        compiler_params=pltpu.CompilerParams(collective_id=collective_id, has_side_effects=True),
        name=name,
    )(array)
    return gathered.reshape(32 * chunk, lanes)


def body(
    row_ids,
    hot_counts,
    dense_feats,
    click_labels,
    block_owners,
    embed_table,
    table_moment,
    table_square,
    dense_slots,
    dense_moment,
    dense_square,
    dense_proj,
    proj_moment,
    proj_square,
    head_weight,
    head_moment,
    head_square,
    biases,
    bias_moment,
    bias_square,
):
    devices = lax.axis_size("row")
    samples = row_ids.shape[0]
    slot_count = dense_slots.shape[0]
    table_rows = embed_table.shape[1]
    block_count = block_owners.shape[0]
    capacity = samples * TOTAL // devices
    live_total = samples * TOTAL
    everything = lax.all_gather(dense_slots.astype(jnp.bfloat16), "row", axis=0, tiled=True)
    fetched = jnp.take(everything, block_owners, axis=0)
    cross_down, cross_up, first_matrix, middle, third_matrix = split_dense(
        fetched.reshape(block_count * BR, RANK)
    )
    bias_dense, bias_cross, bias_one, bias_two, bias_three, bias_last = split_bias(biases)
    flat_ids = row_ids.reshape(-1)
    live_mask = (
        lax.broadcasted_iota(jnp.int32, row_ids.shape, 2) < hot_counts[:, :, None]
    ).reshape(-1)
    sort_key = jnp.where(live_mask, flat_ids // table_rows, devices)
    full_order = jnp.argsort(sort_key, stable=True)
    slot_place = jnp.argsort(full_order)
    ordering = full_order[:live_total]
    segment = ordering // HOT
    requests = (segment % F * table_rows + jnp.take(flat_ids, ordering) % table_rows).reshape(
        devices, capacity
    )
    flat_table = embed_table.astype(jnp.bfloat16).reshape(F * table_rows, EMB)
    received = lax.all_to_all(requests, "row", split_axis=0, concat_axis=0, tiled=True)
    looked_up = jnp.take(flat_table, received, axis=0)
    returned = lax.all_to_all(looked_up, "row", split_axis=0, concat_axis=0, tiled=True)
    padded_rows = jnp.concatenate(
        [returned.reshape(-1, EMB), jnp.zeros((1, EMB), jnp.bfloat16)], axis=0
    )
    pick = jnp.where(live_mask, slot_place, live_total)
    in_slots = jnp.take(padded_rows, pick, axis=0).reshape(samples, F, HOT, EMB)
    pooled = jnp.sum(in_slots, axis=2, dtype=jnp.float32)
    pooled_low = pooled.astype(jnp.bfloat16).reshape(samples, F * EMB)
    dense_part = (
        jnp.dot(dense_feats, dense_proj, precision=highest, preferred_element_type=jnp.float32)
        + bias_dense
    )
    anchor = jnp.concatenate([dense_part, pooled_low.astype(jnp.float32)], axis=1)
    current = anchor
    stored = []
    for depth in range(LAYERS):
        saved, current = cross_forward(
            anchor, current, cross_down[depth], cross_up[depth], bias_cross[depth]
        )
        stored.append(saved)
    first_saved, hidden = dense_forward(current, first_matrix, bias_one)
    second_saved, hidden = dense_forward(hidden, middle, bias_two)
    third_saved, hidden = dense_forward(hidden, third_matrix, bias_three)
    logits = (
        jnp.dot(hidden, head_weight, precision=highest, preferred_element_type=jnp.float32)
        + bias_last
    )
    labels = click_labels.astype(jnp.float32)
    loss_local = jnp.sum(jax.nn.softplus(logits) - labels * logits)
    grad_logits = (jax.nn.sigmoid(logits) - labels) / (samples * devices)
    grad_head_local = jnp.dot(
        grad_logits, hidden, precision=highest, preferred_element_type=jnp.float32
    )
    grad_hidden = grad_logits[:, None] * head_weight[None, :]
    grad_hidden, grad_third, grad_bias_three = dense_backward(
        third_saved, third_matrix, grad_hidden
    )
    grad_hidden, grad_middle, grad_bias_two = dense_backward(second_saved, middle, grad_hidden)
    grad_current, grad_first, grad_bias_one = dense_backward(first_saved, first_matrix, grad_hidden)
    grad_anchor = jnp.zeros_like(anchor)
    grads_down = [None] * LAYERS
    grads_up = [None] * LAYERS
    grads_cross = [None] * LAYERS
    for depth in reversed(range(LAYERS)):
        grad_current, grad_part, grads_down[depth], grads_up[depth], grads_cross[depth] = (
            cross_backward(anchor, stored[depth], cross_down[depth], cross_up[depth], grad_current)
        )
        grad_anchor = grad_anchor + grad_part
    grad_anchor = grad_anchor + grad_current
    grad_pooled = grad_anchor[:, EMB:].astype(jnp.bfloat16).reshape(samples * F, EMB)
    sent_back = jnp.take(grad_pooled, segment, axis=0).reshape(devices, capacity, EMB)
    arrived = lax.all_to_all(sent_back, "row", split_axis=0, concat_axis=0, tiled=True)
    grad_table = table_gradient(arrived.reshape(-1, EMB), received.reshape(-1), table_rows)
    grad_proj_local = jnp.einsum(
        "sa,sb->ab",
        dense_feats,
        grad_anchor[:, :EMB],
        precision=highest,
        preferred_element_type=jnp.float32,
    )
    stacked = jnp.concatenate(
        [
            jnp.stack(grads_down).reshape(-1, RANK),
            jnp.stack(grads_up).reshape(-1, RANK),
            grad_first.reshape(-1, RANK),
            grad_middle.reshape(-1, RANK),
            grad_third,
            jnp.zeros((BR, RANK), jnp.float32),
        ],
        axis=0,
    ).reshape(block_count + 1, BR, RANK)
    matches = block_owners[None, :] == jnp.arange(devices * slot_count, dtype=jnp.int32)[:, None]
    inverse = jnp.sum(
        jnp.where(matches, jnp.arange(block_count, dtype=jnp.int32)[None, :], 0), axis=1
    )
    inverse = inverse + jnp.where(jnp.any(matches, axis=1), 0, block_count)
    grad_slots = lax.psum_scatter(
        jnp.take(stacked, inverse, axis=0), "row", scatter_dimension=0, tiled=True
    )
    bias_local = jnp.concatenate(
        [
            jnp.sum(grad_anchor[:, :EMB], axis=0),
            jnp.stack(grads_cross).reshape(-1),
            grad_bias_one,
            grad_bias_two,
            grad_bias_three,
            jnp.sum(grad_logits)[None],
        ]
    )
    loss_total, grad_proj, grad_head, grad_bias = lax.psum(
        (loss_local, grad_proj_local, grad_head_local, bias_local), "row"
    )
    local_squares = jnp.sum(grad_table * grad_table) + jnp.sum(grad_slots * grad_slots)
    squares = lax.psum(local_squares, "row")
    squares = (
        squares
        + jnp.sum(grad_proj * grad_proj)
        + jnp.sum(grad_head * grad_head)
        + jnp.sum(grad_bias * grad_bias)
    )
    grad_norm = jnp.sqrt(squares)
    clip_scale = clip_norm / jnp.maximum(grad_norm, clip_norm)
    table_new = adamw(embed_table, table_moment, table_square, clip_scale * grad_table, rate_table)
    dense_new = adamw(dense_slots, dense_moment, dense_square, clip_scale * grad_slots, rate_dense)
    proj_new = adamw(dense_proj, proj_moment, proj_square, clip_scale * grad_proj, rate_small)
    head_new = adamw(head_weight, head_moment, head_square, clip_scale * grad_head, rate_small)
    bias_new = adamw(biases, bias_moment, bias_square, clip_scale * grad_bias, rate_small)
    return (
        loss_total,
        grad_norm,
        table_new[0],
        table_new[1],
        table_new[2],
        dense_new[0],
        dense_new[1],
        dense_new[2],
        proj_new[0],
        proj_new[1],
        proj_new[2],
        head_new[0],
        head_new[1],
        head_new[2],
        bias_new[0],
        bias_new[1],
        bias_new[2],
    )


def body_counted(
    row_ids,
    hot_counts,
    dense_feats,
    click_labels,
    block_owners,
    embed_table,
    table_moment,
    table_square,
    dense_slots,
    dense_moment,
    dense_square,
    dense_proj,
    proj_moment,
    proj_square,
    head_weight,
    head_moment,
    head_square,
    biases,
    bias_moment,
    bias_square,
):
    devices = lax.axis_size("row")
    samples = row_ids.shape[0]
    slot_count = dense_slots.shape[0]
    table_rows = embed_table.shape[1]
    block_count = block_owners.shape[0]
    capacity = samples * TOTAL // devices
    live_total = samples * TOTAL
    everything = lax.all_gather(dense_slots.astype(jnp.bfloat16), "row", axis=0, tiled=True)
    fetched = jnp.take(everything, block_owners, axis=0, mode="clip")
    cross_down, cross_up, first_matrix, middle, third_matrix = split_dense(
        fetched.reshape(block_count * BR, RANK)
    )
    bias_dense, bias_cross, bias_one, bias_two, bias_three, bias_last = split_bias(biases)
    lanes = lax.broadcasted_iota(jnp.int32, row_ids.shape, 2)
    features = lax.broadcasted_iota(jnp.int32, row_ids.shape, 1)
    sample_of = lax.broadcasted_iota(jnp.int32, row_ids.shape, 0)
    key = (
        ((row_ids // table_rows) << 21)
        | (features << 16)
        | ((row_ids % table_rows) << 7)
        | sample_of
    )
    key = jnp.where(lanes < hot_counts[:, :, None], key, devices << 21)
    ordered = lax.sort(key.reshape(-1), is_stable=False)[:live_total]
    requests = (ordered & ((1 << 21) - 1)).reshape(devices, capacity)
    received = lax.all_to_all(requests, "row", split_axis=0, concat_axis=0, tiled=True)
    edges = jnp.arange(F + 1, dtype=jnp.int32) << 16
    offsets = jnp.sum((received[:, None, :] < edges[None, :, None]).astype(jnp.int32), axis=2)
    room = (capacity + samples - 1) // samples * samples + samples
    keys = jnp.pad(received, ((0, 0), (0, room - capacity)), constant_values=-1)
    counts, partial = count_tables(offsets.reshape(-1), keys, embed_table, devices, samples)
    summed = scatter_sum(
        partial, 0, F * EMB, jnp.bfloat16, 16, (2, 4, 6, 7, 8), 0, "scatter_pooled"
    )
    pooled_low = summed.T
    dense_part = (
        jnp.dot(dense_feats, dense_proj, precision=highest, preferred_element_type=jnp.float32)
        + bias_dense
    )
    anchor = jnp.concatenate([dense_part, pooled_low.astype(jnp.float32)], axis=1)
    current = anchor
    stored = []
    for depth in range(LAYERS):
        saved, current = cross_forward(
            anchor, current, cross_down[depth], cross_up[depth], bias_cross[depth]
        )
        stored.append(saved)
    first_saved, hidden = dense_forward(current, first_matrix, bias_one)
    second_saved, hidden = dense_forward(hidden, middle, bias_two)
    third_saved, hidden = dense_forward(hidden, third_matrix, bias_three)
    logits = (
        jnp.dot(hidden, head_weight, precision=highest, preferred_element_type=jnp.float32)
        + bias_last
    )
    labels = click_labels.astype(jnp.float32)
    loss_local = jnp.sum(jax.nn.softplus(logits) - labels * logits)
    grad_logits = (jax.nn.sigmoid(logits) - labels) / (samples * devices)
    grad_head_local = jnp.dot(
        grad_logits, hidden, precision=highest, preferred_element_type=jnp.float32
    )
    grad_hidden = grad_logits[:, None] * head_weight[None, :]
    grad_hidden, grad_third, grad_bias_three = dense_backward(
        third_saved, third_matrix, grad_hidden
    )
    grad_hidden, grad_middle, grad_bias_two = dense_backward(second_saved, middle, grad_hidden)
    grad_current, grad_first, grad_bias_one = dense_backward(first_saved, first_matrix, grad_hidden)
    grad_anchor = jnp.zeros_like(anchor)
    grads_down = [None] * LAYERS
    grads_up = [None] * LAYERS
    grads_cross = [None] * LAYERS
    for depth in reversed(range(LAYERS)):
        grad_current, grad_part, grads_down[depth], grads_up[depth], grads_cross[depth] = (
            cross_backward(anchor, stored[depth], cross_down[depth], cross_up[depth], grad_current)
        )
        grad_anchor = grad_anchor + grad_part
    grad_anchor = grad_anchor + grad_current
    grad_pooled = grad_anchor[:, EMB:].astype(jnp.bfloat16)
    gathered_grads = lax.all_gather(grad_pooled, "row", axis=0, tiled=True)
    grad_table, table_squares = row_grads(counts, gathered_grads)
    grad_proj_local = jnp.einsum(
        "sa,sb->ab",
        dense_feats,
        grad_anchor[:, :EMB],
        precision=highest,
        preferred_element_type=jnp.float32,
    )
    stacked = jnp.concatenate(
        [
            jnp.stack(grads_down).reshape(-1, RANK),
            jnp.stack(grads_up).reshape(-1, RANK),
            grad_first.reshape(-1, RANK),
            grad_middle.reshape(-1, RANK),
            grad_third,
            jnp.zeros((BR, RANK), jnp.float32),
        ],
        axis=0,
    ).astype(jnp.bfloat16).reshape(block_count + 1, BR, RANK)
    matches = block_owners[None, :] == jnp.arange(devices * slot_count, dtype=jnp.int32)[:, None]
    inverse = jnp.sum(
        jnp.where(matches, jnp.arange(block_count, dtype=jnp.int32)[None, :], 0), axis=1
    )
    inverse = inverse + jnp.where(jnp.any(matches, axis=1), 0, block_count)
    placed = jnp.take(stacked, inverse, axis=0, mode="clip")
    half = slot_count * BR // 2
    grad_slots = jnp.concatenate(
        [
            scatter_sum(placed, part * half, half, jnp.float32, 16, (2, 4, 6, 7, 8), part + 1, "scatter_dense")
            for part in (0, 1)
        ],
        axis=0,
    ).reshape(slot_count, BR, RANK)
    bias_local = jnp.concatenate(
        [
            jnp.sum(grad_anchor[:, :EMB], axis=0),
            jnp.stack(grads_cross).reshape(-1),
            grad_bias_one,
            grad_bias_two,
            grad_bias_three,
            jnp.sum(grad_logits)[None],
        ]
    )
    loss_total, grad_proj, grad_head, grad_bias = lax.psum(
        (loss_local, grad_proj_local, grad_head_local, bias_local), "row"
    )
    local_squares = jnp.sum(table_squares) + jnp.sum(grad_slots * grad_slots)
    squares = lax.psum(local_squares, "row")
    squares = (
        squares
        + jnp.sum(grad_proj * grad_proj)
        + jnp.sum(grad_head * grad_head)
        + jnp.sum(grad_bias * grad_bias)
    )
    grad_norm = jnp.sqrt(squares)
    clip_scale = clip_norm / jnp.maximum(grad_norm, clip_norm)
    table_new = adamw(embed_table, table_moment, table_square, clip_scale * grad_table, rate_table)
    dense_new = adamw(dense_slots, dense_moment, dense_square, clip_scale * grad_slots, rate_dense)
    proj_new = adamw(dense_proj, proj_moment, proj_square, clip_scale * grad_proj, rate_small)
    head_new = adamw(head_weight, head_moment, head_square, clip_scale * grad_head, rate_small)
    bias_new = adamw(biases, bias_moment, bias_square, clip_scale * grad_bias, rate_small)
    return (
        loss_total,
        grad_norm,
        table_new[0],
        table_new[1],
        table_new[2],
        dense_new[0],
        dense_new[1],
        dense_new[2],
        proj_new[0],
        proj_new[1],
        proj_new[2],
        head_new[0],
        head_new[1],
        head_new[2],
        bias_new[0],
        bias_new[1],
        bias_new[2],
    )


def solution(mesh):
    in_specs = (
        P("row", None, None),
        P("row", None),
        P("row", None),
        P("row"),
        P(),
        P(None, "row", None),
        P(None, "row", None),
        P(None, "row", None),
        P("row", None, None),
        P("row", None, None),
        P("row", None, None),
        P(),
        P(),
        P(),
        P(),
        P(),
        P(),
        P(),
        P(),
        P(),
    )
    out_specs = (
        P(),
        P(),
        P(None, "row", None),
        P(None, "row", None),
        P(None, "row", None),
        P("row", None, None),
        P("row", None, None),
        P("row", None, None),
        P(),
        P(),
        P(),
        P(),
        P(),
        P(),
        P(),
        P(),
        P(),
    )
    fits = mesh.shape["row"] <= 32
    chosen = body_counted if fits else body
    return jax.shard_map(chosen, mesh=mesh, in_specs=in_specs, out_specs=out_specs, check_vma=False)
```

```python
import functools

import jax
import jax.numpy as jnp
from jax import lax
from jax.experimental import pallas as pl
from jax.experimental.pallas import tpu as pltpu
from jax.sharding import PartitionSpec as P

F = 26
HOT = 30
EMB = 128
RANK = 512
LAYERS = 3
H1 = 1024
H2 = 1024
H3 = 512
BR = 128
STEP = 10
WIDTH = 3456
TOTAL = 403
NBIAS = 13057


beta_one = 0.9
beta_two = 0.999
adam_eps = 1e-12
decay_rate = 0.01
clip_norm = 0.001
rate_table = 0.3
rate_dense = 0.03
rate_small = 0.1
highest = lax.Precision.HIGHEST


def split_dense(flat):
    cross_rows = LAYERS * WIDTH
    first = 2 * cross_rows + WIDTH * H1 // RANK
    second = first + H1 * H2 // RANK
    return (
        flat[:cross_rows].reshape(LAYERS, WIDTH, RANK),
        flat[cross_rows : 2 * cross_rows].reshape(LAYERS, WIDTH, RANK),
        flat[2 * cross_rows : first].reshape(WIDTH, H1),
        flat[first:second].reshape(H1, H2),
        flat[second : second + H2 * H3 // RANK],
    )


def split_bias(biases):
    start = EMB + LAYERS * WIDTH
    return (
        biases[:EMB],
        biases[EMB:start].reshape(LAYERS, WIDTH),
        biases[start : start + H1],
        biases[start + H1 : start + H1 + H2],
        biases[start + H1 + H2 : start + H1 + H2 + H3],
        biases[NBIAS - 1],
    )


def cross_forward(anchor, current, weight_down, weight_up, bias_term):
    current_low = current.astype(jnp.bfloat16)
    reduced = jnp.dot(current_low, weight_down, preferred_element_type=jnp.float32).astype(
        jnp.bfloat16
    )
    mixing = (
        jnp.einsum("sr,wr->sw", reduced, weight_up, preferred_element_type=jnp.float32) + bias_term
    )
    return ((current_low, reduced, mixing), anchor * mixing + current)


def cross_backward(anchor, stored, weight_down, weight_up, grad_current):
    current_low, reduced, mixing = stored
    grad_mixing = anchor * grad_current
    grad_mixing_low = grad_mixing.astype(jnp.bfloat16)
    grad_up = jnp.einsum("sw,sr->wr", grad_mixing_low, reduced, preferred_element_type=jnp.float32)
    grad_reduced = jnp.dot(grad_mixing_low, weight_up, preferred_element_type=jnp.float32).astype(
        jnp.bfloat16
    )
    grad_down = jnp.einsum(
        "sw,sr->wr", current_low, grad_reduced, preferred_element_type=jnp.float32
    )
    grad_prev = grad_current + jnp.einsum(
        "sr,wr->sw", grad_reduced, weight_down, preferred_element_type=jnp.float32
    )
    return (grad_prev, grad_current * mixing, grad_down, grad_up, jnp.sum(grad_mixing, axis=0))


def dense_forward(inputs, weight, bias_term):
    inputs_low = inputs.astype(jnp.bfloat16)
    before = jnp.dot(inputs_low, weight, preferred_element_type=jnp.float32) + bias_term
    return ((inputs_low, before), jax.nn.gelu(before))


def dense_backward(stored, weight, grad_out):
    inputs_low, before = stored
    unused, gelu_back = jax.vjp(jax.nn.gelu, before)
    grad_before = gelu_back(grad_out)[0]
    grad_low = grad_before.astype(jnp.bfloat16)
    grad_weight = jnp.einsum("sa,sb->ab", inputs_low, grad_low, preferred_element_type=jnp.float32)
    grad_inputs = jnp.einsum("sb,ab->sa", grad_low, weight, preferred_element_type=jnp.float32)
    return (grad_inputs, grad_weight, jnp.sum(grad_before, axis=0))


def table_gradient(arrived, served, table_rows):
    received = served.shape[0]
    window = min(512, received)
    order_back = jnp.argsort(served, stable=True)
    sorted_ids = jnp.take(served, order_back)
    edges = jnp.arange(F + 1, dtype=jnp.int32) * table_rows
    bounds = jnp.sum((sorted_ids[None, :] < edges[:, None]).astype(jnp.int32), axis=1)
    starts = bounds[:-1]
    finish = bounds[1:]
    windows = (finish - starts + window - 1) // window
    ends_cum = jnp.cumsum(windows)
    begins_cum = ends_cum - windows
    step_count = F + received // window + 1
    turns = jnp.arange(step_count, dtype=jnp.int32)
    feature_of = jnp.sum((ends_cum[None, :] <= turns[:, None]).astype(jnp.int32), axis=1)
    feature_safe = jnp.minimum(feature_of, F - 1)
    first_row = (
        jnp.take(starts, feature_safe) + (turns - jnp.take(begins_cum, feature_safe)) * window
    )
    row_index = first_row[:, None] + jnp.arange(window, dtype=jnp.int32)[None, :]
    row_valid = (feature_of < F)[:, None] & (row_index < jnp.take(finish, feature_safe)[:, None])
    row_safe = jnp.minimum(row_index, received - 1)
    window_grads = jnp.take(arrived, jnp.take(order_back, row_safe), axis=0)
    local_row = jnp.take(sorted_ids, row_safe) - feature_safe[:, None] * table_rows
    local_row = jnp.where(row_valid, local_row, -1)
    selector = (
        local_row[:, :, None] == jnp.arange(table_rows, dtype=jnp.int32)[None, None, :]
    ).astype(jnp.bfloat16)
    partial_sums = jnp.einsum(
        "swr,swe->sre", selector, window_grads, preferred_element_type=jnp.float32
    )
    feature_pick = (feature_of[:, None] == jnp.arange(F, dtype=jnp.int32)[None, :]).astype(
        jnp.float32
    )
    return jnp.einsum(
        "sf,sre->fre",
        feature_pick,
        partial_sums,
        precision=highest,
        preferred_element_type=jnp.float32,
    )


def adamw(weight, moment, square, gradient, step_rate):
    moment = beta_one * moment + (1 - beta_one) * gradient
    square = beta_two * square + (1 - beta_two) * gradient * gradient
    corrected = moment / (1 - beta_one**STEP)
    scaled = square / (1 - beta_two**STEP)
    weight = weight - step_rate * (corrected / (jnp.sqrt(scaled) + adam_eps) + decay_rate * weight)
    return (weight, moment, square)


def count_kernel(devices, samples, table_rows, off_ref, most_ref, keys_ref, table_ref, counts_ref, partial_ref, low_ref, rows_ref, samples_ref):
    feature = pl.program_id(0)
    low_ref[...] = table_ref[0].T.astype(jnp.bfloat16)
    lane = lax.broadcasted_iota(jnp.int32, (1, samples), 1)
    row_iota = lax.broadcasted_iota(jnp.int32, (table_rows, 2 * samples), 0)
    sample_iota = lax.broadcasted_iota(jnp.int32, (2 * samples, 2 * samples), 0)

    def window(source, turn):
        start = off_ref[source * (F + 1) + feature] + turn * samples
        stop = off_ref[source * (F + 1) + feature + 1]
        tile = start // samples
        base = pl.multiple_of(tile * samples, samples)
        piece = keys_ref[pl.ds(source, 1), pl.ds(base, 2 * samples)]
        turned = pltpu.roll(piece, 2 * samples - (start - base), 1)[:, :samples]
        valid = lane < stop - start
        row = jnp.where(valid, (turned >> 7) & (table_rows - 1), -1)
        return row, turned & (samples - 1)

    def product(row, sample):
        row_hot = jnp.where(row_iota == row, 1.0, 0.0).astype(jnp.bfloat16)
        sample_hot = jnp.where(sample_iota == sample, 1.0, 0.0).astype(jnp.bfloat16)
        return lax.dot_general(
            row_hot, sample_hot, (((1,), (1,)), ((), ())), preferred_element_type=jnp.float32
        )

    def counted(first, turn):
        row_a, sample_a = window(first, turn)
        row_b, sample_b = window(first + 1, turn)
        return product(
            jnp.concatenate([row_a, row_b], axis=1),
            jnp.concatenate([sample_a, sample_b + samples], axis=1),
        )

    def span(first):
        return pl.ds(pl.multiple_of(first * samples, 2 * samples), 2 * samples)

    for source in range(devices):
        row, sample = window(source, 0)
        half = pl.ds((source % 2) * samples, samples)
        rows_ref[pl.ds(source // 2, 1), half] = row
        samples_ref[pl.ds(source // 2, 1), half] = sample + (source % 2) * samples

    def pair(step, carry):
        total = product(rows_ref[pl.ds(step, 1), :], samples_ref[pl.ds(step, 1), :])
        counts_ref[0, :, span(step * 2)] = total.astype(jnp.bfloat16)
        return carry

    lax.fori_loop(0, devices // 2, pair, 0, unroll=devices // 2)

    def late(step, carry):
        first = step * 2
        spans = [
            off_ref[(first + i) * (F + 1) + feature + 1] - off_ref[(first + i) * (F + 1) + feature]
            for i in (0, 1)
        ]
        turns = (jnp.maximum(spans[0], spans[1]) + samples - 1) // samples

        @pl.when(turns > 1)
        def again():
            total = lax.fori_loop(1, turns, lambda turn, acc: acc + counted(first, turn), counted(first, 0))
            counts_ref[0, :, span(first)] = total.astype(jnp.bfloat16)

        return carry

    @pl.when(most_ref[feature] > samples)
    def crowded():
        lax.fori_loop(0, devices // 2, late, 0)

    group = devices

    def pool(step, carry):
        part = jnp.dot(
            low_ref[...],
            counts_ref[0, :, pl.ds(pl.multiple_of(step * group * samples, group * samples), group * samples)],
            preferred_element_type=jnp.float32,
        ).astype(jnp.bfloat16)
        for i in range(group):
            partial_ref[step * group + i, 0] = part[:, i * samples : (i + 1) * samples]
        return carry

    lax.fori_loop(0, devices // group, pool, 0)


def count_tables(offsets, keys, embed_table, devices, samples):
    table_rows = embed_table.shape[1]
    return pl.pallas_call(
        functools.partial(count_kernel, devices, samples, table_rows),
        grid_spec=pltpu.PrefetchScalarGridSpec(
            num_scalar_prefetch=2,
            grid=(F,),
            in_specs=[
                pl.BlockSpec(keys.shape, lambda f, off, most: (0, 0)),
                pl.BlockSpec((1, table_rows, EMB), lambda f, off, most: (f, 0, 0)),
            ],
            out_specs=[
                pl.BlockSpec((1, table_rows, devices * samples), lambda f, off, most: (f, 0, 0)),
                pl.BlockSpec((devices, 1, EMB, samples), lambda f, off, most: (0, f, 0, 0)),
            ],
            scratch_shapes=[
                pltpu.VMEM((EMB, table_rows), jnp.bfloat16),
                pltpu.VMEM((devices // 2, 2 * samples), jnp.int32),
                pltpu.VMEM((devices // 2, 2 * samples), jnp.int32),
            ],
        ),
        out_shape=[
            jax.ShapeDtypeStruct((F, table_rows, devices * samples), jnp.bfloat16),
            jax.ShapeDtypeStruct((devices, F, EMB, samples), jnp.bfloat16),
        ],
        compiler_params=pltpu.CompilerParams(vmem_limit_bytes=48 << 20),
        name="count_tables",
    )(offsets.reshape(-1), jnp.max(offsets[:, 1:] - offsets[:, :-1], axis=0), keys, embed_table)


def row_grad_kernel(counts_ref, grads_ref, out_ref, square_ref):
    @pl.when(pl.program_id(0) == 0)
    def start():
        square_ref[...] = jnp.zeros_like(square_ref)

    total = jnp.dot(counts_ref[0], grads_ref[...], preferred_element_type=jnp.float32)
    out_ref[0] = total
    square_ref[...] += jnp.sum((total * total).reshape(-1, 8, EMB), axis=0)


def row_grads(counts, grads):
    table_rows, batch = counts.shape[1:]
    return pl.pallas_call(
        row_grad_kernel,
        grid=(F,),
        in_specs=[
            pl.BlockSpec((1, table_rows, batch), lambda f: (f, 0, 0)),
            pl.BlockSpec((batch, EMB), lambda f: (0, f)),
        ],
        out_specs=[
            pl.BlockSpec((1, table_rows, EMB), lambda f: (f, 0, 0)),
            pl.BlockSpec((8, EMB), lambda f: (0, 0)),
        ],
        out_shape=[
            jax.ShapeDtypeStruct((F, table_rows, EMB), jnp.float32),
            jax.ShapeDtypeStruct((8, EMB), jnp.float32),
        ],
        compiler_params=pltpu.CompilerParams(vmem_limit_bytes=48 << 20),
        name="row_grads",
    )(counts, grads)


MESH = pl.DeviceIdType.MESH


def place():
    me = lax.axis_index("row")
    return me // 8, (me // 4) % 2, (me // 2) % 2, me % 2


def device_at(z, y, x, core):
    return (((z * 2 + y) * 2 + x) * 2 + core,)


def greet(z, y, x, core):
    barrier = pltpu.get_barrier_semaphore()

    def hail(*where):
        pl.semaphore_signal(barrier, inc=1, device_id=device_at(*where), device_id_type=MESH)

    hail(z, y, x, 1 - core)
    hail(z, y, 1 - x, core)
    hail(z, 1 - y, x, core)

    @pl.when(z > 0)
    def below():
        hail(z - 1, y, x, core)

    @pl.when(z < 3)
    def above():
        hail(z + 1, y, x, core)

    @pl.when(jnp.logical_and(z > 0, z < 3))
    def inside():
        pl.semaphore_wait(barrier, 5)

    @pl.when(jnp.logical_or(z == 0, z == 3))
    def edge():
        pl.semaphore_wait(barrier, 4)


def remote(source, target, send_sem, recv_sem, where):
    return pltpu.make_async_remote_copy(
        src_ref=source,
        dst_ref=target,
        send_sem=send_sem,
        recv_sem=recv_sem,
        device_id=device_at(*where),
        device_id_type=MESH,
    )


def add_into(target, source, count):
    @pl.loop(0, count)
    def step(i):
        target[i] = target[i] + source[i]


def scatter_kernel(
    base, slices, lags, x_ref, out_ref, own, got_core, got_one, got_two, got_up, got_down,
    local_sem, send_core, recv_core, send_one, recv_one, send_two, recv_two,
    send_up, recv_up, send_down, recv_down,
):
    z, y, x, core = place()
    rows = own.shape[4]

    def span(q):
        return pl.ds(base + q * rows, rows)

    def kept(q):
        return pl.ds(q * rows, rows)

    def to_core(q):
        return remote(x_ref.at[:, :, :, 1 - core, span(q)], got_core.at[q], send_core.at[q], recv_core.at[q], (z, y, x, 1 - core))

    def to_one(q):
        if q % 2 == 0:
            source, where = own.at[q, :, :, 1 - x], (z, y, 1 - x, core)
        else:
            source, where = own.at[q, :, 1 - y], (z, 1 - y, x, core)
        return remote(source, got_one.at[q], send_one.at[q], recv_one.at[q], where)

    def to_two(q):
        if q % 2 == 0:
            source, where = own.at[q, :, 1 - y, x], (z, 1 - y, x, core)
        else:
            source, where = own.at[q, :, y, 1 - x], (z, y, 1 - x, core)
        return remote(source, got_two.at[q], send_two.at[q], recv_two.at[q], where)

    def to_up(q, level):
        count = 3 - level
        source = own.at[q, 1:4, y, x] if level == 0 else got_up.at[q, 1 : count + 1]
        return remote(source, got_up.at[q, 0:count], send_up.at[q], recv_up.at[q], (z + 1, y, x, core))

    def to_down(q, level):
        count = level
        source = own.at[q, 0:3, y, x] if level == 3 else got_down.at[q, 0:count]
        return remote(source, got_down.at[q, 0:count], send_down.at[q], recv_down.at[q], (z - 1, y, x, core))

    def local(q):
        return pltpu.make_async_copy(x_ref.at[:, :, :, core, span(q)], own.at[q], local_sem.at[q])

    def stage_zero(q):
        local(q).wait()
        to_core(q).wait_recv()

        @pl.loop(0, 16)
        def step(i):
            a, b, c = i // 4, (i // 2) % 2, i % 2
            own[q, a, b, c] = own[q, a, b, c] + got_core[q, a, b, c]

        to_one(q).start()

    def stage_one(q):
        to_one(q).wait_recv()

        @pl.loop(0, 8)
        def step(i):
            a, b = i // 2, i % 2
            if q % 2 == 0:
                own[q, a, b, x] = own[q, a, b, x] + got_one[q, a, b]
            else:
                own[q, a, y, b] = own[q, a, y, b] + got_one[q, a, b]

        to_two(q).start()

    def stage_two(q):
        to_two(q).wait_recv()

        @pl.loop(0, 4)
        def step(a):
            own[q, a, y, x] = own[q, a, y, x] + got_two[q, a]

        @pl.when(z == 0)
        def rise():
            to_up(q, 0).start()

        @pl.when(z == 3)
        def fall():
            to_down(q, 3).start()

    def stage_chain(q, hop):
        @pl.when(z == hop)
        def rise():
            to_up(q, hop - 1).wait_recv()
            for t in range(hop + 1, 4):
                got_up[q, t - hop] = got_up[q, t - hop] + own[q, t, y, x]
            if hop < 3:
                to_up(q, hop).start()

        @pl.when(z == 3 - hop)
        def fall():
            to_down(q, 4 - hop).wait_recv()
            for t in range(0, 3 - hop):
                got_down[q, t] = got_down[q, t] + own[q, t, y, x]
            if hop < 3:
                to_down(q, 3 - hop).start()

    def stage_end(q):
        @pl.when(z == 0)
        def bottom():
            total = own[q, 0, y, x].astype(jnp.float32) + got_down[q, 0].astype(jnp.float32)
            out_ref[kept(q)] = total.astype(out_ref.dtype)

        @pl.when(z == 3)
        def top():
            total = own[q, 3, y, x].astype(jnp.float32) + got_up[q, 0].astype(jnp.float32)
            out_ref[kept(q)] = total.astype(out_ref.dtype)

        for level in (1, 2):

            @pl.when(z == level)
            def middle():
                total = own[q, level, y, x].astype(jnp.float32) + got_up[q, 0].astype(jnp.float32)
                total = total + got_down[q, level].astype(jnp.float32)
                out_ref[kept(q)] = total.astype(out_ref.dtype)

    for q in range(slices):
        local(q).start()
    greet(z, y, x, core)
    for q in range(slices):
        to_core(q).start()
    stages = (
        stage_zero,
        stage_one,
        stage_two,
        lambda q: stage_chain(q, 1),
        lambda q: stage_chain(q, 2),
        lambda q: (stage_chain(q, 3), stage_end(q)),
    )
    for tick in range(slices + lags[-1]):
        for lag, stage in zip((0,) + lags, stages):
            if 0 <= tick - lag < slices:
                stage(tick - lag)
    for q in range(slices):
        to_core(q).wait_send()
        to_one(q).wait_send()
        to_two(q).wait_send()
        for level in range(4):

            @pl.when(z == level)
            def sent():
                if level < 3:
                    to_up(q, level).wait_send()
                if level > 0:
                    to_down(q, level).wait_send()


def scatter_sum(array, base, chunk, out_dtype, slices, lags, collective_id, name):
    lanes = array.shape[-1]
    rows = chunk // slices
    low = array.dtype
    dma = pltpu.SemaphoreType.DMA
    return pl.pallas_call(
        functools.partial(scatter_kernel, base, slices, lags),
        out_shape=jax.ShapeDtypeStruct((chunk, lanes), out_dtype),
        in_specs=[pl.BlockSpec(memory_space=pl.ANY)],
        out_specs=pl.BlockSpec(memory_space=pltpu.VMEM),
        scratch_shapes=[
            pltpu.VMEM((slices, 4, 2, 2, rows, lanes), low),
            pltpu.VMEM((slices, 4, 2, 2, rows, lanes), low),
            pltpu.VMEM((slices, 4, 2, rows, lanes), low),
            pltpu.VMEM((slices, 4, rows, lanes), low),
            pltpu.VMEM((slices, 3, rows, lanes), low),
            pltpu.VMEM((slices, 3, rows, lanes), low),
            dma((slices,)),
            dma((slices,)), dma((slices,)),
            dma((slices,)), dma((slices,)),
            dma((slices,)), dma((slices,)),
            dma((slices,)), dma((slices,)),
            dma((slices,)), dma((slices,)),
        ],
        compiler_params=pltpu.CompilerParams(
            collective_id=collective_id, has_side_effects=True, vmem_limit_bytes=60 << 20
        ),
        name=name,
    )(array.reshape(4, 2, 2, 2, -1, lanes))


def total_kernel(x_ref, out_ref, held, got, send_sem, recv_sem):
    z, y, x, core = place()
    partners = (
        (z, y, x, 1 - core),
        (z, y, 1 - x, core),
        (z, 1 - y, x, core),
        (z + 1 - 2 * (z % 2), y, x, core),
        ((z + 2) % 4, y, x, core),
    )
    barrier = pltpu.get_barrier_semaphore()
    for where in partners:
        pl.semaphore_signal(barrier, inc=1, device_id=device_at(*where), device_id_type=MESH)
    pl.semaphore_wait(barrier, len(partners))
    sends = []
    for step, where in enumerate(partners):
        source = x_ref if step == 0 else held.at[step]
        copy = remote(source, got.at[step], send_sem.at[step], recv_sem.at[step], where)
        copy.start()
        copy.wait_recv()
        sends.append(copy)
        if step < len(partners) - 1:
            held[step + 1] = source[...] + got[step]
        else:
            out_ref[...] = source[...] + got[step]
    for copy in sends:
        copy.wait_send()


def total_of(array, collective_id):
    steps = 5
    return pl.pallas_call(
        total_kernel,
        out_shape=jax.ShapeDtypeStruct(array.shape, array.dtype),
        in_specs=[pl.BlockSpec(memory_space=pltpu.VMEM)],
        out_specs=pl.BlockSpec(memory_space=pltpu.VMEM),
        scratch_shapes=[
            pltpu.VMEM((steps,) + array.shape, array.dtype),
            pltpu.VMEM((steps,) + array.shape, array.dtype),
            pltpu.SemaphoreType.DMA((steps,)),
            pltpu.SemaphoreType.DMA((steps,)),
        ],
        compiler_params=pltpu.CompilerParams(collective_id=collective_id, has_side_effects=True),
        name="total_small",
    )(array)


def slot_kernel(scale_ref, tiles_ref, weight_ref, moment_ref, square_ref, weight_out, moment_out, square_out):
    columns = []
    for h in range(4):
        pieces = [tiles_ref[4 * j + h, 0] for j in range(8)]
        columns.append(jnp.concatenate(pieces, axis=0))
    gradient = scale_ref[0] * jnp.concatenate(columns, axis=1).astype(jnp.float32)
    weight, moment, square = adamw(weight_ref[0], moment_ref[0], square_ref[0], gradient, rate_dense)
    weight_out[0] = weight
    moment_out[0] = moment
    square_out[0] = square


def slot_update(scale, tiles, weight, moment, square):
    slots = weight.shape[0]
    block = pl.BlockSpec((1, BR, RANK), lambda s: (s, 0, 0))
    return tuple(
        pl.pallas_call(
            slot_kernel,
            grid=(slots,),
            in_specs=[
                pl.BlockSpec(memory_space=pltpu.SMEM),
                pl.BlockSpec((32, 1, 16, 128), lambda s: (0, s, 0, 0)),
                block,
                block,
                block,
            ],
            out_specs=[block] * 3,
            out_shape=[jax.ShapeDtypeStruct(weight.shape, jnp.float32)] * 3,
            name="slot_update",
        )(scale[None], tiles, weight, moment, square)
    )


NN = (((1,), (0,)), ((), ()))
NT = (((1,), (1,)), ((), ()))
TN = (((0,), (0,)), ((), ()))
CHUNKS = 3
CBLK = 9
CW = CBLK * BR
FCH = 9
FBLK = 6
ONE_AT = 6 * CHUNKS * CBLK
TWO_AT = ONE_AT + FCH * FBLK
THREE_AT = TWO_AT + 16
GROUPS = tuple((k * 27, 27) for k in (0, 3, 1, 4, 2, 5)) + ((ONE_AT, 54), (TWO_AT, 16), (THREE_AT, 8))
GELU_A = 0.7978845608028654
GELU_B = 0.044715


def mul(left, right, dims):
    return lax.dot_general(left, right, dims, preferred_element_type=jnp.float32)


def gelu_of(value):
    return 0.5 * value * (1.0 + jnp.tanh(GELU_A * (value + GELU_B * (value * value * value))))


def gelu_slope(value):
    bend = jnp.tanh(GELU_A * (value + GELU_B * (value * value * value)))
    inner = GELU_A * (1.0 + 3.0 * GELU_B * (value * value))
    return 0.5 * (1.0 + bend) + 0.5 * value * (1.0 - bend * bend) * inner


def dense_kernel(
    batch, tiles_hbm, pooled_ref, dense_ref, label_ref, head_ref, last_ref, cross_bias_ref, one_bias_ref,
    two_bias_ref, three_bias_ref, grads_hbm, grad_pooled_ref, grad_dense_ref, cross_grad_ref, small_ref,
    tiles, anchor, current, mixing, low, grad_anchor, wide_one, wide_two, stage, load_sem, store_sem,
):
    samples = dense_ref.shape[0]
    bf16, f32 = jnp.bfloat16, jnp.float32

    def load(group):
        first, count = GROUPS[group]
        return pltpu.make_async_copy(
            tiles_hbm.at[:, pl.ds(first, count)], tiles.at[:, pl.ds(first, count)], load_sem.at[group]
        )

    for group in range(len(GROUPS)):
        load(group).start()

    def matrix(first, count):
        columns = []
        for h in range(4):
            pieces = [tiles[4 * j + h, pl.ds(first, count)] for j in range(8)]
            columns.append(jnp.stack(pieces, axis=1).reshape(count * BR, 128))
        return jnp.concatenate(columns, axis=1)

    def store(slot, first, count):
        return pltpu.make_async_copy(
            stage.at[slot, :, pl.ds(0, count)], grads_hbm.at[:, pl.ds(first, count)], store_sem.at[slot]
        )

    def emit(slot, first, count, value):
        value = value.astype(bf16).reshape(count, BR, RANK)
        for j in range(8):
            for h in range(4):
                stage[slot, 4 * j + h, pl.ds(0, count)] = value[:, 16 * j : 16 * j + 16, 128 * h : 128 * h + 128]
        store(slot, first, count).start()

    for i in range(F + 1):
        block = dense_ref[...] if i == 0 else pooled_ref[(i - 1) * EMB : i * EMB, :].astype(f32).T
        c, at = i // CBLK, (i % CBLK) * BR
        anchor[c, :, at : at + BR] = block
        current[c, :, at : at + BR] = block
        low[c, :, at : at + BR] = block.astype(bf16)

    reduced = []
    for depth in range(LAYERS):
        load(2 * depth).wait()
        down, up = depth * 27, (LAYERS + depth) * 27
        total = lax.fori_loop(
            0,
            CHUNKS,
            lambda c, acc: acc + mul(low[depth * CHUNKS + c], matrix(down + c * CBLK, CBLK), NN),
            jnp.zeros((samples, RANK), f32),
        )
        small = total.astype(bf16)
        reduced.append(small)
        load(2 * depth + 1).wait()

        @pl.loop(0, CHUNKS)
        def mix(c):
            value = mul(small, matrix(up + c * CBLK, CBLK), NT) + cross_bias_ref[pl.ds(depth * CHUNKS + c, 1), :]
            mixing[depth * CHUNKS + c] = value
            after = anchor[c] * value + current[c]
            current[c] = after
            if depth + 1 < LAYERS:
                low[(depth + 1) * CHUNKS + c] = after.astype(bf16)

    at_row = lax.broadcasted_iota(jnp.int32, (BR, 4 * BR), 0)
    at_col = lax.broadcasted_iota(jnp.int32, (BR, 4 * BR), 1)
    widen = jnp.where(at_col % (2 * BR) == 2 * at_row + at_col // (2 * BR), 1.0, 0.0).astype(bf16)
    pick_row = lax.broadcasted_iota(jnp.int32, (8 * BR, BR), 0)
    pick_col = lax.broadcasted_iota(jnp.int32, (8 * BR, BR), 1)
    pick = jnp.where(pick_row % (2 * BR) == 2 * pick_col + pick_row // (4 * BR), 1.0, 0.0).astype(bf16)

    def widened(block):
        spreaded = mul(block, widen, NN).astype(bf16)
        return jnp.concatenate([spreaded[:, : 2 * BR], spreaded[:, 2 * BR :]], axis=0)

    def narrowed(wide):
        parts = []
        for p in range(2):
            value = wide[p * samples : (p + 1) * samples]
            high = value.astype(bf16)
            parts += [high, (value - high.astype(f32)).astype(bf16)]
        return mul(jnp.concatenate(parts, axis=1), pick, NN)

    load(6).wait()

    def first_step(c, acc):
        for m in range(3):
            at = pl.multiple_of((c % 3) * 3 * BR + m * BR, BR)
            wide_one[c, :, m * 2 * BR : (m + 1) * 2 * BR] = widened(current[c // 3, :, pl.ds(at, BR)].astype(bf16))
        return acc + mul(wide_one[c], matrix(ONE_AT + c * FBLK, FBLK), NN)

    total = lax.fori_loop(0, FCH, first_step, jnp.zeros((2 * samples, RANK), f32))
    pre_one = [total[p * samples : (p + 1) * samples] + one_bias_ref[pl.ds(p, 1), :] for p in range(2)]
    load(7).wait()
    total = jnp.zeros((2 * samples, RANK), f32)
    for c in range(2):
        hidden = gelu_of(pre_one[c]).astype(bf16)
        for m in range(4):
            wide_two[c, :, m * 2 * BR : (m + 1) * 2 * BR] = widened(hidden[:, m * BR : (m + 1) * BR])
        total = total + mul(wide_two[c], matrix(TWO_AT + c * 8, 8), NN)
    pre_two = [total[p * samples : (p + 1) * samples] + two_bias_ref[pl.ds(p, 1), :] for p in range(2)]
    load(8).wait()
    hidden_two = jnp.concatenate([gelu_of(value).astype(bf16) for value in pre_two], axis=1)
    pre_three = mul(hidden_two, matrix(THREE_AT, 8), NN) + three_bias_ref[...]
    hidden_three = gelu_of(pre_three)
    head = head_ref[...]
    logits = jnp.sum(hidden_three * head, axis=1, keepdims=True) + last_ref[...]
    labels = label_ref[...]
    losses = jnp.maximum(logits, 0.0) + jnp.log1p(jnp.exp(-jnp.abs(logits))) - labels * logits
    grad_logits = (1.0 / (1.0 + jnp.exp(-logits)) - labels) / batch
    small_ref[6:7, :] = jnp.broadcast_to(jnp.sum(losses, axis=0, keepdims=True), (1, RANK))
    small_ref[7:8, :] = jnp.broadcast_to(jnp.sum(grad_logits, axis=0, keepdims=True), (1, RANK))
    small_ref[5:6, :] = jnp.sum(hidden_three * grad_logits, axis=0, keepdims=True)

    grad_before = grad_logits * head * gelu_slope(pre_three)
    small_ref[4:5, :] = jnp.sum(grad_before, axis=0, keepdims=True)
    grad_low = grad_before.astype(bf16)
    emit(0, THREE_AT, 8, mul(hidden_two, grad_low, TN))
    grad_hidden = mul(grad_low, matrix(THREE_AT, 8), NT)
    parts = []
    for p in range(2):
        grad_before = grad_hidden[:, p * RANK : (p + 1) * RANK] * gelu_slope(pre_two[p])
        small_ref[2 + p : 3 + p, :] = jnp.sum(grad_before, axis=0, keepdims=True)
        parts.append(grad_before.astype(bf16))
    grad_low = jnp.concatenate(parts, axis=0)
    parts = []
    for c in range(2):
        if c == 1:
            store(0, THREE_AT, 8).wait()
        emit(1 - c, TWO_AT + c * 8, 8, mul(wide_two[c], grad_low, TN))
        wide = mul(grad_low, matrix(TWO_AT + c * 8, 8), NT)
        grad_hidden = jnp.concatenate(
            [narrowed(wide[:, m * 2 * BR : (m + 1) * 2 * BR]) for m in range(4)], axis=1
        )
        grad_before = grad_hidden * gelu_slope(pre_one[c])
        small_ref[c : c + 1, :] = jnp.sum(grad_before, axis=0, keepdims=True)
        parts.append(grad_before.astype(bf16))
    grad_one = jnp.concatenate(parts, axis=0)
    store(1, TWO_AT, 8).wait()
    store(0, TWO_AT + 8, 8).wait()

    @pl.loop(0, FCH)
    def first_back(c):
        slot = c % 2
        at = ONE_AT + c * FBLK

        @pl.when(c >= 2)
        def ready():
            store(slot, at, FBLK).wait()

        emit(slot, at, FBLK, mul(wide_one[c], grad_one, TN))
        wide = mul(grad_one, matrix(at, FBLK), NT)
        for m in range(3):
            spot = pl.multiple_of((c % 3) * 3 * BR + m * BR, BR)
            current[c // 3, :, pl.ds(spot, BR)] = narrowed(wide[:, m * 2 * BR : (m + 1) * 2 * BR])

    for slot in range(2):
        store(slot, ONE_AT, FBLK).wait()

    sent = 0
    for depth in reversed(range(LAYERS)):
        down, up = depth * 27, (LAYERS + depth) * 27
        base = sent

        def up_back(c, acc):
            slot = (base + c) % 2
            before = current[c]
            grad_mixing = anchor[c] * before
            cross_grad_ref[pl.ds(depth * CHUNKS + c, 1), :] = jnp.sum(grad_mixing, axis=0, keepdims=True)
            grad_low = grad_mixing.astype(bf16)

            @pl.when(base + c >= 2)
            def ready():
                store(slot, up, CBLK).wait()

            emit(slot, up + c * CBLK, CBLK, mul(grad_low, reduced[depth], TN))
            part = before * mixing[depth * CHUNKS + c]
            grad_anchor[c] = part if depth == LAYERS - 1 else grad_anchor[c] + part
            return acc + mul(grad_low, matrix(up + c * CBLK, CBLK), NN)

        total = lax.fori_loop(0, CHUNKS, up_back, jnp.zeros((samples, RANK), f32))
        grad_reduced = total.astype(bf16)

        @pl.loop(0, CHUNKS)
        def down_back(c):
            slot = (base + CHUNKS + c) % 2
            store(slot, down, CBLK).wait()
            emit(slot, down + c * CBLK, CBLK, mul(low[depth * CHUNKS + c], grad_reduced, TN))
            after = current[c] + mul(grad_reduced, matrix(down + c * CBLK, CBLK), NT)
            current[c] = after
            if depth == 0:
                grad_anchor[c] = grad_anchor[c] + after

        sent += 2 * CHUNKS
    grad_dense_ref[...] = grad_anchor[0, :, :EMB]
    for i in range(1, F + 1):
        c, at = i // CBLK, (i % CBLK) * BR
        grad_pooled_ref[:, (i - 1) * EMB : i * EMB] = grad_anchor[c, :, at : at + BR].astype(bf16)
    for slot in range(2):
        store(slot, 0, CBLK).wait()


def dense_step(tiles, pooled, dense_part, labels, head, bias_last, bias_cross, bias_one, bias_two, bias_three, batch):
    samples = dense_part.shape[0]
    f32, bf16 = jnp.float32, jnp.bfloat16
    whole = pl.BlockSpec(memory_space=pltpu.VMEM)
    away = pl.BlockSpec(memory_space=pl.ANY)
    shape = jax.ShapeDtypeStruct
    return pl.pallas_call(
        functools.partial(dense_kernel, batch),
        out_shape=[
            shape(tiles.shape, bf16),
            shape((samples, F * EMB), bf16),
            shape((samples, EMB), f32),
            shape((LAYERS * CHUNKS, CW), f32),
            shape((8, RANK), f32),
        ],
        in_specs=[away] + [whole] * 9,
        out_specs=[away] + [whole] * 4,
        scratch_shapes=[
            pltpu.VMEM(tiles.shape, bf16),
            pltpu.VMEM((CHUNKS, samples, CW), f32),
            pltpu.VMEM((CHUNKS, samples, CW), f32),
            pltpu.VMEM((LAYERS * CHUNKS, samples, CW), f32),
            pltpu.VMEM((LAYERS * CHUNKS, samples, CW), bf16),
            pltpu.VMEM((CHUNKS, samples, CW), f32),
            pltpu.VMEM((FCH, 2 * samples, FBLK * BR), bf16),
            pltpu.VMEM((2, 2 * samples, 8 * BR), bf16),
            pltpu.VMEM((2, 32, CBLK, 16, 128), bf16),
            pltpu.SemaphoreType.DMA((len(GROUPS),)),
            pltpu.SemaphoreType.DMA((2,)),
        ],
        compiler_params=pltpu.CompilerParams(vmem_limit_bytes=61 << 20),
        name="dense_step",
    )(tiles, pooled, dense_part, labels, head, bias_last, bias_cross, bias_one, bias_two, bias_three)


def body(
    row_ids,
    hot_counts,
    dense_feats,
    click_labels,
    block_owners,
    embed_table,
    table_moment,
    table_square,
    dense_slots,
    dense_moment,
    dense_square,
    dense_proj,
    proj_moment,
    proj_square,
    head_weight,
    head_moment,
    head_square,
    biases,
    bias_moment,
    bias_square,
):
    devices = lax.axis_size("row")
    samples = row_ids.shape[0]
    slot_count = dense_slots.shape[0]
    table_rows = embed_table.shape[1]
    block_count = block_owners.shape[0]
    capacity = samples * TOTAL // devices
    live_total = samples * TOTAL
    everything = lax.all_gather(dense_slots.astype(jnp.bfloat16), "row", axis=0, tiled=True)
    fetched = jnp.take(everything, block_owners, axis=0)
    cross_down, cross_up, first_matrix, middle, third_matrix = split_dense(
        fetched.reshape(block_count * BR, RANK)
    )
    bias_dense, bias_cross, bias_one, bias_two, bias_three, bias_last = split_bias(biases)
    flat_ids = row_ids.reshape(-1)
    live_mask = (
        lax.broadcasted_iota(jnp.int32, row_ids.shape, 2) < hot_counts[:, :, None]
    ).reshape(-1)
    sort_key = jnp.where(live_mask, flat_ids // table_rows, devices)
    full_order = jnp.argsort(sort_key, stable=True)
    slot_place = jnp.argsort(full_order)
    ordering = full_order[:live_total]
    segment = ordering // HOT
    requests = (segment % F * table_rows + jnp.take(flat_ids, ordering) % table_rows).reshape(
        devices, capacity
    )
    flat_table = embed_table.astype(jnp.bfloat16).reshape(F * table_rows, EMB)
    received = lax.all_to_all(requests, "row", split_axis=0, concat_axis=0, tiled=True)
    looked_up = jnp.take(flat_table, received, axis=0)
    returned = lax.all_to_all(looked_up, "row", split_axis=0, concat_axis=0, tiled=True)
    padded_rows = jnp.concatenate(
        [returned.reshape(-1, EMB), jnp.zeros((1, EMB), jnp.bfloat16)], axis=0
    )
    pick = jnp.where(live_mask, slot_place, live_total)
    in_slots = jnp.take(padded_rows, pick, axis=0).reshape(samples, F, HOT, EMB)
    pooled = jnp.sum(in_slots, axis=2, dtype=jnp.float32)
    pooled_low = pooled.astype(jnp.bfloat16).reshape(samples, F * EMB)
    dense_part = (
        jnp.dot(dense_feats, dense_proj, precision=highest, preferred_element_type=jnp.float32)
        + bias_dense
    )
    anchor = jnp.concatenate([dense_part, pooled_low.astype(jnp.float32)], axis=1)
    current = anchor
    stored = []
    for depth in range(LAYERS):
        saved, current = cross_forward(
            anchor, current, cross_down[depth], cross_up[depth], bias_cross[depth]
        )
        stored.append(saved)
    first_saved, hidden = dense_forward(current, first_matrix, bias_one)
    second_saved, hidden = dense_forward(hidden, middle, bias_two)
    third_saved, hidden = dense_forward(hidden, third_matrix, bias_three)
    logits = (
        jnp.dot(hidden, head_weight, precision=highest, preferred_element_type=jnp.float32)
        + bias_last
    )
    labels = click_labels.astype(jnp.float32)
    loss_local = jnp.sum(jax.nn.softplus(logits) - labels * logits)
    grad_logits = (jax.nn.sigmoid(logits) - labels) / (samples * devices)
    grad_head_local = jnp.dot(
        grad_logits, hidden, precision=highest, preferred_element_type=jnp.float32
    )
    grad_hidden = grad_logits[:, None] * head_weight[None, :]
    grad_hidden, grad_third, grad_bias_three = dense_backward(
        third_saved, third_matrix, grad_hidden
    )
    grad_hidden, grad_middle, grad_bias_two = dense_backward(second_saved, middle, grad_hidden)
    grad_current, grad_first, grad_bias_one = dense_backward(first_saved, first_matrix, grad_hidden)
    grad_anchor = jnp.zeros_like(anchor)
    grads_down = [None] * LAYERS
    grads_up = [None] * LAYERS
    grads_cross = [None] * LAYERS
    for depth in reversed(range(LAYERS)):
        grad_current, grad_part, grads_down[depth], grads_up[depth], grads_cross[depth] = (
            cross_backward(anchor, stored[depth], cross_down[depth], cross_up[depth], grad_current)
        )
        grad_anchor = grad_anchor + grad_part
    grad_anchor = grad_anchor + grad_current
    grad_pooled = grad_anchor[:, EMB:].astype(jnp.bfloat16).reshape(samples * F, EMB)
    sent_back = jnp.take(grad_pooled, segment, axis=0).reshape(devices, capacity, EMB)
    arrived = lax.all_to_all(sent_back, "row", split_axis=0, concat_axis=0, tiled=True)
    grad_table = table_gradient(arrived.reshape(-1, EMB), received.reshape(-1), table_rows)
    grad_proj_local = jnp.einsum(
        "sa,sb->ab",
        dense_feats,
        grad_anchor[:, :EMB],
        precision=highest,
        preferred_element_type=jnp.float32,
    )
    stacked = jnp.concatenate(
        [
            jnp.stack(grads_down).reshape(-1, RANK),
            jnp.stack(grads_up).reshape(-1, RANK),
            grad_first.reshape(-1, RANK),
            grad_middle.reshape(-1, RANK),
            grad_third,
            jnp.zeros((BR, RANK), jnp.float32),
        ],
        axis=0,
    ).reshape(block_count + 1, BR, RANK)
    matches = block_owners[None, :] == jnp.arange(devices * slot_count, dtype=jnp.int32)[:, None]
    inverse = jnp.sum(
        jnp.where(matches, jnp.arange(block_count, dtype=jnp.int32)[None, :], 0), axis=1
    )
    inverse = inverse + jnp.where(jnp.any(matches, axis=1), 0, block_count)
    grad_slots = lax.psum_scatter(
        jnp.take(stacked, inverse, axis=0), "row", scatter_dimension=0, tiled=True
    )
    bias_local = jnp.concatenate(
        [
            jnp.sum(grad_anchor[:, :EMB], axis=0),
            jnp.stack(grads_cross).reshape(-1),
            grad_bias_one,
            grad_bias_two,
            grad_bias_three,
            jnp.sum(grad_logits)[None],
        ]
    )
    loss_total, grad_proj, grad_head, grad_bias = lax.psum(
        (loss_local, grad_proj_local, grad_head_local, bias_local), "row"
    )
    local_squares = jnp.sum(grad_table * grad_table) + jnp.sum(grad_slots * grad_slots)
    squares = lax.psum(local_squares, "row")
    squares = (
        squares
        + jnp.sum(grad_proj * grad_proj)
        + jnp.sum(grad_head * grad_head)
        + jnp.sum(grad_bias * grad_bias)
    )
    grad_norm = jnp.sqrt(squares)
    clip_scale = clip_norm / jnp.maximum(grad_norm, clip_norm)
    table_new = adamw(embed_table, table_moment, table_square, clip_scale * grad_table, rate_table)
    dense_new = adamw(dense_slots, dense_moment, dense_square, clip_scale * grad_slots, rate_dense)
    proj_new = adamw(dense_proj, proj_moment, proj_square, clip_scale * grad_proj, rate_small)
    head_new = adamw(head_weight, head_moment, head_square, clip_scale * grad_head, rate_small)
    bias_new = adamw(biases, bias_moment, bias_square, clip_scale * grad_bias, rate_small)
    return (
        loss_total,
        grad_norm,
        table_new[0],
        table_new[1],
        table_new[2],
        dense_new[0],
        dense_new[1],
        dense_new[2],
        proj_new[0],
        proj_new[1],
        proj_new[2],
        head_new[0],
        head_new[1],
        head_new[2],
        bias_new[0],
        bias_new[1],
        bias_new[2],
    )


def body_counted(
    row_ids,
    hot_counts,
    dense_feats,
    click_labels,
    block_owners,
    embed_table,
    table_moment,
    table_square,
    dense_slots,
    dense_moment,
    dense_square,
    dense_proj,
    proj_moment,
    proj_square,
    head_weight,
    head_moment,
    head_square,
    biases,
    bias_moment,
    bias_square,
):
    devices = lax.axis_size("row")
    samples = row_ids.shape[0]
    slot_count = dense_slots.shape[0]
    table_rows = embed_table.shape[1]
    block_count = block_owners.shape[0]
    capacity = samples * TOTAL // devices
    live_total = samples * TOTAL
    bf16 = jnp.bfloat16
    slot_tiles = (
        dense_slots.astype(bf16)
        .reshape(slot_count, 8, 16, 4, 128)
        .transpose(1, 3, 0, 2, 4)
        .reshape(devices, slot_count * 16, 128)
    )
    slot_tiles = lax.all_to_all(slot_tiles, "row", split_axis=0, concat_axis=0, tiled=True)
    lanes = lax.broadcasted_iota(jnp.int32, row_ids.shape, 2)
    features = lax.broadcasted_iota(jnp.int32, row_ids.shape, 1)
    sample_of = lax.broadcasted_iota(jnp.int32, row_ids.shape, 0)
    key = (
        ((row_ids // table_rows) << 21)
        | (features << 16)
        | ((row_ids % table_rows) << 7)
        | sample_of
    )
    key = jnp.where(lanes < hot_counts[:, :, None], key, devices << 21)
    ordered = lax.sort(key.reshape(-1), is_stable=False)[:live_total]
    block_tiles = jnp.take(
        slot_tiles.reshape(devices * slot_count, 16, 128),
        block_owners + jnp.minimum(ordered[0], 0),
        axis=0,
        mode="clip",
    )
    tiles = lax.all_gather(block_tiles.reshape(block_count * 16, 128), "row", axis=0, tiled=True)
    tiles = tiles.reshape(devices, block_count, 16, 128)
    bias_dense, bias_cross, bias_one, bias_two, bias_three, bias_last = split_bias(biases)
    requests = (ordered & ((1 << 21) - 1)).reshape(devices, capacity)
    received = lax.all_to_all(requests, "row", split_axis=0, concat_axis=0, tiled=True)
    edges = jnp.arange(F + 1, dtype=jnp.int32) << 16
    offsets = jnp.sum((received[:, None, :] < edges[None, :, None]).astype(jnp.int32), axis=2)
    room = (capacity + samples - 1) // samples * samples + samples
    keys = jnp.pad(received, ((0, 0), (0, room - capacity)), constant_values=-1)
    counts, partial = count_tables(offsets, keys, embed_table, devices, samples)
    pooled = scatter_sum(partial, 0, F * EMB, bf16, 16, (2, 4, 6, 7, 8), 0, "scatter_pooled")
    dense_part = (
        jnp.dot(dense_feats, dense_proj, precision=highest, preferred_element_type=jnp.float32)
        + bias_dense
    )
    grad_tiles, grad_pooled, grad_dense, grad_cross, grad_small = dense_step(
        tiles,
        pooled,
        dense_part,
        click_labels.astype(jnp.float32)[:, None],
        head_weight[None, :],
        jnp.broadcast_to(bias_last, (samples, 1)),
        bias_cross.reshape(LAYERS * CHUNKS, CW),
        bias_one.reshape(2, RANK),
        bias_two.reshape(2, RANK),
        bias_three[None, :],
        samples * devices,
    )
    gathered_grads = lax.all_gather(grad_pooled, "row", axis=0, tiled=True)
    grad_mine = scatter_sum(
        grad_tiles.reshape(devices, block_count * 16, 128),
        0,
        block_count * 16,
        jnp.float32,
        16,
        (2, 4, 6, 7, 8),
        1,
        "scatter_dense",
    )
    grad_table, table_squares = row_grads(counts, gathered_grads)
    matches = block_owners[None, :] == jnp.arange(devices * slot_count, dtype=jnp.int32)[:, None]
    inverse = jnp.sum(
        jnp.where(matches, jnp.arange(block_count, dtype=jnp.int32)[None, :], 0), axis=1
    )
    named = jnp.any(matches, axis=1)
    returned = jnp.take(
        grad_mine.astype(bf16).reshape(block_count, 16, 128), inverse, axis=0, mode="clip"
    )
    returned = jnp.where(named[:, None, None], returned, 0)
    returned = lax.all_to_all(
        returned.reshape(devices, slot_count * 16, 128), "row", split_axis=0, concat_axis=0, tiled=True
    )
    grad_proj_local = jnp.einsum(
        "sa,sb->ab",
        dense_feats,
        grad_dense,
        precision=highest,
        preferred_element_type=jnp.float32,
    )
    bias_local = jnp.concatenate(
        [
            jnp.sum(grad_dense, axis=0),
            grad_cross.reshape(-1),
            grad_small[0:5].reshape(-1),
            grad_small[7, :1],
        ]
    )
    squares_local = jnp.sum(table_squares) + jnp.sum(grad_mine * grad_mine)
    packed = jnp.concatenate(
        [
            grad_small[6, :1],
            squares_local[None],
            grad_proj_local.reshape(-1),
            grad_small[5],
            bias_local,
        ]
    )
    room = -packed.shape[0] % 1024
    packed = total_of(jnp.pad(packed, (0, room)).reshape(-1, 128), 2).reshape(-1)
    cuts = [0, 1, 2]
    for size in (dense_proj.size, head_weight.size, biases.size):
        cuts.append(cuts[-1] + size)
    loss_total, squares, grad_proj, grad_head, grad_bias = [
        packed[first:last] for first, last in zip(cuts[:-1], cuts[1:])
    ]
    loss_total, squares = loss_total[0], squares[0]
    grad_proj = grad_proj.reshape(dense_proj.shape)
    squares = (
        squares
        + jnp.sum(grad_proj * grad_proj)
        + jnp.sum(grad_head * grad_head)
        + jnp.sum(grad_bias * grad_bias)
    )
    grad_norm = jnp.sqrt(squares)
    clip_scale = clip_norm / jnp.maximum(grad_norm, clip_norm)
    table_new = adamw(embed_table, table_moment, table_square, clip_scale * grad_table, rate_table)
    dense_new = slot_update(
        clip_scale,
        returned.reshape(devices, slot_count, 16, 128),
        dense_slots,
        dense_moment,
        dense_square,
    )
    proj_new = adamw(dense_proj, proj_moment, proj_square, clip_scale * grad_proj, rate_small)
    head_new = adamw(head_weight, head_moment, head_square, clip_scale * grad_head, rate_small)
    bias_new = adamw(biases, bias_moment, bias_square, clip_scale * grad_bias, rate_small)
    return (
        (loss_total, grad_norm) + table_new + dense_new + proj_new + head_new + bias_new
    )


def solution(mesh):
    in_specs = (
        P("row", None, None),
        P("row", None),
        P("row", None),
        P("row"),
        P(),
        P(None, "row", None),
        P(None, "row", None),
        P(None, "row", None),
        P("row", None, None),
        P("row", None, None),
        P("row", None, None),
        P(),
        P(),
        P(),
        P(),
        P(),
        P(),
        P(),
        P(),
        P(),
    )
    out_specs = (
        P(),
        P(),
        P(None, "row", None),
        P(None, "row", None),
        P(None, "row", None),
        P("row", None, None),
        P("row", None, None),
        P("row", None, None),
        P(),
        P(),
        P(),
        P(),
        P(),
        P(),
        P(),
        P(),
        P(),
    )
    fits = mesh.shape["row"] == 32
    chosen = body_counted if fits else body
    return jax.shard_map(chosen, mesh=mesh, in_specs=in_specs, out_specs=out_specs, check_vma=False)
```

```python
import functools

import jax
import jax.numpy as jnp
from jax import lax
from jax.experimental import pallas as pl
from jax.experimental.pallas import tpu as pltpu
from jax.sharding import PartitionSpec as P

F = 26
HOT = 30
EMB = 128
RANK = 512
LAYERS = 3
H1 = 1024
H2 = 1024
H3 = 512
BR = 128
STEP = 10
WIDTH = 3456
TOTAL = 403
NBIAS = 13057


beta_one = 0.9
beta_two = 0.999
adam_eps = 1e-12
decay_rate = 0.01
clip_norm = 0.001
rate_table = 0.3
rate_dense = 0.03
rate_small = 0.1
highest = lax.Precision.HIGHEST


def split_dense(flat):
    cross_rows = LAYERS * WIDTH
    first = 2 * cross_rows + WIDTH * H1 // RANK
    second = first + H1 * H2 // RANK
    return (
        flat[:cross_rows].reshape(LAYERS, WIDTH, RANK),
        flat[cross_rows : 2 * cross_rows].reshape(LAYERS, WIDTH, RANK),
        flat[2 * cross_rows : first].reshape(WIDTH, H1),
        flat[first:second].reshape(H1, H2),
        flat[second : second + H2 * H3 // RANK],
    )


def split_bias(biases):
    start = EMB + LAYERS * WIDTH
    return (
        biases[:EMB],
        biases[EMB:start].reshape(LAYERS, WIDTH),
        biases[start : start + H1],
        biases[start + H1 : start + H1 + H2],
        biases[start + H1 + H2 : start + H1 + H2 + H3],
        biases[NBIAS - 1],
    )


def cross_forward(anchor, current, weight_down, weight_up, bias_term):
    current_low = current.astype(jnp.bfloat16)
    reduced = jnp.dot(current_low, weight_down, preferred_element_type=jnp.float32).astype(
        jnp.bfloat16
    )
    mixing = (
        jnp.einsum("sr,wr->sw", reduced, weight_up, preferred_element_type=jnp.float32) + bias_term
    )
    return ((current_low, reduced, mixing), anchor * mixing + current)


def cross_backward(anchor, stored, weight_down, weight_up, grad_current):
    current_low, reduced, mixing = stored
    grad_mixing = anchor * grad_current
    grad_mixing_low = grad_mixing.astype(jnp.bfloat16)
    grad_up = jnp.einsum("sw,sr->wr", grad_mixing_low, reduced, preferred_element_type=jnp.float32)
    grad_reduced = jnp.dot(grad_mixing_low, weight_up, preferred_element_type=jnp.float32).astype(
        jnp.bfloat16
    )
    grad_down = jnp.einsum(
        "sw,sr->wr", current_low, grad_reduced, preferred_element_type=jnp.float32
    )
    grad_prev = grad_current + jnp.einsum(
        "sr,wr->sw", grad_reduced, weight_down, preferred_element_type=jnp.float32
    )
    return (grad_prev, grad_current * mixing, grad_down, grad_up, jnp.sum(grad_mixing, axis=0))


def dense_forward(inputs, weight, bias_term):
    inputs_low = inputs.astype(jnp.bfloat16)
    before = jnp.dot(inputs_low, weight, preferred_element_type=jnp.float32) + bias_term
    return ((inputs_low, before), jax.nn.gelu(before))


def dense_backward(stored, weight, grad_out):
    inputs_low, before = stored
    unused, gelu_back = jax.vjp(jax.nn.gelu, before)
    grad_before = gelu_back(grad_out)[0]
    grad_low = grad_before.astype(jnp.bfloat16)
    grad_weight = jnp.einsum("sa,sb->ab", inputs_low, grad_low, preferred_element_type=jnp.float32)
    grad_inputs = jnp.einsum("sb,ab->sa", grad_low, weight, preferred_element_type=jnp.float32)
    return (grad_inputs, grad_weight, jnp.sum(grad_before, axis=0))


def table_gradient(arrived, served, table_rows):
    received = served.shape[0]
    window = min(512, received)
    order_back = jnp.argsort(served, stable=True)
    sorted_ids = jnp.take(served, order_back)
    edges = jnp.arange(F + 1, dtype=jnp.int32) * table_rows
    bounds = jnp.sum((sorted_ids[None, :] < edges[:, None]).astype(jnp.int32), axis=1)
    starts = bounds[:-1]
    finish = bounds[1:]
    windows = (finish - starts + window - 1) // window
    ends_cum = jnp.cumsum(windows)
    begins_cum = ends_cum - windows
    step_count = F + received // window + 1
    turns = jnp.arange(step_count, dtype=jnp.int32)
    feature_of = jnp.sum((ends_cum[None, :] <= turns[:, None]).astype(jnp.int32), axis=1)
    feature_safe = jnp.minimum(feature_of, F - 1)
    first_row = (
        jnp.take(starts, feature_safe) + (turns - jnp.take(begins_cum, feature_safe)) * window
    )
    row_index = first_row[:, None] + jnp.arange(window, dtype=jnp.int32)[None, :]
    row_valid = (feature_of < F)[:, None] & (row_index < jnp.take(finish, feature_safe)[:, None])
    row_safe = jnp.minimum(row_index, received - 1)
    window_grads = jnp.take(arrived, jnp.take(order_back, row_safe), axis=0)
    local_row = jnp.take(sorted_ids, row_safe) - feature_safe[:, None] * table_rows
    local_row = jnp.where(row_valid, local_row, -1)
    selector = (
        local_row[:, :, None] == jnp.arange(table_rows, dtype=jnp.int32)[None, None, :]
    ).astype(jnp.bfloat16)
    partial_sums = jnp.einsum(
        "swr,swe->sre", selector, window_grads, preferred_element_type=jnp.float32
    )
    feature_pick = (feature_of[:, None] == jnp.arange(F, dtype=jnp.int32)[None, :]).astype(
        jnp.float32
    )
    return jnp.einsum(
        "sf,sre->fre",
        feature_pick,
        partial_sums,
        precision=highest,
        preferred_element_type=jnp.float32,
    )


def adamw(weight, moment, square, gradient, step_rate):
    moment = beta_one * moment + (1 - beta_one) * gradient
    square = beta_two * square + (1 - beta_two) * gradient * gradient
    corrected = moment / (1 - beta_one**STEP)
    scaled = square / (1 - beta_two**STEP)
    weight = weight - step_rate * (corrected / (jnp.sqrt(scaled) + adam_eps) + decay_rate * weight)
    return (weight, moment, square)


def count_kernel(devices, samples, table_rows, off_ref, most_ref, keys_ref, table_ref, counts_ref, partial_ref, low_ref, rows_ref, samples_ref):
    feature = pl.program_id(0)
    low_ref[...] = table_ref[0].T.astype(jnp.bfloat16)
    lane = lax.broadcasted_iota(jnp.int32, (1, samples), 1)
    row_iota = lax.broadcasted_iota(jnp.int32, (table_rows, 2 * samples), 0)
    sample_iota = lax.broadcasted_iota(jnp.int32, (2 * samples, 2 * samples), 0)

    def window(source, turn):
        start = off_ref[source * (F + 1) + feature] + turn * samples
        stop = off_ref[source * (F + 1) + feature + 1]
        tile = start // samples
        base = pl.multiple_of(tile * samples, samples)
        piece = keys_ref[pl.ds(source, 1), pl.ds(base, 2 * samples)]
        turned = pltpu.roll(piece, 2 * samples - (start - base), 1)[:, :samples]
        valid = lane < stop - start
        row = jnp.where(valid, (turned >> 7) & (table_rows - 1), -1)
        return row, turned & (samples - 1)

    def product(row, sample):
        row_hot = jnp.where(row_iota == row, 1.0, 0.0).astype(jnp.bfloat16)
        sample_hot = jnp.where(sample_iota == sample, 1.0, 0.0).astype(jnp.bfloat16)
        return lax.dot_general(
            row_hot, sample_hot, (((1,), (1,)), ((), ())), preferred_element_type=jnp.float32
        )

    def counted(first, turn):
        row_a, sample_a = window(first, turn)
        row_b, sample_b = window(first + 1, turn)
        return product(
            jnp.concatenate([row_a, row_b], axis=1),
            jnp.concatenate([sample_a, sample_b + samples], axis=1),
        )

    def span(first):
        return pl.ds(pl.multiple_of(first * samples, 2 * samples), 2 * samples)

    for source in range(devices):
        row, sample = window(source, 0)
        half = pl.ds((source % 2) * samples, samples)
        rows_ref[pl.ds(source // 2, 1), half] = row
        samples_ref[pl.ds(source // 2, 1), half] = sample + (source % 2) * samples

    def pair(step, carry):
        total = product(rows_ref[pl.ds(step, 1), :], samples_ref[pl.ds(step, 1), :])
        counts_ref[0, :, span(step * 2)] = total.astype(jnp.bfloat16)
        return carry

    lax.fori_loop(0, devices // 2, pair, 0, unroll=devices // 2)

    def late(step, carry):
        first = step * 2
        spans = [
            off_ref[(first + i) * (F + 1) + feature + 1] - off_ref[(first + i) * (F + 1) + feature]
            for i in (0, 1)
        ]
        turns = (jnp.maximum(spans[0], spans[1]) + samples - 1) // samples

        @pl.when(turns > 1)
        def again():
            total = lax.fori_loop(1, turns, lambda turn, acc: acc + counted(first, turn), counted(first, 0))
            counts_ref[0, :, span(first)] = total.astype(jnp.bfloat16)

        return carry

    @pl.when(most_ref[feature] > samples)
    def crowded():
        lax.fori_loop(0, devices // 2, late, 0)

    group = devices

    def pool(step, carry):
        part = jnp.dot(
            low_ref[...],
            counts_ref[0, :, pl.ds(pl.multiple_of(step * group * samples, group * samples), group * samples)],
            preferred_element_type=jnp.float32,
        ).astype(jnp.bfloat16)
        for i in range(group):
            partial_ref[step * group + i, 0] = part[:, i * samples : (i + 1) * samples]
        return carry

    lax.fori_loop(0, devices // group, pool, 0)


def count_tables(offsets, keys, embed_table, devices, samples):
    table_rows = embed_table.shape[1]
    return pl.pallas_call(
        functools.partial(count_kernel, devices, samples, table_rows),
        grid_spec=pltpu.PrefetchScalarGridSpec(
            num_scalar_prefetch=2,
            grid=(F,),
            in_specs=[
                pl.BlockSpec(keys.shape, lambda f, off, most: (0, 0)),
                pl.BlockSpec((1, table_rows, EMB), lambda f, off, most: (f, 0, 0)),
            ],
            out_specs=[
                pl.BlockSpec((1, table_rows, devices * samples), lambda f, off, most: (f, 0, 0)),
                pl.BlockSpec((devices, 1, EMB, samples), lambda f, off, most: (0, f, 0, 0)),
            ],
            scratch_shapes=[
                pltpu.VMEM((EMB, table_rows), jnp.bfloat16),
                pltpu.VMEM((devices // 2, 2 * samples), jnp.int32),
                pltpu.VMEM((devices // 2, 2 * samples), jnp.int32),
            ],
        ),
        out_shape=[
            jax.ShapeDtypeStruct((F, table_rows, devices * samples), jnp.bfloat16),
            jax.ShapeDtypeStruct((devices, F, EMB, samples), jnp.bfloat16),
        ],
        compiler_params=pltpu.CompilerParams(vmem_limit_bytes=48 << 20),
        name="count_tables",
    )(offsets.reshape(-1), jnp.max(offsets[:, 1:] - offsets[:, :-1], axis=0), keys, embed_table)


MESH = pl.DeviceIdType.MESH


def place():
    me = lax.axis_index("row")
    return me // 8, (me // 4) % 2, (me // 2) % 2, me % 2


def device_at(z, y, x, core):
    return (((z * 2 + y) * 2 + x) * 2 + core,)


def greet(z, y, x, core, far=0):
    barrier = pltpu.get_barrier_semaphore()

    def hail(*where):
        pl.semaphore_signal(barrier, inc=1, device_id=device_at(*where), device_id_type=MESH)

    hail(z, y, x, 1 - core)
    hail(z, y, 1 - x, core)
    hail(z, 1 - y, x, core)
    if far:
        hail((z + 2) % 4, y, x, core)

    @pl.when(z > 0)
    def below():
        hail(z - 1, y, x, core)

    @pl.when(z < 3)
    def above():
        hail(z + 1, y, x, core)

    @pl.when(jnp.logical_and(z > 0, z < 3))
    def inside():
        pl.semaphore_wait(barrier, 5 + far)

    @pl.when(jnp.logical_or(z == 0, z == 3))
    def edge():
        pl.semaphore_wait(barrier, 4 + far)


def remote(source, target, send_sem, recv_sem, where):
    return pltpu.make_async_remote_copy(
        src_ref=source,
        dst_ref=target,
        send_sem=send_sem,
        recv_sem=recv_sem,
        device_id=device_at(*where),
        device_id_type=MESH,
    )


def scatter_parts(
    base, kinds, x_ref, out_ref, own, got_core, got_one, tail, local_sem, send_core, recv_core,
    send_one, recv_one, send_two, recv_two, send_up, recv_up, send_down, recv_down, squares=None,
):
    z, y, x, core = place()
    slices = len(kinds)
    rows = own.shape[4]

    def span(q):
        return pl.ds(base + q * rows, rows)

    def kept(q):
        return pl.ds(q * rows, rows)

    def along_x(q):
        return kinds[q] % 2 == 0

    def chain_last(q):
        return kinds[q] < 2

    def got_two(q):
        return tail.at[q, 0:4] if chain_last(q) else tail.at[q, 12]

    def rising(q, first, count):
        if chain_last(q):
            return tail.at[q, 4 + first : 4 + first + count]
        return tail.at[q, 2 * first : 2 * first + 2 * count]

    def falling(q, count):
        if chain_last(q):
            return tail.at[q, 7 : 7 + count]
        return tail.at[q, 6 : 6 + 2 * count]

    def close(q, total):
        out_ref[kept(q)] = total.astype(out_ref.dtype)
        if squares is not None:
            squares[...] += jnp.sum((total * total).reshape(-1, 8, total.shape[1]), axis=0)

    def to_core(q):
        return remote(x_ref.at[:, :, :, 1 - core, span(q)], got_core.at[q], send_core.at[q], recv_core.at[q], (z, y, x, 1 - core))

    def to_one(q):
        if along_x(q):
            source, where = own.at[q, :, :, 1 - x], (z, y, 1 - x, core)
        else:
            source, where = own.at[q, :, 1 - y], (z, 1 - y, x, core)
        return remote(source, got_one.at[q], send_one.at[q], recv_one.at[q], where)

    def to_two(q):
        there = (z, 1 - y, x, core) if along_x(q) else (z, y, 1 - x, core)
        if chain_last(q):
            source = own.at[q, :, 1 - y, x] if along_x(q) else own.at[q, :, y, 1 - x]
        else:
            source = own.at[q, z, 1 - y, x] if along_x(q) else own.at[q, z, y, 1 - x]
        return remote(source, got_two(q), send_two.at[q], recv_two.at[q], there)

    def chained(q, first, count):
        part = pl.ds(first, count)
        if chain_last(q):
            return own.at[q, part, y, x]
        return own.at[q, part, :, x] if along_x(q) else own.at[q, part, y]

    def to_up(q, level):
        count = 3 - level
        target = rising(q, 0, count)
        if level == 0:
            source = chained(q, 1, 3)
            target = target if chain_last(q) else tail.at[q, 0:6].reshape(3, 2, rows, own.shape[5])
        else:
            source = rising(q, 1, count)
        return remote(source, target, send_up.at[q], recv_up.at[q], (z + 1, y, x, core))

    def to_down(q, level):
        count = level
        target = falling(q, count)
        if level == 3:
            source = chained(q, 0, 3)
            target = target if chain_last(q) else tail.at[q, 6:12].reshape(3, 2, rows, own.shape[5])
        else:
            source = target
        return remote(source, target, send_down.at[q], recv_down.at[q], (z - 1, y, x, core))

    def local(q):
        return pltpu.make_async_copy(x_ref.at[:, :, :, core, span(q)], own.at[q], local_sem.at[q])

    def width(q):
        return 1 if chain_last(q) else 2

    def own_at(q, t, b):
        if chain_last(q):
            return (q, t, y, x)
        return (q, t, b, x) if along_x(q) else (q, t, y, b)

    def rise_at(q, place_of, b):
        return (q, 4 + place_of) if chain_last(q) else (q, 2 * place_of + b)

    def fall_at(q, place_of, b):
        return (q, 7 + place_of) if chain_last(q) else (q, 6 + 2 * place_of + b)

    def start_chain(q):
        @pl.when(z == 0)
        def rise():
            to_up(q, 0).start()

        @pl.when(z == 3)
        def fall():
            to_down(q, 3).start()

    def stage_zero(q):
        local(q).wait()
        to_core(q).wait_recv()

        @pl.loop(0, 16)
        def step(i):
            a, b, c = i // 4, (i // 2) % 2, i % 2
            own[q, a, b, c] = own[q, a, b, c] + got_core[q, a, b, c]

        to_one(q).start()

    def stage_one(q):
        to_one(q).wait_recv()

        @pl.loop(0, 8)
        def step(i):
            a, b = i // 2, i % 2
            if along_x(q):
                own[q, a, b, x] = own[q, a, b, x] + got_one[q, a, b]
            else:
                own[q, a, y, b] = own[q, a, y, b] + got_one[q, a, b]

        if chain_last(q):
            to_two(q).start()
        else:
            start_chain(q)

    def stage_two(q):
        to_two(q).wait_recv()

        @pl.loop(0, 4)
        def step(a):
            own[q, a, y, x] = own[q, a, y, x] + tail[q, a]

        start_chain(q)

    def stage_chain(q, hop):
        @pl.when(z == hop)
        def rise():
            to_up(q, hop - 1).wait_recv()
            for t in range(hop + 1, 4):
                for b in range(width(q)):
                    at = rise_at(q, t - hop, b)
                    tail[at] = tail[at] + own[own_at(q, t, b)]
            if hop < 3:
                to_up(q, hop).start()

        @pl.when(z == 3 - hop)
        def fall():
            to_down(q, 4 - hop).wait_recv()
            for t in range(0, 3 - hop):
                for b in range(width(q)):
                    at = fall_at(q, t, b)
                    tail[at] = tail[at] + own[own_at(q, t, b)]
            if hop < 3:
                to_down(q, 3 - hop).start()

        if hop == 3:
            for level in range(4):

                @pl.when(z == level)
                def finish_chain():
                    for b in range(width(q)):
                        total = own[own_at(q, level, b)].astype(jnp.float32)
                        if level > 0:
                            total = total + tail[rise_at(q, 0, b)].astype(jnp.float32)
                        if level < 3:
                            total = total + tail[fall_at(q, level, b)].astype(jnp.float32)
                        if chain_last(q):
                            close(q, total)
                        else:
                            own[own_at(q, level, b)] = total.astype(own.dtype)

            if not chain_last(q):
                to_two(q).start()

    def stage_end(q):
        to_two(q).wait_recv()
        total = own[q, z, y, x].astype(jnp.float32) + tail[q, 12].astype(jnp.float32)
        close(q, total)

    def prepare():
        for q in range(slices):
            local(q).start()

    def begin():
        for q in range(slices):
            to_core(q).start()

    def step_of(number):
        def run(q):
            if number == 0:
                stage_zero(q)
            elif number == 1:
                stage_one(q)
            elif chain_last(q):
                stage_two(q) if number == 2 else stage_chain(q, number - 2)
            else:
                stage_end(q) if number == 5 else stage_chain(q, number - 1)

        return run

    stages = tuple(step_of(number) for number in range(6))

    def finish():
        for q in range(slices):
            to_core(q).wait_send()
            to_one(q).wait_send()
            to_two(q).wait_send()
            for level in range(4):

                @pl.when(z == level)
                def sent():
                    if level < 3:
                        to_up(q, level).wait_send()
                    if level > 0:
                        to_down(q, level).wait_send()

    return prepare, begin, stages, finish


def run_tick(tick, slices, lags, stages):
    for lag, stage in zip((0,) + lags, stages):
        if 0 <= tick - lag < slices:
            stage(tick - lag)


def scatter_kernel(base, kinds, lags, *refs):
    prepare, begin, stages, finish = scatter_parts(base, kinds, *refs)
    prepare()
    greet(*place())
    begin()
    for tick in range(len(kinds) + lags[-1]):
        run_tick(tick, len(kinds), lags, stages)
    finish()


def scatter_room(slices, rows, lanes, low):
    return [
        pltpu.VMEM((slices, 4, 2, 2, rows, lanes), low),
        pltpu.VMEM((slices, 4, 2, 2, rows, lanes), low),
        pltpu.VMEM((slices, 4, 2, rows, lanes), low),
        pltpu.VMEM((slices, 13, rows, lanes), low),
    ] + [pltpu.SemaphoreType.DMA((slices,))] * 11


def scatter_sum(array, base, chunk, out_dtype, kinds, lags, collective_id, name):
    lanes = array.shape[-1]
    slices = len(kinds)
    return pl.pallas_call(
        functools.partial(scatter_kernel, base, kinds, lags),
        out_shape=jax.ShapeDtypeStruct((chunk, lanes), out_dtype),
        in_specs=[pl.BlockSpec(memory_space=pl.ANY)],
        out_specs=pl.BlockSpec(memory_space=pltpu.VMEM),
        scratch_shapes=scatter_room(slices, chunk // slices, lanes, array.dtype),
        compiler_params=pltpu.CompilerParams(
            collective_id=collective_id, has_side_effects=True, vmem_limit_bytes=60 << 20
        ),
        name=name,
    )(array.reshape(4, 2, 2, 2, -1, lanes))


def spread_parts(
    slices, width, x_ref, out_ref, local_sem, send_one, recv_one, send_up, recv_up, send_down, recv_down,
    send_two, recv_two, send_core, recv_core,
):
    z, y, x, core = place()

    def span(q):
        return pl.ds(q * width, width)

    def local(q):
        return pltpu.make_async_copy(x_ref.at[span(q)], out_ref.at[z, y, x, core, span(q)], local_sem.at[q])

    def to_one(q):
        where = (z, y, 1 - x, core) if q % 2 == 0 else (z, 1 - y, x, core)
        target = out_ref.at[z, y, x, core, span(q)]
        return remote(x_ref.at[span(q)], target, send_one.at[q], recv_one.at[q], where)

    def level(block, q):
        if q % 2 == 0:
            return out_ref.at[block, y, :, core, span(q)]
        return out_ref.at[block, :, x, core, span(q)]

    def to_up(q, k):
        block = level(z - k, q)
        return remote(block, block, send_up.at[q, k], recv_up.at[q, k], (z + 1, y, x, core))

    def to_down(q, k):
        block = level(z + k, q)
        return remote(block, block, send_down.at[q, k], recv_down.at[q, k], (z - 1, y, x, core))

    def to_two(q):
        if q % 2 == 0:
            block, where = out_ref.at[:, y, :, core, span(q)], (z, 1 - y, x, core)
        else:
            block, where = out_ref.at[:, :, x, core, span(q)], (z, y, 1 - x, core)
        return remote(block, block, send_two.at[q], recv_two.at[q], where)

    def to_core(q):
        block = out_ref.at[:, :, :, core, span(q)]
        return remote(block, block, send_core.at[q], recv_core.at[q], (z, y, x, 1 - core))

    def send_on(q, k):
        @pl.when(jnp.logical_and(z < 3, z >= k))
        def rise():
            to_up(q, k).start()

        @pl.when(jnp.logical_and(z > 0, z + k <= 3))
        def fall():
            to_down(q, k).start()

    def stage_one(q):
        local(q).wait()
        to_one(q).wait_recv()
        send_on(q, 0)

    def stage_chain(q, hop):
        @pl.when(z >= hop)
        def rise():
            to_up(q, hop - 1).wait_recv()

        @pl.when(z + hop <= 3)
        def fall():
            to_down(q, hop - 1).wait_recv()

        if hop < 3:
            send_on(q, hop)
        else:
            to_two(q).start()

    def stage_two(q):
        to_two(q).wait_recv()
        to_core(q).start()

    def stage_core(q):
        to_core(q).wait_recv()

    def prepare():
        for q in range(slices):
            local(q).start()

    def begin():
        for q in range(slices):
            to_one(q).start()

    stages = (
        stage_one,
        lambda q: stage_chain(q, 1),
        lambda q: stage_chain(q, 2),
        lambda q: stage_chain(q, 3),
        stage_two,
        stage_core,
    )

    def finish():
        for q in range(slices):
            to_one(q).wait_send()
            for k in range(3):

                @pl.when(jnp.logical_and(z < 3, z >= k))
                def rise():
                    to_up(q, k).wait_send()

                @pl.when(jnp.logical_and(z > 0, z + k <= 3))
                def fall():
                    to_down(q, k).wait_send()

            to_two(q).wait_send()
            to_core(q).wait_send()

    return prepare, begin, stages, finish


def spread_room(slices):
    dma = pltpu.SemaphoreType.DMA
    return [dma((slices,))] * 3 + [dma((slices, 3))] * 4 + [dma((slices,))] * 4


def back_kernel(
    kinds, lags, spread_slices, spread_lags, compute_lag, order,
    x_ref, grads_ref, counts_ref, small_ref, out_ref, gathered_ref, table_ref, small_out, norm_ref, scale_ref,
    square_ref, held, got_small, send_small, recv_small, counts_buf, grads_buf, partial, ready, counts_sem, grads_sem, table_sem, *rest,
):
    slices = len(kinds)
    per_slice = F // spread_slices
    steps = 2 * per_slice
    last = 2 * F
    half = counts_buf.shape[2]
    prepare, begin, stages, finish = scatter_parts(0, kinds, x_ref, out_ref, *rest[:15], squares=square_ref)
    also_prepare, also_begin, also_stages, also_finish = spread_parts(
        spread_slices, per_slice, grads_ref, gathered_ref, *rest[15:]
    )

    def counts_load(n):
        at = pl.ds(pl.multiple_of((n % 2) * half, half), half)
        return pltpu.make_async_copy(counts_ref.at[n // 2, :, at], counts_buf.at[n % 2], counts_sem.at[n % 2])

    def grads_load(n):
        source = gathered_ref.at[pl.ds((n % 2) * 2, 2), :, :, :, n // 2]
        return pltpu.make_async_copy(source, grads_buf.at[n % 2], grads_sem.at[n % 2])

    def table_store(f):
        return pltpu.make_async_copy(ready.at[f % 2], table_ref.at[f], table_sem.at[f % 2])

    def compute(q):
        first = q * steps
        grads_load(first).start()
        grads_load(first + 1).start()

        @pl.loop(0, steps)
        def step(i):
            n = first + i
            f = n // 2
            slot = n % 2
            counts_load(n).wait()
            grads_load(n).wait()
            part = jnp.dot(
                counts_buf[slot], grads_buf[slot].reshape(half, EMB), preferred_element_type=jnp.float32
            )

            @pl.when(n + 2 < last)
            def more():
                counts_load(n + 2).start()

            @pl.when(i + 2 < steps)
            def also():
                grads_load(n + 2).start()

            @pl.when(slot == 0)
            def keep():
                partial[...] = part

            @pl.when(slot == 1)
            def close():
                @pl.when(f >= 2)
                def free():
                    table_store(f).wait()

                total = partial[...] + part
                ready[f % 2] = total
                table_store(f).start()
                square_ref[...] += jnp.sum((total * total).reshape(-1, 8, EMB), axis=0)

    also_prepare()
    prepare()
    counts_load(0).start()
    counts_load(1).start()
    square_ref[...] = jnp.zeros_like(square_ref)
    greet(*place(), far=1)
    also_begin()
    begin()
    for tick in range(max(slices + lags[-1], spread_slices + compute_lag)):
        for which in order:
            if which == 0:
                run_tick(tick, spread_slices, spread_lags, also_stages)
            elif which == 1:
                run_tick(tick, slices, lags, stages)
            elif which == 2:
                if 0 <= tick - compute_lag < spread_slices:
                    compute(tick - compute_lag)
    z, y, x, core = place()
    row = lax.broadcasted_iota(jnp.int32, small_ref.shape, 0)
    lane = lax.broadcasted_iota(jnp.int32, small_ref.shape, 1)
    own_square = jnp.sum(jnp.sum(square_ref[...], axis=1, keepdims=True), axis=0, keepdims=True)
    held[0] = small_ref[...] + jnp.where(jnp.logical_and(row == 0, lane == 1), own_square, 0.0)
    partners = (
        (z, y, x, 1 - core),
        (z, y, 1 - x, core),
        (z, 1 - y, x, core),
        (z + 1 - 2 * (z % 2), y, x, core),
        ((z + 2) % 4, y, x, core),
    )
    sends = []
    for step, where in enumerate(partners):
        copy = remote(held.at[step], got_small.at[step], send_small.at[step], recv_small.at[step], where)
        copy.start()
        copy.wait_recv()
        sends.append(copy)
        total = held[step] + got_small[step]
        if step < len(partners) - 1:
            held[step + 1] = total
    small_out[...] = total
    squares = jnp.where(row > 0, total * total, jnp.where(lane == 1, total, 0.0))
    norm = jnp.sqrt(jnp.sum(jnp.sum(squares, axis=1, keepdims=True), axis=0, keepdims=True))
    norm_ref[...] = norm
    scale_ref[...] = clip_norm / jnp.maximum(norm, clip_norm)
    for copy in sends:
        copy.wait_send()
    for f in (F - 2, F - 1):
        table_store(f).wait()
    also_finish()
    finish()


def back_exchange(tiles, grads, counts, small, kinds, lags, spread_slices, spread_lags, compute_lag, order, collective_id):
    chunk, lanes = tiles.shape[-2:]
    slices = len(kinds)
    table_rows, batch = counts.shape[1:]
    samples = grads.shape[1]
    f32, bf16 = jnp.float32, jnp.bfloat16
    away = pl.BlockSpec(memory_space=pl.ANY)
    near = pl.BlockSpec(memory_space=pltpu.VMEM)
    dma = pltpu.SemaphoreType.DMA
    mine, _, table, total, norm, scale = pl.pallas_call(
        functools.partial(back_kernel, kinds, lags, spread_slices, spread_lags, compute_lag, order),
        out_shape=[
            jax.ShapeDtypeStruct((chunk, lanes), bf16),
            jax.ShapeDtypeStruct((4, 2, 2, 2) + grads.shape, bf16),
            jax.ShapeDtypeStruct((F, table_rows, EMB), f32),
            jax.ShapeDtypeStruct(small.shape, f32),
            jax.ShapeDtypeStruct((1, 1), f32),
            jax.ShapeDtypeStruct((1, 1), f32),
        ],
        in_specs=[away] * 3 + [near],
        out_specs=[near, away, away] + [near] * 3,
        scratch_shapes=[
            pltpu.VMEM((8, EMB), f32),
            pltpu.VMEM((5,) + small.shape, f32),
            pltpu.VMEM((5,) + small.shape, f32),
            dma((5,)),
            dma((5,)),
            pltpu.VMEM((2, table_rows, batch // 2), bf16),
            pltpu.VMEM((2, 2, 2, 2, 2, samples, EMB), bf16),
            pltpu.VMEM((table_rows, EMB), f32),
            pltpu.VMEM((2, table_rows, EMB), f32),
            dma((2,)),
            dma((2,)),
            dma((2,)),
        ]
        + scatter_room(slices, chunk // slices, lanes, bf16)
        + spread_room(spread_slices),
        compiler_params=pltpu.CompilerParams(
            collective_id=collective_id, has_side_effects=True, vmem_limit_bytes=61 << 20
        ),
        name="back_exchange",
    )(tiles.reshape(4, 2, 2, 2, chunk, lanes), grads, counts, small)
    return mine, table, total, norm[0, 0], scale[0, 0]


def slot_kernel(scale_ref, tiles_ref, weight_ref, moment_ref, square_ref, weight_out, moment_out, square_out):
    columns = []
    count = tiles_ref.shape[1]
    for h in range(4):
        pieces = [tiles_ref[4 * j + h] for j in range(8)]
        columns.append(jnp.stack(pieces, axis=1).reshape(count, BR, 128))
    gradient = scale_ref[0] * jnp.concatenate(columns, axis=2).astype(jnp.float32)
    weight, moment, square = adamw(weight_ref[...], moment_ref[...], square_ref[...], gradient, rate_dense)
    weight_out[...] = weight
    moment_out[...] = moment
    square_out[...] = square


def slot_update(scale, tiles, weight, moment, square):
    slots = weight.shape[0]
    group = 3
    block = pl.BlockSpec((group, BR, RANK), lambda s: (s, 0, 0))
    return tuple(
        pl.pallas_call(
            slot_kernel,
            grid=(slots // group,),
            in_specs=[
                pl.BlockSpec(memory_space=pltpu.SMEM),
                pl.BlockSpec((32, group, 16, 128), lambda s: (0, s, 0, 0)),
                block,
                block,
                block,
            ],
            out_specs=[block] * 3,
            out_shape=[jax.ShapeDtypeStruct(weight.shape, jnp.float32)] * 3,
            compiler_params=pltpu.CompilerParams(vmem_limit_bytes=48 << 20),
            name="slot_update",
        )(scale.reshape(1), tiles, weight, moment, square)
    )


NN = (((1,), (0,)), ((), ()))
NT = (((1,), (1,)), ((), ()))
TN = (((0,), (0,)), ((), ()))
CHUNKS = 3
CBLK = 9
CW = CBLK * BR
FCH = 9
FBLK = 6
ONE_AT = 6 * CHUNKS * CBLK
TWO_AT = ONE_AT + FCH * FBLK
THREE_AT = TWO_AT + 16
GROUPS = tuple((k * 27, 27) for k in (0, 3, 1, 4, 2, 5)) + ((ONE_AT, 54), (TWO_AT, 16), (THREE_AT, 8))
NDENSE = 13
PROJ_ROW = 1
HEAD_ROW = PROJ_ROW + NDENSE
DENSE_ROW = HEAD_ROW + 4
CROSS_ROW = DENSE_ROW + 1
ONE_ROW = CROSS_ROW + LAYERS * 27
TWO_ROW = ONE_ROW + 8
THREE_ROW = TWO_ROW + 8
LAST_ROW = THREE_ROW + 4
SMALL_ROWS = 128
GELU_A = 0.7978845608028654
GELU_B = 0.044715


def mul(left, right, dims):
    return lax.dot_general(left, right, dims, preferred_element_type=jnp.float32)


def gelu_of(value):
    return 0.5 * value * (1.0 + jnp.tanh(GELU_A * (value + GELU_B * (value * value * value))))


def gelu_slope(value):
    bend = jnp.tanh(GELU_A * (value + GELU_B * (value * value * value)))
    inner = GELU_A * (1.0 + 3.0 * GELU_B * (value * value))
    return 0.5 * (1.0 + bend) + 0.5 * value * (1.0 - bend * bend) * inner


def dense_kernel(
    batch, tiles_hbm, pooled_ref, feats_ref, dense_ref, label_ref, head_ref, last_ref, cross_bias_ref, one_bias_ref,
    two_bias_ref, three_bias_ref, grads_hbm, grad_pooled_ref, small_ref,
    tiles, anchor, current, mixing, low, grad_anchor, wide_one, wide_two, stage, load_sem, store_sem,
):
    samples = dense_ref.shape[0]
    bf16, f32 = jnp.bfloat16, jnp.float32

    def load(group):
        first, count = GROUPS[group]
        return pltpu.make_async_copy(
            tiles_hbm.at[:, pl.ds(first, count)], tiles.at[:, pl.ds(first, count)], load_sem.at[group]
        )

    for group in range(len(GROUPS)):
        load(group).start()

    def matrix(first, count):
        columns = []
        for h in range(4):
            pieces = [tiles[4 * j + h, pl.ds(first, count)] for j in range(8)]
            columns.append(jnp.stack(pieces, axis=1).reshape(count * BR, 128))
        return jnp.concatenate(columns, axis=1)

    def store(slot, first, count):
        return pltpu.make_async_copy(
            stage.at[slot, :, pl.ds(0, count)], grads_hbm.at[:, pl.ds(first, count)], store_sem.at[slot]
        )

    def emit(slot, first, count, value):
        value = value.astype(bf16).reshape(count, BR, RANK)
        for j in range(8):
            for h in range(4):
                stage[slot, 4 * j + h, pl.ds(0, count)] = value[:, 16 * j : 16 * j + 16, 128 * h : 128 * h + 128]
        store(slot, first, count).start()

    small_ref[...] = jnp.zeros_like(small_ref)

    def note(row, value):
        for m in range(value.shape[1] // 128):
            small_ref[pl.ds(row + m, 1), :] = value[:, m * 128 : (m + 1) * 128]

    for i in range(F + 1):
        block = dense_ref[...] if i == 0 else pooled_ref[(i - 1) * EMB : i * EMB, :].astype(f32).T
        c, at = i // CBLK, (i % CBLK) * BR
        anchor[c, :, at : at + BR] = block
        current[c, :, at : at + BR] = block
        low[c, :, at : at + BR] = block.astype(bf16)

    reduced = []
    for depth in range(LAYERS):
        load(2 * depth).wait()
        down, up = depth * 27, (LAYERS + depth) * 27
        total = lax.fori_loop(
            0,
            CHUNKS,
            lambda c, acc: acc + mul(low[depth * CHUNKS + c], matrix(down + c * CBLK, CBLK), NN),
            jnp.zeros((samples, RANK), f32),
        )
        small = total.astype(bf16)
        reduced.append(small)
        load(2 * depth + 1).wait()

        @pl.loop(0, CHUNKS)
        def mix(c):
            value = mul(small, matrix(up + c * CBLK, CBLK), NT) + cross_bias_ref[pl.ds(depth * CHUNKS + c, 1), :]
            mixing[depth * CHUNKS + c] = value
            after = anchor[c] * value + current[c]
            current[c] = after
            if depth + 1 < LAYERS:
                low[(depth + 1) * CHUNKS + c] = after.astype(bf16)

    at_row = lax.broadcasted_iota(jnp.int32, (BR, 4 * BR), 0)
    at_col = lax.broadcasted_iota(jnp.int32, (BR, 4 * BR), 1)
    widen = jnp.where(at_col % (2 * BR) == 2 * at_row + at_col // (2 * BR), 1.0, 0.0).astype(bf16)
    pick_row = lax.broadcasted_iota(jnp.int32, (8 * BR, BR), 0)
    pick_col = lax.broadcasted_iota(jnp.int32, (8 * BR, BR), 1)
    pick = jnp.where(pick_row % (2 * BR) == 2 * pick_col + pick_row // (4 * BR), 1.0, 0.0).astype(bf16)

    def widened(block):
        spreaded = mul(block, widen, NN).astype(bf16)
        return jnp.concatenate([spreaded[:, : 2 * BR], spreaded[:, 2 * BR :]], axis=0)

    def narrowed(wide):
        parts = []
        for p in range(2):
            value = wide[p * samples : (p + 1) * samples]
            high = value.astype(bf16)
            parts += [high, (value - high.astype(f32)).astype(bf16)]
        return mul(jnp.concatenate(parts, axis=1), pick, NN)

    load(6).wait()

    def first_step(c, acc):
        for m in range(3):
            at = pl.multiple_of((c % 3) * 3 * BR + m * BR, BR)
            wide_one[c, :, m * 2 * BR : (m + 1) * 2 * BR] = widened(current[c // 3, :, pl.ds(at, BR)].astype(bf16))
        return acc + mul(wide_one[c], matrix(ONE_AT + c * FBLK, FBLK), NN)

    total = lax.fori_loop(0, FCH, first_step, jnp.zeros((2 * samples, RANK), f32))
    pre_one = [total[p * samples : (p + 1) * samples] + one_bias_ref[pl.ds(p, 1), :] for p in range(2)]
    load(7).wait()
    total = jnp.zeros((2 * samples, RANK), f32)
    for c in range(2):
        hidden = gelu_of(pre_one[c]).astype(bf16)
        for m in range(4):
            wide_two[c, :, m * 2 * BR : (m + 1) * 2 * BR] = widened(hidden[:, m * BR : (m + 1) * BR])
        total = total + mul(wide_two[c], matrix(TWO_AT + c * 8, 8), NN)
    pre_two = [total[p * samples : (p + 1) * samples] + two_bias_ref[pl.ds(p, 1), :] for p in range(2)]
    load(8).wait()
    hidden_two = jnp.concatenate([gelu_of(value).astype(bf16) for value in pre_two], axis=1)
    pre_three = mul(hidden_two, matrix(THREE_AT, 8), NN) + three_bias_ref[...]
    hidden_three = gelu_of(pre_three)
    head = head_ref[...]
    logits = jnp.sum(hidden_three * head, axis=1, keepdims=True) + last_ref[...]
    labels = label_ref[...]
    losses = jnp.maximum(logits, 0.0) + jnp.log1p(jnp.exp(-jnp.abs(logits))) - labels * logits
    grad_logits = (1.0 / (1.0 + jnp.exp(-logits)) - labels) / batch
    first_lane = lax.broadcasted_iota(jnp.int32, (1, 128), 1) == 0
    note(0, jnp.where(first_lane, jnp.sum(losses, axis=0, keepdims=True), 0.0))
    note(LAST_ROW, jnp.where(first_lane, jnp.sum(grad_logits, axis=0, keepdims=True), 0.0))
    note(HEAD_ROW, jnp.sum(hidden_three * grad_logits, axis=0, keepdims=True))

    grad_before = grad_logits * head * gelu_slope(pre_three)
    note(THREE_ROW, jnp.sum(grad_before, axis=0, keepdims=True))
    grad_low = grad_before.astype(bf16)
    emit(0, THREE_AT, 8, mul(hidden_two, grad_low, TN))
    grad_hidden = mul(grad_low, matrix(THREE_AT, 8), NT)
    parts = []
    for p in range(2):
        grad_before = grad_hidden[:, p * RANK : (p + 1) * RANK] * gelu_slope(pre_two[p])
        note(TWO_ROW + 4 * p, jnp.sum(grad_before, axis=0, keepdims=True))
        parts.append(grad_before.astype(bf16))
    grad_low = jnp.concatenate(parts, axis=0)
    parts = []
    for c in range(2):
        if c == 1:
            store(0, THREE_AT, 8).wait()
        emit(1 - c, TWO_AT + c * 8, 8, mul(wide_two[c], grad_low, TN))
        wide = mul(grad_low, matrix(TWO_AT + c * 8, 8), NT)
        grad_hidden = jnp.concatenate(
            [narrowed(wide[:, m * 2 * BR : (m + 1) * 2 * BR]) for m in range(4)], axis=1
        )
        grad_before = grad_hidden * gelu_slope(pre_one[c])
        note(ONE_ROW + 4 * c, jnp.sum(grad_before, axis=0, keepdims=True))
        parts.append(grad_before.astype(bf16))
    grad_one = jnp.concatenate(parts, axis=0)
    store(1, TWO_AT, 8).wait()
    store(0, TWO_AT + 8, 8).wait()

    @pl.loop(0, FCH)
    def first_back(c):
        slot = c % 2
        at = ONE_AT + c * FBLK

        @pl.when(c >= 2)
        def ready():
            store(slot, at, FBLK).wait()

        emit(slot, at, FBLK, mul(wide_one[c], grad_one, TN))
        wide = mul(grad_one, matrix(at, FBLK), NT)
        for m in range(3):
            spot = pl.multiple_of((c % 3) * 3 * BR + m * BR, BR)
            current[c // 3, :, pl.ds(spot, BR)] = narrowed(wide[:, m * 2 * BR : (m + 1) * 2 * BR])

    for slot in range(2):
        store(slot, ONE_AT, FBLK).wait()

    sent = 0
    for depth in reversed(range(LAYERS)):
        down, up = depth * 27, (LAYERS + depth) * 27
        base = sent

        def up_back(c, acc):
            slot = (base + c) % 2
            before = current[c]
            grad_mixing = anchor[c] * before
            note(CROSS_ROW + depth * 27 + c * CBLK, jnp.sum(grad_mixing, axis=0, keepdims=True))
            grad_low = grad_mixing.astype(bf16)

            @pl.when(base + c >= 2)
            def ready():
                store(slot, up, CBLK).wait()

            emit(slot, up + c * CBLK, CBLK, mul(grad_low, reduced[depth], TN))
            part = before * mixing[depth * CHUNKS + c]
            grad_anchor[c] = part if depth == LAYERS - 1 else grad_anchor[c] + part
            return acc + mul(grad_low, matrix(up + c * CBLK, CBLK), NN)

        total = lax.fori_loop(0, CHUNKS, up_back, jnp.zeros((samples, RANK), f32))
        grad_reduced = total.astype(bf16)

        @pl.loop(0, CHUNKS)
        def down_back(c):
            slot = (base + CHUNKS + c) % 2
            store(slot, down, CBLK).wait()
            emit(slot, down + c * CBLK, CBLK, mul(low[depth * CHUNKS + c], grad_reduced, TN))
            after = current[c] + mul(grad_reduced, matrix(down + c * CBLK, CBLK), NT)
            current[c] = after
            if depth == 0:
                grad_anchor[c] = grad_anchor[c] + after

        sent += 2 * CHUNKS
    grad_dense = grad_anchor[0, :, :EMB]
    note(DENSE_ROW, jnp.sum(grad_dense, axis=0, keepdims=True))
    small_ref[PROJ_ROW : PROJ_ROW + NDENSE, :] = lax.dot_general(
        feats_ref[...], grad_dense, TN, precision=highest, preferred_element_type=f32
    )[:NDENSE]
    for i in range(1, F + 1):
        c, at = i // CBLK, (i % CBLK) * BR
        grad_pooled_ref[i - 1] = grad_anchor[c, :, at : at + BR].astype(bf16)
    for slot in range(2):
        store(slot, 0, CBLK).wait()


def dense_step(tiles, pooled, feats, dense_part, labels, head, bias_last, bias_cross, bias_one, bias_two, bias_three, batch):
    samples = dense_part.shape[0]
    f32, bf16 = jnp.float32, jnp.bfloat16
    whole = pl.BlockSpec(memory_space=pltpu.VMEM)
    away = pl.BlockSpec(memory_space=pl.ANY)
    shape = jax.ShapeDtypeStruct
    return pl.pallas_call(
        functools.partial(dense_kernel, batch),
        out_shape=[
            shape(tiles.shape, bf16),
            shape((F, samples, EMB), bf16),
            shape((SMALL_ROWS, 128), f32),
        ],
        in_specs=[away] + [whole] * 10,
        out_specs=[away] + [whole] * 2,
        scratch_shapes=[
            pltpu.VMEM(tiles.shape, bf16),
            pltpu.VMEM((CHUNKS, samples, CW), f32),
            pltpu.VMEM((CHUNKS, samples, CW), f32),
            pltpu.VMEM((LAYERS * CHUNKS, samples, CW), f32),
            pltpu.VMEM((LAYERS * CHUNKS, samples, CW), bf16),
            pltpu.VMEM((CHUNKS, samples, CW), f32),
            pltpu.VMEM((FCH, 2 * samples, FBLK * BR), bf16),
            pltpu.VMEM((2, 2 * samples, 8 * BR), bf16),
            pltpu.VMEM((2, 32, CBLK, 16, 128), bf16),
            pltpu.SemaphoreType.DMA((len(GROUPS),)),
            pltpu.SemaphoreType.DMA((2,)),
        ],
        compiler_params=pltpu.CompilerParams(vmem_limit_bytes=61 << 20),
        name="dense_step",
    )(tiles, pooled, feats, dense_part, labels, head, bias_last, bias_cross, bias_one, bias_two, bias_three)


def body(
    row_ids,
    hot_counts,
    dense_feats,
    click_labels,
    block_owners,
    embed_table,
    table_moment,
    table_square,
    dense_slots,
    dense_moment,
    dense_square,
    dense_proj,
    proj_moment,
    proj_square,
    head_weight,
    head_moment,
    head_square,
    biases,
    bias_moment,
    bias_square,
):
    devices = lax.axis_size("row")
    samples = row_ids.shape[0]
    slot_count = dense_slots.shape[0]
    table_rows = embed_table.shape[1]
    block_count = block_owners.shape[0]
    capacity = samples * TOTAL // devices
    live_total = samples * TOTAL
    everything = lax.all_gather(dense_slots.astype(jnp.bfloat16), "row", axis=0, tiled=True)
    fetched = jnp.take(everything, block_owners, axis=0)
    cross_down, cross_up, first_matrix, middle, third_matrix = split_dense(
        fetched.reshape(block_count * BR, RANK)
    )
    bias_dense, bias_cross, bias_one, bias_two, bias_three, bias_last = split_bias(biases)
    flat_ids = row_ids.reshape(-1)
    live_mask = (
        lax.broadcasted_iota(jnp.int32, row_ids.shape, 2) < hot_counts[:, :, None]
    ).reshape(-1)
    sort_key = jnp.where(live_mask, flat_ids // table_rows, devices)
    full_order = jnp.argsort(sort_key, stable=True)
    slot_place = jnp.argsort(full_order)
    ordering = full_order[:live_total]
    segment = ordering // HOT
    requests = (segment % F * table_rows + jnp.take(flat_ids, ordering) % table_rows).reshape(
        devices, capacity
    )
    flat_table = embed_table.astype(jnp.bfloat16).reshape(F * table_rows, EMB)
    received = lax.all_to_all(requests, "row", split_axis=0, concat_axis=0, tiled=True)
    looked_up = jnp.take(flat_table, received, axis=0)
    returned = lax.all_to_all(looked_up, "row", split_axis=0, concat_axis=0, tiled=True)
    padded_rows = jnp.concatenate(
        [returned.reshape(-1, EMB), jnp.zeros((1, EMB), jnp.bfloat16)], axis=0
    )
    pick = jnp.where(live_mask, slot_place, live_total)
    in_slots = jnp.take(padded_rows, pick, axis=0).reshape(samples, F, HOT, EMB)
    pooled = jnp.sum(in_slots, axis=2, dtype=jnp.float32)
    pooled_low = pooled.astype(jnp.bfloat16).reshape(samples, F * EMB)
    dense_part = (
        jnp.dot(dense_feats, dense_proj, precision=highest, preferred_element_type=jnp.float32)
        + bias_dense
    )
    anchor = jnp.concatenate([dense_part, pooled_low.astype(jnp.float32)], axis=1)
    current = anchor
    stored = []
    for depth in range(LAYERS):
        saved, current = cross_forward(
            anchor, current, cross_down[depth], cross_up[depth], bias_cross[depth]
        )
        stored.append(saved)
    first_saved, hidden = dense_forward(current, first_matrix, bias_one)
    second_saved, hidden = dense_forward(hidden, middle, bias_two)
    third_saved, hidden = dense_forward(hidden, third_matrix, bias_three)
    logits = (
        jnp.dot(hidden, head_weight, precision=highest, preferred_element_type=jnp.float32)
        + bias_last
    )
    labels = click_labels.astype(jnp.float32)
    loss_local = jnp.sum(jax.nn.softplus(logits) - labels * logits)
    grad_logits = (jax.nn.sigmoid(logits) - labels) / (samples * devices)
    grad_head_local = jnp.dot(
        grad_logits, hidden, precision=highest, preferred_element_type=jnp.float32
    )
    grad_hidden = grad_logits[:, None] * head_weight[None, :]
    grad_hidden, grad_third, grad_bias_three = dense_backward(
        third_saved, third_matrix, grad_hidden
    )
    grad_hidden, grad_middle, grad_bias_two = dense_backward(second_saved, middle, grad_hidden)
    grad_current, grad_first, grad_bias_one = dense_backward(first_saved, first_matrix, grad_hidden)
    grad_anchor = jnp.zeros_like(anchor)
    grads_down = [None] * LAYERS
    grads_up = [None] * LAYERS
    grads_cross = [None] * LAYERS
    for depth in reversed(range(LAYERS)):
        grad_current, grad_part, grads_down[depth], grads_up[depth], grads_cross[depth] = (
            cross_backward(anchor, stored[depth], cross_down[depth], cross_up[depth], grad_current)
        )
        grad_anchor = grad_anchor + grad_part
    grad_anchor = grad_anchor + grad_current
    grad_pooled = grad_anchor[:, EMB:].astype(jnp.bfloat16).reshape(samples * F, EMB)
    sent_back = jnp.take(grad_pooled, segment, axis=0).reshape(devices, capacity, EMB)
    arrived = lax.all_to_all(sent_back, "row", split_axis=0, concat_axis=0, tiled=True)
    grad_table = table_gradient(arrived.reshape(-1, EMB), received.reshape(-1), table_rows)
    grad_proj_local = jnp.einsum(
        "sa,sb->ab",
        dense_feats,
        grad_anchor[:, :EMB],
        precision=highest,
        preferred_element_type=jnp.float32,
    )
    stacked = jnp.concatenate(
        [
            jnp.stack(grads_down).reshape(-1, RANK),
            jnp.stack(grads_up).reshape(-1, RANK),
            grad_first.reshape(-1, RANK),
            grad_middle.reshape(-1, RANK),
            grad_third,
            jnp.zeros((BR, RANK), jnp.float32),
        ],
        axis=0,
    ).reshape(block_count + 1, BR, RANK)
    matches = block_owners[None, :] == jnp.arange(devices * slot_count, dtype=jnp.int32)[:, None]
    inverse = jnp.sum(
        jnp.where(matches, jnp.arange(block_count, dtype=jnp.int32)[None, :], 0), axis=1
    )
    inverse = inverse + jnp.where(jnp.any(matches, axis=1), 0, block_count)
    grad_slots = lax.psum_scatter(
        jnp.take(stacked, inverse, axis=0), "row", scatter_dimension=0, tiled=True
    )
    bias_local = jnp.concatenate(
        [
            jnp.sum(grad_anchor[:, :EMB], axis=0),
            jnp.stack(grads_cross).reshape(-1),
            grad_bias_one,
            grad_bias_two,
            grad_bias_three,
            jnp.sum(grad_logits)[None],
        ]
    )
    loss_total, grad_proj, grad_head, grad_bias = lax.psum(
        (loss_local, grad_proj_local, grad_head_local, bias_local), "row"
    )
    local_squares = jnp.sum(grad_table * grad_table) + jnp.sum(grad_slots * grad_slots)
    squares = lax.psum(local_squares, "row")
    squares = (
        squares
        + jnp.sum(grad_proj * grad_proj)
        + jnp.sum(grad_head * grad_head)
        + jnp.sum(grad_bias * grad_bias)
    )
    grad_norm = jnp.sqrt(squares)
    clip_scale = clip_norm / jnp.maximum(grad_norm, clip_norm)
    table_new = adamw(embed_table, table_moment, table_square, clip_scale * grad_table, rate_table)
    dense_new = adamw(dense_slots, dense_moment, dense_square, clip_scale * grad_slots, rate_dense)
    proj_new = adamw(dense_proj, proj_moment, proj_square, clip_scale * grad_proj, rate_small)
    head_new = adamw(head_weight, head_moment, head_square, clip_scale * grad_head, rate_small)
    bias_new = adamw(biases, bias_moment, bias_square, clip_scale * grad_bias, rate_small)
    return (
        loss_total,
        grad_norm,
        table_new[0],
        table_new[1],
        table_new[2],
        dense_new[0],
        dense_new[1],
        dense_new[2],
        proj_new[0],
        proj_new[1],
        proj_new[2],
        head_new[0],
        head_new[1],
        head_new[2],
        bias_new[0],
        bias_new[1],
        bias_new[2],
    )


def body_counted(
    row_ids,
    hot_counts,
    dense_feats,
    click_labels,
    block_owners,
    embed_table,
    table_moment,
    table_square,
    dense_slots,
    dense_moment,
    dense_square,
    dense_proj,
    proj_moment,
    proj_square,
    head_weight,
    head_moment,
    head_square,
    biases,
    bias_moment,
    bias_square,
):
    devices = lax.axis_size("row")
    samples = row_ids.shape[0]
    slot_count = dense_slots.shape[0]
    table_rows = embed_table.shape[1]
    block_count = block_owners.shape[0]
    capacity = samples * TOTAL // devices
    live_total = samples * TOTAL
    bf16 = jnp.bfloat16
    slot_tiles = (
        dense_slots.astype(bf16)
        .reshape(slot_count, 8, 16, 4, 128)
        .transpose(1, 3, 0, 2, 4)
        .reshape(devices, slot_count * 16, 128)
    )
    slot_tiles = lax.all_to_all(slot_tiles, "row", split_axis=0, concat_axis=0, tiled=True)
    lanes = lax.broadcasted_iota(jnp.int32, row_ids.shape, 2)
    features = lax.broadcasted_iota(jnp.int32, row_ids.shape, 1)
    sample_of = lax.broadcasted_iota(jnp.int32, row_ids.shape, 0)
    key = (
        ((row_ids // table_rows) << 21)
        | (features << 16)
        | ((row_ids % table_rows) << 7)
        | sample_of
    )
    key = jnp.where(lanes < hot_counts[:, :, None], key, devices << 21)
    ordered = lax.sort(key.reshape(-1), is_stable=False)[:live_total]
    block_tiles = jnp.take(
        slot_tiles.reshape(devices * slot_count, 16, 128),
        block_owners + jnp.minimum(ordered[0], 0),
        axis=0,
        mode="clip",
    )
    tiles = lax.all_gather(block_tiles.reshape(block_count * 16, 128), "row", axis=0, tiled=True)
    tiles = tiles.reshape(devices, block_count, 16, 128)
    bias_dense, bias_cross, bias_one, bias_two, bias_three, bias_last = split_bias(biases)
    requests = (ordered & ((1 << 21) - 1)).reshape(devices, capacity)
    received = lax.all_to_all(requests, "row", split_axis=0, concat_axis=0, tiled=True)
    edges = jnp.arange(F + 1, dtype=jnp.int32) << 16
    offsets = jnp.sum((received[:, None, :] < edges[None, :, None]).astype(jnp.int32), axis=2)
    room = (capacity + samples - 1) // samples * samples + samples
    keys = jnp.pad(received, ((0, 0), (0, room - capacity)), constant_values=-1)
    counts, partial = count_tables(offsets, keys, embed_table, devices, samples)
    pooled = scatter_sum(partial, 0, F * EMB, bf16, (0, 1) * 8, (2, 4, 6, 7, 8), 0, "scatter_pooled")
    dense_part = (
        jnp.dot(dense_feats, dense_proj, precision=highest, preferred_element_type=jnp.float32)
        + bias_dense
    )
    grad_tiles, grad_pooled, grad_small = dense_step(
        tiles,
        pooled,
        jnp.pad(dense_feats, ((0, 0), (0, 3))),
        dense_part,
        click_labels.astype(jnp.float32)[:, None],
        head_weight[None, :],
        jnp.broadcast_to(bias_last, (samples, 1)),
        bias_cross.reshape(LAYERS * CHUNKS, CW),
        bias_one.reshape(2, RANK),
        bias_two.reshape(2, RANK),
        bias_three[None, :],
        samples * devices,
    )
    grad_mine, grad_table, small_total, grad_norm, clip_scale = back_exchange(
        grad_tiles.reshape(devices, block_count * 16, 128),
        grad_pooled,
        counts,
        grad_small,
        (0, 1, 0, 1, 2, 3, 0, 1) * 2,
        (3, 6, 8, 9, 10),
        13,
        (1, 2, 3, 4, 5),
        6,
        (0, 1, 2),
        1,
    )
    matches = block_owners[None, :] == jnp.arange(devices * slot_count, dtype=jnp.int32)[:, None]
    inverse = jnp.sum(
        jnp.where(matches, jnp.arange(block_count, dtype=jnp.int32)[None, :], 0), axis=1
    )
    named = jnp.any(matches, axis=1)
    returned = jnp.take(
        grad_mine.reshape(block_count, 16, 128), inverse, axis=0, mode="clip"
    )
    returned = jnp.where(named[:, None, None], returned, 0)
    returned = lax.all_to_all(
        returned.reshape(devices, slot_count * 16, 128), "row", split_axis=0, concat_axis=0, tiled=True
    )
    loss_total = small_total[0, 0]
    grad_proj = small_total[PROJ_ROW : PROJ_ROW + NDENSE]
    grad_head = small_total[HEAD_ROW : HEAD_ROW + 4].reshape(-1)
    grad_bias = small_total[DENSE_ROW : LAST_ROW + 1].reshape(-1)[:NBIAS]
    table_new = adamw(embed_table, table_moment, table_square, clip_scale * grad_table, rate_table)
    dense_new = slot_update(
        clip_scale,
        returned.reshape(devices, slot_count, 16, 128),
        dense_slots,
        dense_moment,
        dense_square,
    )
    proj_new = adamw(dense_proj, proj_moment, proj_square, clip_scale * grad_proj, rate_small)
    head_new = adamw(head_weight, head_moment, head_square, clip_scale * grad_head, rate_small)
    bias_new = adamw(biases, bias_moment, bias_square, clip_scale * grad_bias, rate_small)
    return (
        (loss_total, grad_norm) + table_new + dense_new + proj_new + head_new + bias_new
    )


def solution(mesh):
    in_specs = (
        P("row", None, None),
        P("row", None),
        P("row", None),
        P("row"),
        P(),
        P(None, "row", None),
        P(None, "row", None),
        P(None, "row", None),
        P("row", None, None),
        P("row", None, None),
        P("row", None, None),
        P(),
        P(),
        P(),
        P(),
        P(),
        P(),
        P(),
        P(),
        P(),
    )
    out_specs = (
        P(),
        P(),
        P(None, "row", None),
        P(None, "row", None),
        P(None, "row", None),
        P("row", None, None),
        P("row", None, None),
        P("row", None, None),
        P(),
        P(),
        P(),
        P(),
        P(),
        P(),
        P(),
        P(),
        P(),
    )
    fits = mesh.shape["row"] == 32
    chosen = body_counted if fits else body
    return jax.shard_map(chosen, mesh=mesh, in_specs=in_specs, out_specs=out_specs, check_vma=False)
```

```python
import functools

import jax
import jax.numpy as jnp
from jax import lax
from jax.experimental import pallas as pl
from jax.experimental.pallas import tpu as pltpu
from jax.sharding import PartitionSpec as P

F = 26
HOT = 30
EMB = 128
RANK = 512
LAYERS = 3
H1 = 1024
H2 = 1024
H3 = 512
BR = 128
STEP = 10
WIDTH = 3456
TOTAL = 403
NBIAS = 13057


beta_one = 0.9
beta_two = 0.999
adam_eps = 1e-12
decay_rate = 0.01
clip_norm = 0.001
rate_table = 0.3
rate_dense = 0.03
rate_small = 0.1
highest = lax.Precision.HIGHEST


def split_dense(flat):
    cross_rows = LAYERS * WIDTH
    first = 2 * cross_rows + WIDTH * H1 // RANK
    second = first + H1 * H2 // RANK
    return (
        flat[:cross_rows].reshape(LAYERS, WIDTH, RANK),
        flat[cross_rows : 2 * cross_rows].reshape(LAYERS, WIDTH, RANK),
        flat[2 * cross_rows : first].reshape(WIDTH, H1),
        flat[first:second].reshape(H1, H2),
        flat[second : second + H2 * H3 // RANK],
    )


def split_bias(biases):
    start = EMB + LAYERS * WIDTH
    return (
        biases[:EMB],
        biases[EMB:start].reshape(LAYERS, WIDTH),
        biases[start : start + H1],
        biases[start + H1 : start + H1 + H2],
        biases[start + H1 + H2 : start + H1 + H2 + H3],
        biases[NBIAS - 1],
    )


def cross_forward(anchor, current, weight_down, weight_up, bias_term):
    current_low = current.astype(jnp.bfloat16)
    reduced = jnp.dot(current_low, weight_down, preferred_element_type=jnp.float32).astype(
        jnp.bfloat16
    )
    mixing = (
        jnp.einsum("sr,wr->sw", reduced, weight_up, preferred_element_type=jnp.float32) + bias_term
    )
    return ((current_low, reduced, mixing), anchor * mixing + current)


def cross_backward(anchor, stored, weight_down, weight_up, grad_current):
    current_low, reduced, mixing = stored
    grad_mixing = anchor * grad_current
    grad_mixing_low = grad_mixing.astype(jnp.bfloat16)
    grad_up = jnp.einsum("sw,sr->wr", grad_mixing_low, reduced, preferred_element_type=jnp.float32)
    grad_reduced = jnp.dot(grad_mixing_low, weight_up, preferred_element_type=jnp.float32).astype(
        jnp.bfloat16
    )
    grad_down = jnp.einsum(
        "sw,sr->wr", current_low, grad_reduced, preferred_element_type=jnp.float32
    )
    grad_prev = grad_current + jnp.einsum(
        "sr,wr->sw", grad_reduced, weight_down, preferred_element_type=jnp.float32
    )
    return (grad_prev, grad_current * mixing, grad_down, grad_up, jnp.sum(grad_mixing, axis=0))


def dense_forward(inputs, weight, bias_term):
    inputs_low = inputs.astype(jnp.bfloat16)
    before = jnp.dot(inputs_low, weight, preferred_element_type=jnp.float32) + bias_term
    return ((inputs_low, before), jax.nn.gelu(before))


def dense_backward(stored, weight, grad_out):
    inputs_low, before = stored
    unused, gelu_back = jax.vjp(jax.nn.gelu, before)
    grad_before = gelu_back(grad_out)[0]
    grad_low = grad_before.astype(jnp.bfloat16)
    grad_weight = jnp.einsum("sa,sb->ab", inputs_low, grad_low, preferred_element_type=jnp.float32)
    grad_inputs = jnp.einsum("sb,ab->sa", grad_low, weight, preferred_element_type=jnp.float32)
    return (grad_inputs, grad_weight, jnp.sum(grad_before, axis=0))


def table_gradient(arrived, served, table_rows):
    received = served.shape[0]
    window = min(512, received)
    order_back = jnp.argsort(served, stable=True)
    sorted_ids = jnp.take(served, order_back)
    edges = jnp.arange(F + 1, dtype=jnp.int32) * table_rows
    bounds = jnp.sum((sorted_ids[None, :] < edges[:, None]).astype(jnp.int32), axis=1)
    starts = bounds[:-1]
    finish = bounds[1:]
    windows = (finish - starts + window - 1) // window
    ends_cum = jnp.cumsum(windows)
    begins_cum = ends_cum - windows
    step_count = F + received // window + 1
    turns = jnp.arange(step_count, dtype=jnp.int32)
    feature_of = jnp.sum((ends_cum[None, :] <= turns[:, None]).astype(jnp.int32), axis=1)
    feature_safe = jnp.minimum(feature_of, F - 1)
    first_row = (
        jnp.take(starts, feature_safe) + (turns - jnp.take(begins_cum, feature_safe)) * window
    )
    row_index = first_row[:, None] + jnp.arange(window, dtype=jnp.int32)[None, :]
    row_valid = (feature_of < F)[:, None] & (row_index < jnp.take(finish, feature_safe)[:, None])
    row_safe = jnp.minimum(row_index, received - 1)
    window_grads = jnp.take(arrived, jnp.take(order_back, row_safe), axis=0)
    local_row = jnp.take(sorted_ids, row_safe) - feature_safe[:, None] * table_rows
    local_row = jnp.where(row_valid, local_row, -1)
    selector = (
        local_row[:, :, None] == jnp.arange(table_rows, dtype=jnp.int32)[None, None, :]
    ).astype(jnp.bfloat16)
    partial_sums = jnp.einsum(
        "swr,swe->sre", selector, window_grads, preferred_element_type=jnp.float32
    )
    feature_pick = (feature_of[:, None] == jnp.arange(F, dtype=jnp.int32)[None, :]).astype(
        jnp.float32
    )
    return jnp.einsum(
        "sf,sre->fre",
        feature_pick,
        partial_sums,
        precision=highest,
        preferred_element_type=jnp.float32,
    )


def adamw(weight, moment, square, gradient, step_rate):
    moment = beta_one * moment + (1 - beta_one) * gradient
    square = beta_two * square + (1 - beta_two) * gradient * gradient
    corrected = moment / (1 - beta_one**STEP)
    scaled = square / (1 - beta_two**STEP)
    weight = weight - step_rate * (corrected / (jnp.sqrt(scaled) + adam_eps) + decay_rate * weight)
    return (weight, moment, square)


def count_kernel(devices, samples, table_rows, off_ref, most_ref, keys_ref, table_ref, counts_ref, partial_ref, low_ref, rows_ref, samples_ref):
    feature = pl.program_id(0)
    low_ref[...] = table_ref[0].T.astype(jnp.bfloat16)
    lane = lax.broadcasted_iota(jnp.int32, (1, samples), 1)
    row_iota = lax.broadcasted_iota(jnp.int32, (table_rows, 2 * samples), 0)
    sample_iota = lax.broadcasted_iota(jnp.int32, (2 * samples, 2 * samples), 0)

    def window(source, turn):
        start = off_ref[source * (F + 1) + feature] + turn * samples
        stop = off_ref[source * (F + 1) + feature + 1]
        tile = start // samples
        base = pl.multiple_of(tile * samples, samples)
        piece = keys_ref[pl.ds(source, 1), pl.ds(base, 2 * samples)]
        turned = pltpu.roll(piece, 2 * samples - (start - base), 1)[:, :samples]
        valid = lane < stop - start
        row = jnp.where(valid, (turned >> 7) & (table_rows - 1), -1)
        return row, turned & (samples - 1)

    def product(row, sample):
        row_hot = jnp.where(row_iota == row, 1.0, 0.0).astype(jnp.bfloat16)
        sample_hot = jnp.where(sample_iota == sample, 1.0, 0.0).astype(jnp.bfloat16)
        return lax.dot_general(
            row_hot, sample_hot, (((1,), (1,)), ((), ())), preferred_element_type=jnp.float32
        )

    def counted(first, turn):
        row_a, sample_a = window(first, turn)
        row_b, sample_b = window(first + 1, turn)
        return product(
            jnp.concatenate([row_a, row_b], axis=1),
            jnp.concatenate([sample_a, sample_b + samples], axis=1),
        )

    def span(first):
        return pl.ds(pl.multiple_of(first * samples, 2 * samples), 2 * samples)

    for source in range(devices):
        row, sample = window(source, 0)
        half = pl.ds((source % 2) * samples, samples)
        rows_ref[pl.ds(source // 2, 1), half] = row
        samples_ref[pl.ds(source // 2, 1), half] = sample + (source % 2) * samples

    def pair(step, carry):
        total = product(rows_ref[pl.ds(step, 1), :], samples_ref[pl.ds(step, 1), :])
        counts_ref[0, :, span(step * 2)] = total.astype(jnp.bfloat16)
        return carry

    lax.fori_loop(0, devices // 2, pair, 0, unroll=devices // 2)

    def late(step, carry):
        first = step * 2
        spans = [
            off_ref[(first + i) * (F + 1) + feature + 1] - off_ref[(first + i) * (F + 1) + feature]
            for i in (0, 1)
        ]
        turns = (jnp.maximum(spans[0], spans[1]) + samples - 1) // samples

        @pl.when(turns > 1)
        def again():
            total = lax.fori_loop(1, turns, lambda turn, acc: acc + counted(first, turn), counted(first, 0))
            counts_ref[0, :, span(first)] = total.astype(jnp.bfloat16)

        return carry

    @pl.when(most_ref[feature] > samples)
    def crowded():
        lax.fori_loop(0, devices // 2, late, 0)

    group = devices

    def pool(step, carry):
        part = jnp.dot(
            low_ref[...],
            counts_ref[0, :, pl.ds(pl.multiple_of(step * group * samples, group * samples), group * samples)],
            preferred_element_type=jnp.float32,
        ).astype(jnp.bfloat16)
        for i in range(group):
            partial_ref[step * group + i, 0] = part[:, i * samples : (i + 1) * samples]
        return carry

    lax.fori_loop(0, devices // group, pool, 0)


def count_tables(offsets, keys, embed_table, devices, samples):
    table_rows = embed_table.shape[1]
    return pl.pallas_call(
        functools.partial(count_kernel, devices, samples, table_rows),
        grid_spec=pltpu.PrefetchScalarGridSpec(
            num_scalar_prefetch=2,
            grid=(F,),
            in_specs=[
                pl.BlockSpec(keys.shape, lambda f, off, most: (0, 0)),
                pl.BlockSpec((1, table_rows, EMB), lambda f, off, most: (f, 0, 0)),
            ],
            out_specs=[
                pl.BlockSpec((1, table_rows, devices * samples), lambda f, off, most: (f, 0, 0)),
                pl.BlockSpec((devices, 1, EMB, samples), lambda f, off, most: (0, f, 0, 0)),
            ],
            scratch_shapes=[
                pltpu.VMEM((EMB, table_rows), jnp.bfloat16),
                pltpu.VMEM((devices // 2, 2 * samples), jnp.int32),
                pltpu.VMEM((devices // 2, 2 * samples), jnp.int32),
            ],
        ),
        out_shape=[
            jax.ShapeDtypeStruct((F, table_rows, devices * samples), jnp.bfloat16),
            jax.ShapeDtypeStruct((devices, F, EMB, samples), jnp.bfloat16),
        ],
        compiler_params=pltpu.CompilerParams(vmem_limit_bytes=48 << 20),
        name="count_tables",
    )(offsets.reshape(-1), jnp.max(offsets[:, 1:] - offsets[:, :-1], axis=0), keys, embed_table)


MESH = pl.DeviceIdType.MESH


def place():
    me = lax.axis_index("row")
    return me // 8, (me // 4) % 2, (me // 2) % 2, me % 2


def device_at(z, y, x, core):
    return (((z * 2 + y) * 2 + x) * 2 + core,)


def greet(z, y, x, core, far=0):
    barrier = pltpu.get_barrier_semaphore()

    def hail(*where):
        pl.semaphore_signal(barrier, inc=1, device_id=device_at(*where), device_id_type=MESH)

    hail(z, y, x, 1 - core)
    hail(z, y, 1 - x, core)
    hail(z, 1 - y, x, core)
    if far:
        hail((z + 2) % 4, y, x, core)

    @pl.when(z > 0)
    def below():
        hail(z - 1, y, x, core)

    @pl.when(z < 3)
    def above():
        hail(z + 1, y, x, core)

    @pl.when(jnp.logical_and(z > 0, z < 3))
    def inside():
        pl.semaphore_wait(barrier, 5 + far)

    @pl.when(jnp.logical_or(z == 0, z == 3))
    def edge():
        pl.semaphore_wait(barrier, 4 + far)


def remote(source, target, send_sem, recv_sem, where):
    return pltpu.make_async_remote_copy(
        src_ref=source,
        dst_ref=target,
        send_sem=send_sem,
        recv_sem=recv_sem,
        device_id=device_at(*where),
        device_id_type=MESH,
    )


def scatter_parts(
    base, kinds, x_ref, out_ref, own, got_core, got_one, tail, local_sem, send_core, recv_core,
    send_one, recv_one, send_two, recv_two, send_up, recv_up, send_down, recv_down, squares=None,
):
    z, y, x, core = place()
    slices = len(kinds)
    rows = own.shape[4]

    def span(q):
        return pl.ds(base + q * rows, rows)

    def kept(q):
        return pl.ds(q * rows, rows)

    def along_x(q):
        return kinds[q] % 2 == 0

    def chain_last(q):
        return kinds[q] < 2

    def got_two(q):
        return tail.at[q, 0:4] if chain_last(q) else tail.at[q, 12]

    def rising(q, first, count):
        if chain_last(q):
            return tail.at[q, 4 + first : 4 + first + count]
        return tail.at[q, 2 * first : 2 * first + 2 * count]

    def falling(q, count):
        if chain_last(q):
            return tail.at[q, 7 : 7 + count]
        return tail.at[q, 6 : 6 + 2 * count]

    def close(q, total):
        out_ref[kept(q)] = total.astype(out_ref.dtype)
        if squares is not None:
            squares[...] += jnp.sum((total * total).reshape(-1, 8, total.shape[1]), axis=0)

    def to_core(q):
        return remote(x_ref.at[:, :, :, 1 - core, span(q)], got_core.at[q], send_core.at[q], recv_core.at[q], (z, y, x, 1 - core))

    def to_one(q):
        if along_x(q):
            source, where = own.at[q, :, :, 1 - x], (z, y, 1 - x, core)
        else:
            source, where = own.at[q, :, 1 - y], (z, 1 - y, x, core)
        return remote(source, got_one.at[q], send_one.at[q], recv_one.at[q], where)

    def to_two(q):
        there = (z, 1 - y, x, core) if along_x(q) else (z, y, 1 - x, core)
        if chain_last(q):
            source = own.at[q, :, 1 - y, x] if along_x(q) else own.at[q, :, y, 1 - x]
        else:
            source = own.at[q, z, 1 - y, x] if along_x(q) else own.at[q, z, y, 1 - x]
        return remote(source, got_two(q), send_two.at[q], recv_two.at[q], there)

    def chained(q, first, count):
        part = pl.ds(first, count)
        if chain_last(q):
            return own.at[q, part, y, x]
        return own.at[q, part, :, x] if along_x(q) else own.at[q, part, y]

    def to_up(q, level):
        count = 3 - level
        target = rising(q, 0, count)
        if level == 0:
            source = chained(q, 1, 3)
            target = target if chain_last(q) else tail.at[q, 0:6].reshape(3, 2, rows, own.shape[5])
        else:
            source = rising(q, 1, count)
        return remote(source, target, send_up.at[q], recv_up.at[q], (z + 1, y, x, core))

    def to_down(q, level):
        count = level
        target = falling(q, count)
        if level == 3:
            source = chained(q, 0, 3)
            target = target if chain_last(q) else tail.at[q, 6:12].reshape(3, 2, rows, own.shape[5])
        else:
            source = target
        return remote(source, target, send_down.at[q], recv_down.at[q], (z - 1, y, x, core))

    def local(q):
        return pltpu.make_async_copy(x_ref.at[:, :, :, core, span(q)], own.at[q], local_sem.at[q])

    def width(q):
        return 1 if chain_last(q) else 2

    def own_at(q, t, b):
        if chain_last(q):
            return (q, t, y, x)
        return (q, t, b, x) if along_x(q) else (q, t, y, b)

    def rise_at(q, place_of, b):
        return (q, 4 + place_of) if chain_last(q) else (q, 2 * place_of + b)

    def fall_at(q, place_of, b):
        return (q, 7 + place_of) if chain_last(q) else (q, 6 + 2 * place_of + b)

    def start_chain(q):
        @pl.when(z == 0)
        def rise():
            to_up(q, 0).start()

        @pl.when(z == 3)
        def fall():
            to_down(q, 3).start()

    def stage_zero(q):
        local(q).wait()
        to_core(q).wait_recv()

        @pl.loop(0, 16)
        def step(i):
            a, b, c = i // 4, (i // 2) % 2, i % 2
            own[q, a, b, c] = own[q, a, b, c] + got_core[q, a, b, c]

        to_one(q).start()

    def stage_one(q):
        to_one(q).wait_recv()

        @pl.loop(0, 8)
        def step(i):
            a, b = i // 2, i % 2
            if along_x(q):
                own[q, a, b, x] = own[q, a, b, x] + got_one[q, a, b]
            else:
                own[q, a, y, b] = own[q, a, y, b] + got_one[q, a, b]

        if chain_last(q):
            to_two(q).start()
        else:
            start_chain(q)

    def stage_two(q):
        to_two(q).wait_recv()

        @pl.loop(0, 4)
        def step(a):
            own[q, a, y, x] = own[q, a, y, x] + tail[q, a]

        start_chain(q)

    def stage_chain(q, hop):
        @pl.when(z == hop)
        def rise():
            to_up(q, hop - 1).wait_recv()
            for t in range(hop + 1, 4):
                for b in range(width(q)):
                    at = rise_at(q, t - hop, b)
                    tail[at] = tail[at] + own[own_at(q, t, b)]
            if hop < 3:
                to_up(q, hop).start()

        @pl.when(z == 3 - hop)
        def fall():
            to_down(q, 4 - hop).wait_recv()
            for t in range(0, 3 - hop):
                for b in range(width(q)):
                    at = fall_at(q, t, b)
                    tail[at] = tail[at] + own[own_at(q, t, b)]
            if hop < 3:
                to_down(q, 3 - hop).start()

        if hop == 3:
            for level in range(4):

                @pl.when(z == level)
                def finish_chain():
                    for b in range(width(q)):
                        total = own[own_at(q, level, b)].astype(jnp.float32)
                        if level > 0:
                            total = total + tail[rise_at(q, 0, b)].astype(jnp.float32)
                        if level < 3:
                            total = total + tail[fall_at(q, level, b)].astype(jnp.float32)
                        if chain_last(q):
                            close(q, total)
                        else:
                            own[own_at(q, level, b)] = total.astype(own.dtype)

            if not chain_last(q):
                to_two(q).start()

    def stage_end(q):
        to_two(q).wait_recv()
        total = own[q, z, y, x].astype(jnp.float32) + tail[q, 12].astype(jnp.float32)
        close(q, total)

    def prepare():
        for q in range(slices):
            local(q).start()

    def begin():
        for q in range(slices):
            to_core(q).start()

    def step_of(number):
        def run(q):
            if number == 0:
                stage_zero(q)
            elif number == 1:
                stage_one(q)
            elif chain_last(q):
                stage_two(q) if number == 2 else stage_chain(q, number - 2)
            else:
                stage_end(q) if number == 5 else stage_chain(q, number - 1)

        return run

    stages = tuple(step_of(number) for number in range(6))

    def finish():
        for q in range(slices):
            to_core(q).wait_send()
            to_one(q).wait_send()
            to_two(q).wait_send()
            for level in range(4):

                @pl.when(z == level)
                def sent():
                    if level < 3:
                        to_up(q, level).wait_send()
                    if level > 0:
                        to_down(q, level).wait_send()

    return prepare, begin, stages, finish


def run_tick(tick, slices, lags, stages):
    for lag, stage in zip((0,) + lags, stages):
        if 0 <= tick - lag < slices:
            stage(tick - lag)


def scatter_room(slices, rows, lanes, low):
    return [
        pltpu.VMEM((slices, 4, 2, 2, rows, lanes), low),
        pltpu.VMEM((slices, 4, 2, 2, rows, lanes), low),
        pltpu.VMEM((slices, 4, 2, rows, lanes), low),
        pltpu.VMEM((slices, 13, rows, lanes), low),
    ] + [pltpu.SemaphoreType.DMA((slices,))] * 11


def spread_parts(
    slices, width, x_ref, out_ref, local_sem, send_one, recv_one, send_up, recv_up, send_down, recv_down,
    send_two, recv_two, send_core, recv_core,
):
    z, y, x, core = place()

    def span(q):
        return pl.ds(q * width, width)

    def local(q):
        return pltpu.make_async_copy(x_ref.at[span(q)], out_ref.at[z, y, x, core, span(q)], local_sem.at[q])

    def to_one(q):
        where = (z, y, 1 - x, core) if q % 2 == 0 else (z, 1 - y, x, core)
        target = out_ref.at[z, y, x, core, span(q)]
        return remote(x_ref.at[span(q)], target, send_one.at[q], recv_one.at[q], where)

    def level(block, q):
        if q % 2 == 0:
            return out_ref.at[block, y, :, core, span(q)]
        return out_ref.at[block, :, x, core, span(q)]

    def to_up(q, k):
        block = level(z - k, q)
        return remote(block, block, send_up.at[q, k], recv_up.at[q, k], (z + 1, y, x, core))

    def to_down(q, k):
        block = level(z + k, q)
        return remote(block, block, send_down.at[q, k], recv_down.at[q, k], (z - 1, y, x, core))

    def to_two(q):
        if q % 2 == 0:
            block, where = out_ref.at[:, y, :, core, span(q)], (z, 1 - y, x, core)
        else:
            block, where = out_ref.at[:, :, x, core, span(q)], (z, y, 1 - x, core)
        return remote(block, block, send_two.at[q], recv_two.at[q], where)

    def to_core(q):
        block = out_ref.at[:, :, :, core, span(q)]
        return remote(block, block, send_core.at[q], recv_core.at[q], (z, y, x, 1 - core))

    def send_on(q, k):
        @pl.when(jnp.logical_and(z < 3, z >= k))
        def rise():
            to_up(q, k).start()

        @pl.when(jnp.logical_and(z > 0, z + k <= 3))
        def fall():
            to_down(q, k).start()

    def stage_one(q):
        local(q).wait()
        to_one(q).wait_recv()
        send_on(q, 0)

    def stage_chain(q, hop):
        @pl.when(z >= hop)
        def rise():
            to_up(q, hop - 1).wait_recv()

        @pl.when(z + hop <= 3)
        def fall():
            to_down(q, hop - 1).wait_recv()

        if hop < 3:
            send_on(q, hop)
        else:
            to_two(q).start()

    def stage_two(q):
        to_two(q).wait_recv()
        to_core(q).start()

    def stage_core(q):
        to_core(q).wait_recv()

    def prepare():
        for q in range(slices):
            local(q).start()

    def begin():
        for q in range(slices):
            to_one(q).start()

    stages = (
        stage_one,
        lambda q: stage_chain(q, 1),
        lambda q: stage_chain(q, 2),
        lambda q: stage_chain(q, 3),
        stage_two,
        stage_core,
    )

    def finish():
        for q in range(slices):
            to_one(q).wait_send()
            for k in range(3):

                @pl.when(jnp.logical_and(z < 3, z >= k))
                def rise():
                    to_up(q, k).wait_send()

                @pl.when(jnp.logical_and(z > 0, z + k <= 3))
                def fall():
                    to_down(q, k).wait_send()

            to_two(q).wait_send()
            to_core(q).wait_send()

    return prepare, begin, stages, finish


def spread_room(slices):
    dma = pltpu.SemaphoreType.DMA
    return [dma((slices,))] * 3 + [dma((slices, 3))] * 4 + [dma((slices,))] * 4


def front_kernel(kinds, lags, spread_slices, spread_lags, delay, x_ref, tiles_ref, out_ref, gathered_ref, *rest):
    slices = len(kinds)
    prepare, begin, stages, finish = scatter_parts(0, kinds, x_ref, out_ref, *rest[:15])
    also_prepare, also_begin, also_stages, also_finish = spread_parts(
        spread_slices, tiles_ref.shape[0] // spread_slices, tiles_ref, gathered_ref, *rest[15:]
    )
    also_prepare()
    prepare()
    greet(*place())
    also_begin()
    begin()
    for tick in range(max(slices + lags[-1], spread_slices + spread_lags[-1] + delay)):
        run_tick(tick - delay, spread_slices, spread_lags, also_stages)
        run_tick(tick, slices, lags, stages)
    also_finish()
    finish()


def front_exchange(array, tiles, chunk, kinds, lags, spread_slices, spread_lags, delay, collective_id):
    lanes = array.shape[-1]
    slices = len(kinds)
    away = pl.BlockSpec(memory_space=pl.ANY)
    summed, gathered = pl.pallas_call(
        functools.partial(front_kernel, kinds, lags, spread_slices, spread_lags, delay),
        out_shape=[
            jax.ShapeDtypeStruct((chunk, lanes), array.dtype),
            jax.ShapeDtypeStruct((4, 2, 2, 2) + tiles.shape, tiles.dtype),
        ],
        in_specs=[away] * 2,
        out_specs=[pl.BlockSpec(memory_space=pltpu.VMEM), away],
        scratch_shapes=scatter_room(slices, chunk // slices, lanes, array.dtype) + spread_room(spread_slices),
        compiler_params=pltpu.CompilerParams(
            collective_id=collective_id, has_side_effects=True, vmem_limit_bytes=60 << 20
        ),
        name="front_exchange",
    )(array.reshape(4, 2, 2, 2, -1, lanes), tiles)
    return summed, gathered.reshape((32,) + tiles.shape)


def back_kernel(
    kinds, lags, spread_slices, spread_lags, compute_lag, delay,
    x_ref, grads_ref, counts_ref, small_ref, out_ref, gathered_ref, table_ref, small_out, norm_ref, scale_ref,
    square_ref, held, got_small, send_small, recv_small, counts_buf, grads_buf, partial, ready, counts_sem, grads_sem, table_sem, *rest,
):
    slices = len(kinds)
    per_slice = F // spread_slices
    steps = 2 * per_slice
    last = 2 * F
    half = counts_buf.shape[2]
    prepare, begin, stages, finish = scatter_parts(0, kinds, x_ref, out_ref, *rest[:15], squares=square_ref)
    also_prepare, also_begin, also_stages, also_finish = spread_parts(
        spread_slices, per_slice, grads_ref, gathered_ref, *rest[15:]
    )

    def counts_load(n):
        at = pl.ds(pl.multiple_of((n % 2) * half, half), half)
        return pltpu.make_async_copy(counts_ref.at[n // 2, :, at], counts_buf.at[n % 2], counts_sem.at[n % 2])

    def grads_load(n):
        source = gathered_ref.at[pl.ds((n % 2) * 2, 2), :, :, :, n // 2]
        return pltpu.make_async_copy(source, grads_buf.at[n % 2], grads_sem.at[n % 2])

    def table_store(f):
        return pltpu.make_async_copy(ready.at[f % 2], table_ref.at[f], table_sem.at[f % 2])

    def compute(q):
        first = q * steps
        grads_load(first).start()
        grads_load(first + 1).start()

        @pl.loop(0, steps)
        def step(i):
            n = first + i
            f = n // 2
            slot = n % 2
            counts_load(n).wait()
            grads_load(n).wait()
            part = jnp.dot(
                counts_buf[slot], grads_buf[slot].reshape(half, EMB), preferred_element_type=jnp.float32
            )

            @pl.when(n + 2 < last)
            def more():
                counts_load(n + 2).start()

            @pl.when(i + 2 < steps)
            def also():
                grads_load(n + 2).start()

            @pl.when(slot == 0)
            def keep():
                partial[...] = part

            @pl.when(slot == 1)
            def close():
                @pl.when(f >= 2)
                def free():
                    table_store(f).wait()

                total = partial[...] + part
                ready[f % 2] = total
                table_store(f).start()
                square_ref[...] += jnp.sum((total * total).reshape(-1, 8, EMB), axis=0)

    also_prepare()
    prepare()
    counts_load(0).start()
    counts_load(1).start()
    square_ref[...] = jnp.zeros_like(square_ref)
    greet(*place(), far=1)
    also_begin()
    begin()
    for tick in range(max(slices + lags[-1], spread_slices + compute_lag + delay)):
        run_tick(tick - delay, spread_slices, spread_lags, also_stages)
        run_tick(tick, slices, lags, stages)
        if 0 <= tick - delay - compute_lag < spread_slices:
            compute(tick - delay - compute_lag)
    z, y, x, core = place()
    row = lax.broadcasted_iota(jnp.int32, small_ref.shape, 0)
    lane = lax.broadcasted_iota(jnp.int32, small_ref.shape, 1)
    own_square = jnp.sum(jnp.sum(square_ref[...], axis=1, keepdims=True), axis=0, keepdims=True)
    held[0] = small_ref[...] + jnp.where(jnp.logical_and(row == 0, lane == 1), own_square, 0.0)
    partners = (
        (z, y, x, 1 - core),
        (z, y, 1 - x, core),
        (z, 1 - y, x, core),
        (z + 1 - 2 * (z % 2), y, x, core),
        ((z + 2) % 4, y, x, core),
    )
    sends = []
    for step, where in enumerate(partners):
        copy = remote(held.at[step], got_small.at[step], send_small.at[step], recv_small.at[step], where)
        copy.start()
        copy.wait_recv()
        sends.append(copy)
        total = held[step] + got_small[step]
        if step < len(partners) - 1:
            held[step + 1] = total
    small_out[...] = total
    squares = jnp.where(row > 0, total * total, jnp.where(lane == 1, total, 0.0))
    norm = jnp.sqrt(jnp.sum(jnp.sum(squares, axis=1, keepdims=True), axis=0, keepdims=True))
    norm_ref[...] = norm
    scale_ref[...] = clip_norm / jnp.maximum(norm, clip_norm)
    for copy in sends:
        copy.wait_send()
    for f in (F - 2, F - 1):
        table_store(f).wait()
    also_finish()
    finish()


def back_exchange(tiles, grads, counts, small, kinds, lags, spread_slices, spread_lags, compute_lag, delay, collective_id):
    chunk, lanes = tiles.shape[-2:]
    slices = len(kinds)
    table_rows, batch = counts.shape[1:]
    samples = grads.shape[1]
    f32, bf16 = jnp.float32, jnp.bfloat16
    away = pl.BlockSpec(memory_space=pl.ANY)
    near = pl.BlockSpec(memory_space=pltpu.VMEM)
    dma = pltpu.SemaphoreType.DMA
    mine, _, table, total, norm, scale = pl.pallas_call(
        functools.partial(back_kernel, kinds, lags, spread_slices, spread_lags, compute_lag, delay),
        out_shape=[
            jax.ShapeDtypeStruct((chunk, lanes), bf16),
            jax.ShapeDtypeStruct((4, 2, 2, 2) + grads.shape, bf16),
            jax.ShapeDtypeStruct((F, table_rows, EMB), f32),
            jax.ShapeDtypeStruct(small.shape, f32),
            jax.ShapeDtypeStruct((1, 1), f32),
            jax.ShapeDtypeStruct((1, 1), f32),
        ],
        in_specs=[away] * 3 + [near],
        out_specs=[near, away, away] + [near] * 3,
        scratch_shapes=[
            pltpu.VMEM((8, EMB), f32),
            pltpu.VMEM((5,) + small.shape, f32),
            pltpu.VMEM((5,) + small.shape, f32),
            dma((5,)),
            dma((5,)),
            pltpu.VMEM((2, table_rows, batch // 2), bf16),
            pltpu.VMEM((2, 2, 2, 2, 2, samples, EMB), bf16),
            pltpu.VMEM((table_rows, EMB), f32),
            pltpu.VMEM((2, table_rows, EMB), f32),
            dma((2,)),
            dma((2,)),
            dma((2,)),
        ]
        + scatter_room(slices, chunk // slices, lanes, bf16)
        + spread_room(spread_slices),
        compiler_params=pltpu.CompilerParams(
            collective_id=collective_id, has_side_effects=True, vmem_limit_bytes=61 << 20
        ),
        name="back_exchange",
    )(tiles.reshape(4, 2, 2, 2, chunk, lanes), grads, counts, small)
    return mine, table, total, norm[0, 0], scale[0, 0]


def slot_kernel(scale_ref, tiles_ref, weight_ref, moment_ref, square_ref, weight_out, moment_out, square_out):
    columns = []
    count = tiles_ref.shape[1]
    for h in range(4):
        pieces = [tiles_ref[4 * j + h] for j in range(8)]
        columns.append(jnp.stack(pieces, axis=1).reshape(count, BR, 128))
    gradient = scale_ref[0] * jnp.concatenate(columns, axis=2).astype(jnp.float32)
    weight, moment, square = adamw(weight_ref[...], moment_ref[...], square_ref[...], gradient, rate_dense)
    weight_out[...] = weight
    moment_out[...] = moment
    square_out[...] = square


def slot_update(scale, tiles, weight, moment, square):
    slots = weight.shape[0]
    group = 3
    block = pl.BlockSpec((group, BR, RANK), lambda s: (s, 0, 0))
    return tuple(
        pl.pallas_call(
            slot_kernel,
            grid=(slots // group,),
            in_specs=[
                pl.BlockSpec(memory_space=pltpu.SMEM),
                pl.BlockSpec((32, group, 16, 128), lambda s: (0, s, 0, 0)),
                block,
                block,
                block,
            ],
            out_specs=[block] * 3,
            out_shape=[jax.ShapeDtypeStruct(weight.shape, jnp.float32)] * 3,
            compiler_params=pltpu.CompilerParams(vmem_limit_bytes=48 << 20),
            name="slot_update",
        )(scale.reshape(1), tiles, weight, moment, square)
    )


NN = (((1,), (0,)), ((), ()))
NT = (((1,), (1,)), ((), ()))
TN = (((0,), (0,)), ((), ()))
CHUNKS = 3
CBLK = 9
CW = CBLK * BR
FCH = 9
FBLK = 6
ONE_AT = 6 * CHUNKS * CBLK
TWO_AT = ONE_AT + FCH * FBLK
THREE_AT = TWO_AT + 16
GROUPS = tuple((k * 27, 27) for k in (0, 3, 1, 4, 2, 5)) + ((ONE_AT, 54), (TWO_AT, 16), (THREE_AT, 8))
NDENSE = 13
PROJ_ROW = 1
HEAD_ROW = PROJ_ROW + NDENSE
DENSE_ROW = HEAD_ROW + 4
CROSS_ROW = DENSE_ROW + 1
ONE_ROW = CROSS_ROW + LAYERS * 27
TWO_ROW = ONE_ROW + 8
THREE_ROW = TWO_ROW + 8
LAST_ROW = THREE_ROW + 4
SMALL_ROWS = 128
GELU_A = 0.7978845608028654
GELU_B = 0.044715


def mul(left, right, dims):
    return lax.dot_general(left, right, dims, preferred_element_type=jnp.float32)


def gelu_of(value):
    return 0.5 * value * (1.0 + jnp.tanh(GELU_A * (value + GELU_B * (value * value * value))))


def gelu_slope(value):
    bend = jnp.tanh(GELU_A * (value + GELU_B * (value * value * value)))
    inner = GELU_A * (1.0 + 3.0 * GELU_B * (value * value))
    return 0.5 * (1.0 + bend) + 0.5 * value * (1.0 - bend * bend) * inner


def dense_kernel(
    batch, early_hbm, tiles_hbm, pooled_ref, feats_ref, dense_ref, label_ref, head_ref, last_ref, cross_bias_ref, one_bias_ref,
    two_bias_ref, three_bias_ref, grads_hbm, grad_pooled_ref, small_ref,
    tiles, anchor, current, mixing, low, grad_anchor, wide_one, wide_two, stage, load_sem, store_sem,
):
    samples = dense_ref.shape[0]
    bf16, f32 = jnp.bfloat16, jnp.float32

    def load(group):
        first, count = GROUPS[group]
        early = early_hbm.shape[1]
        late = tiles.shape[1] - tiles_hbm.shape[1]
        source, at = (early_hbm, first) if first < early else (tiles_hbm, first - late)
        return pltpu.make_async_copy(
            source.at[:, pl.ds(at, count)], tiles.at[:, pl.ds(first, count)], load_sem.at[group]
        )

    for group in range(len(GROUPS)):
        load(group).start()

    def matrix(first, count):
        columns = []
        for h in range(4):
            pieces = [tiles[4 * j + h, pl.ds(first, count)] for j in range(8)]
            columns.append(jnp.stack(pieces, axis=1).reshape(count * BR, 128))
        return jnp.concatenate(columns, axis=1)

    def store(slot, first, count):
        return pltpu.make_async_copy(
            stage.at[slot, :, pl.ds(0, count)], grads_hbm.at[:, pl.ds(first, count)], store_sem.at[slot]
        )

    def emit(slot, first, count, value):
        value = value.astype(bf16).reshape(count, BR, RANK)
        for j in range(8):
            for h in range(4):
                stage[slot, 4 * j + h, pl.ds(0, count)] = value[:, 16 * j : 16 * j + 16, 128 * h : 128 * h + 128]
        store(slot, first, count).start()

    small_ref[...] = jnp.zeros_like(small_ref)

    def note(row, value):
        for m in range(value.shape[1] // 128):
            small_ref[pl.ds(row + m, 1), :] = value[:, m * 128 : (m + 1) * 128]

    for i in range(F + 1):
        block = dense_ref[...] if i == 0 else pooled_ref[(i - 1) * EMB : i * EMB, :].astype(f32).T
        c, at = i // CBLK, (i % CBLK) * BR
        anchor[c, :, at : at + BR] = block
        current[c, :, at : at + BR] = block
        low[c, :, at : at + BR] = block.astype(bf16)

    reduced = []
    for depth in range(LAYERS):
        load(2 * depth).wait()
        down, up = depth * 27, (LAYERS + depth) * 27
        total = lax.fori_loop(
            0,
            CHUNKS,
            lambda c, acc: acc + mul(low[depth * CHUNKS + c], matrix(down + c * CBLK, CBLK), NN),
            jnp.zeros((samples, RANK), f32),
        )
        small = total.astype(bf16)
        reduced.append(small)
        load(2 * depth + 1).wait()

        @pl.loop(0, CHUNKS)
        def mix(c):
            value = mul(small, matrix(up + c * CBLK, CBLK), NT) + cross_bias_ref[pl.ds(depth * CHUNKS + c, 1), :]
            mixing[depth * CHUNKS + c] = value
            after = anchor[c] * value + current[c]
            current[c] = after
            if depth + 1 < LAYERS:
                low[(depth + 1) * CHUNKS + c] = after.astype(bf16)

    at_row = lax.broadcasted_iota(jnp.int32, (BR, 4 * BR), 0)
    at_col = lax.broadcasted_iota(jnp.int32, (BR, 4 * BR), 1)
    widen = jnp.where(at_col % (2 * BR) == 2 * at_row + at_col // (2 * BR), 1.0, 0.0).astype(bf16)
    pick_row = lax.broadcasted_iota(jnp.int32, (8 * BR, BR), 0)
    pick_col = lax.broadcasted_iota(jnp.int32, (8 * BR, BR), 1)
    pick = jnp.where(pick_row % (2 * BR) == 2 * pick_col + pick_row // (4 * BR), 1.0, 0.0).astype(bf16)

    def widened(block):
        spreaded = mul(block, widen, NN).astype(bf16)
        return jnp.concatenate([spreaded[:, : 2 * BR], spreaded[:, 2 * BR :]], axis=0)

    def narrowed(wide):
        parts = []
        for p in range(2):
            value = wide[p * samples : (p + 1) * samples]
            high = value.astype(bf16)
            parts += [high, (value - high.astype(f32)).astype(bf16)]
        return mul(jnp.concatenate(parts, axis=1), pick, NN)

    load(6).wait()

    def first_step(c, acc):
        for m in range(3):
            at = pl.multiple_of((c % 3) * 3 * BR + m * BR, BR)
            wide_one[c, :, m * 2 * BR : (m + 1) * 2 * BR] = widened(current[c // 3, :, pl.ds(at, BR)].astype(bf16))
        return acc + mul(wide_one[c], matrix(ONE_AT + c * FBLK, FBLK), NN)

    total = lax.fori_loop(0, FCH, first_step, jnp.zeros((2 * samples, RANK), f32))
    pre_one = [total[p * samples : (p + 1) * samples] + one_bias_ref[pl.ds(p, 1), :] for p in range(2)]
    load(7).wait()
    total = jnp.zeros((2 * samples, RANK), f32)
    for c in range(2):
        hidden = gelu_of(pre_one[c]).astype(bf16)
        for m in range(4):
            wide_two[c, :, m * 2 * BR : (m + 1) * 2 * BR] = widened(hidden[:, m * BR : (m + 1) * BR])
        total = total + mul(wide_two[c], matrix(TWO_AT + c * 8, 8), NN)
    pre_two = [total[p * samples : (p + 1) * samples] + two_bias_ref[pl.ds(p, 1), :] for p in range(2)]
    load(8).wait()
    hidden_two = jnp.concatenate([gelu_of(value).astype(bf16) for value in pre_two], axis=1)
    pre_three = mul(hidden_two, matrix(THREE_AT, 8), NN) + three_bias_ref[...]
    hidden_three = gelu_of(pre_three)
    head = head_ref[...]
    logits = jnp.sum(hidden_three * head, axis=1, keepdims=True) + last_ref[...]
    labels = label_ref[...]
    losses = jnp.maximum(logits, 0.0) + jnp.log1p(jnp.exp(-jnp.abs(logits))) - labels * logits
    grad_logits = (1.0 / (1.0 + jnp.exp(-logits)) - labels) / batch
    first_lane = lax.broadcasted_iota(jnp.int32, (1, 128), 1) == 0
    note(0, jnp.where(first_lane, jnp.sum(losses, axis=0, keepdims=True), 0.0))
    note(LAST_ROW, jnp.where(first_lane, jnp.sum(grad_logits, axis=0, keepdims=True), 0.0))
    note(HEAD_ROW, jnp.sum(hidden_three * grad_logits, axis=0, keepdims=True))

    grad_before = grad_logits * head * gelu_slope(pre_three)
    note(THREE_ROW, jnp.sum(grad_before, axis=0, keepdims=True))
    grad_low = grad_before.astype(bf16)
    emit(0, THREE_AT, 8, mul(hidden_two, grad_low, TN))
    grad_hidden = mul(grad_low, matrix(THREE_AT, 8), NT)
    parts = []
    for p in range(2):
        grad_before = grad_hidden[:, p * RANK : (p + 1) * RANK] * gelu_slope(pre_two[p])
        note(TWO_ROW + 4 * p, jnp.sum(grad_before, axis=0, keepdims=True))
        parts.append(grad_before.astype(bf16))
    grad_low = jnp.concatenate(parts, axis=0)
    parts = []
    for c in range(2):
        if c == 1:
            store(0, THREE_AT, 8).wait()
        emit(1 - c, TWO_AT + c * 8, 8, mul(wide_two[c], grad_low, TN))
        wide = mul(grad_low, matrix(TWO_AT + c * 8, 8), NT)
        grad_hidden = jnp.concatenate(
            [narrowed(wide[:, m * 2 * BR : (m + 1) * 2 * BR]) for m in range(4)], axis=1
        )
        grad_before = grad_hidden * gelu_slope(pre_one[c])
        note(ONE_ROW + 4 * c, jnp.sum(grad_before, axis=0, keepdims=True))
        parts.append(grad_before.astype(bf16))
    grad_one = jnp.concatenate(parts, axis=0)
    store(1, TWO_AT, 8).wait()
    store(0, TWO_AT + 8, 8).wait()

    @pl.loop(0, FCH)
    def first_back(c):
        slot = c % 2
        at = ONE_AT + c * FBLK

        @pl.when(c >= 2)
        def ready():
            store(slot, at, FBLK).wait()

        emit(slot, at, FBLK, mul(wide_one[c], grad_one, TN))
        wide = mul(grad_one, matrix(at, FBLK), NT)
        for m in range(3):
            spot = pl.multiple_of((c % 3) * 3 * BR + m * BR, BR)
            current[c // 3, :, pl.ds(spot, BR)] = narrowed(wide[:, m * 2 * BR : (m + 1) * 2 * BR])

    for slot in range(2):
        store(slot, ONE_AT, FBLK).wait()

    sent = 0
    for depth in reversed(range(LAYERS)):
        down, up = depth * 27, (LAYERS + depth) * 27
        base = sent

        def up_back(c, acc):
            slot = (base + c) % 2
            before = current[c]
            grad_mixing = anchor[c] * before
            note(CROSS_ROW + depth * 27 + c * CBLK, jnp.sum(grad_mixing, axis=0, keepdims=True))
            grad_low = grad_mixing.astype(bf16)

            @pl.when(base + c >= 2)
            def ready():
                store(slot, up, CBLK).wait()

            emit(slot, up + c * CBLK, CBLK, mul(grad_low, reduced[depth], TN))
            part = before * mixing[depth * CHUNKS + c]
            grad_anchor[c] = part if depth == LAYERS - 1 else grad_anchor[c] + part
            return acc + mul(grad_low, matrix(up + c * CBLK, CBLK), NN)

        total = lax.fori_loop(0, CHUNKS, up_back, jnp.zeros((samples, RANK), f32))
        grad_reduced = total.astype(bf16)

        @pl.loop(0, CHUNKS)
        def down_back(c):
            slot = (base + CHUNKS + c) % 2
            store(slot, down, CBLK).wait()
            emit(slot, down + c * CBLK, CBLK, mul(low[depth * CHUNKS + c], grad_reduced, TN))
            after = current[c] + mul(grad_reduced, matrix(down + c * CBLK, CBLK), NT)
            current[c] = after
            if depth == 0:
                grad_anchor[c] = grad_anchor[c] + after

        sent += 2 * CHUNKS
    grad_dense = grad_anchor[0, :, :EMB]
    note(DENSE_ROW, jnp.sum(grad_dense, axis=0, keepdims=True))
    small_ref[PROJ_ROW : PROJ_ROW + NDENSE, :] = lax.dot_general(
        feats_ref[...], grad_dense, TN, precision=highest, preferred_element_type=f32
    )[:NDENSE]
    for i in range(1, F + 1):
        c, at = i // CBLK, (i % CBLK) * BR
        grad_pooled_ref[i - 1] = grad_anchor[c, :, at : at + BR].astype(bf16)
    for slot in range(2):
        store(slot, 0, CBLK).wait()


def dense_step(early, tiles, pooled, feats, dense_part, labels, head, bias_last, bias_cross, bias_one, bias_two, bias_three, batch):
    samples = dense_part.shape[0]
    block_count = THREE_AT + 8
    f32, bf16 = jnp.float32, jnp.bfloat16
    whole = pl.BlockSpec(memory_space=pltpu.VMEM)
    away = pl.BlockSpec(memory_space=pl.ANY)
    shape = jax.ShapeDtypeStruct
    return pl.pallas_call(
        functools.partial(dense_kernel, batch),
        out_shape=[
            shape((32, block_count, 16, 128), bf16),
            shape((F, samples, EMB), bf16),
            shape((SMALL_ROWS, 128), f32),
        ],
        in_specs=[away] * 2 + [whole] * 10,
        out_specs=[away] + [whole] * 2,
        scratch_shapes=[
            pltpu.VMEM((32, block_count, 16, 128), bf16),
            pltpu.VMEM((CHUNKS, samples, CW), f32),
            pltpu.VMEM((CHUNKS, samples, CW), f32),
            pltpu.VMEM((LAYERS * CHUNKS, samples, CW), f32),
            pltpu.VMEM((LAYERS * CHUNKS, samples, CW), bf16),
            pltpu.VMEM((CHUNKS, samples, CW), f32),
            pltpu.VMEM((FCH, 2 * samples, FBLK * BR), bf16),
            pltpu.VMEM((2, 2 * samples, 8 * BR), bf16),
            pltpu.VMEM((2, 32, CBLK, 16, 128), bf16),
            pltpu.SemaphoreType.DMA((len(GROUPS),)),
            pltpu.SemaphoreType.DMA((2,)),
        ],
        compiler_params=pltpu.CompilerParams(vmem_limit_bytes=61 << 20),
        name="dense_step",
    )(early, tiles, pooled, feats, dense_part, labels, head, bias_last, bias_cross, bias_one, bias_two, bias_three)


def body(
    row_ids,
    hot_counts,
    dense_feats,
    click_labels,
    block_owners,
    embed_table,
    table_moment,
    table_square,
    dense_slots,
    dense_moment,
    dense_square,
    dense_proj,
    proj_moment,
    proj_square,
    head_weight,
    head_moment,
    head_square,
    biases,
    bias_moment,
    bias_square,
):
    devices = lax.axis_size("row")
    samples = row_ids.shape[0]
    slot_count = dense_slots.shape[0]
    table_rows = embed_table.shape[1]
    block_count = block_owners.shape[0]
    capacity = samples * TOTAL // devices
    live_total = samples * TOTAL
    everything = lax.all_gather(dense_slots.astype(jnp.bfloat16), "row", axis=0, tiled=True)
    fetched = jnp.take(everything, block_owners, axis=0)
    cross_down, cross_up, first_matrix, middle, third_matrix = split_dense(
        fetched.reshape(block_count * BR, RANK)
    )
    bias_dense, bias_cross, bias_one, bias_two, bias_three, bias_last = split_bias(biases)
    flat_ids = row_ids.reshape(-1)
    live_mask = (
        lax.broadcasted_iota(jnp.int32, row_ids.shape, 2) < hot_counts[:, :, None]
    ).reshape(-1)
    sort_key = jnp.where(live_mask, flat_ids // table_rows, devices)
    full_order = jnp.argsort(sort_key, stable=True)
    slot_place = jnp.argsort(full_order)
    ordering = full_order[:live_total]
    segment = ordering // HOT
    requests = (segment % F * table_rows + jnp.take(flat_ids, ordering) % table_rows).reshape(
        devices, capacity
    )
    flat_table = embed_table.astype(jnp.bfloat16).reshape(F * table_rows, EMB)
    received = lax.all_to_all(requests, "row", split_axis=0, concat_axis=0, tiled=True)
    looked_up = jnp.take(flat_table, received, axis=0)
    returned = lax.all_to_all(looked_up, "row", split_axis=0, concat_axis=0, tiled=True)
    padded_rows = jnp.concatenate(
        [returned.reshape(-1, EMB), jnp.zeros((1, EMB), jnp.bfloat16)], axis=0
    )
    pick = jnp.where(live_mask, slot_place, live_total)
    in_slots = jnp.take(padded_rows, pick, axis=0).reshape(samples, F, HOT, EMB)
    pooled = jnp.sum(in_slots, axis=2, dtype=jnp.float32)
    pooled_low = pooled.astype(jnp.bfloat16).reshape(samples, F * EMB)
    dense_part = (
        jnp.dot(dense_feats, dense_proj, precision=highest, preferred_element_type=jnp.float32)
        + bias_dense
    )
    anchor = jnp.concatenate([dense_part, pooled_low.astype(jnp.float32)], axis=1)
    current = anchor
    stored = []
    for depth in range(LAYERS):
        saved, current = cross_forward(
            anchor, current, cross_down[depth], cross_up[depth], bias_cross[depth]
        )
        stored.append(saved)
    first_saved, hidden = dense_forward(current, first_matrix, bias_one)
    second_saved, hidden = dense_forward(hidden, middle, bias_two)
    third_saved, hidden = dense_forward(hidden, third_matrix, bias_three)
    logits = (
        jnp.dot(hidden, head_weight, precision=highest, preferred_element_type=jnp.float32)
        + bias_last
    )
    labels = click_labels.astype(jnp.float32)
    loss_local = jnp.sum(jax.nn.softplus(logits) - labels * logits)
    grad_logits = (jax.nn.sigmoid(logits) - labels) / (samples * devices)
    grad_head_local = jnp.dot(
        grad_logits, hidden, precision=highest, preferred_element_type=jnp.float32
    )
    grad_hidden = grad_logits[:, None] * head_weight[None, :]
    grad_hidden, grad_third, grad_bias_three = dense_backward(
        third_saved, third_matrix, grad_hidden
    )
    grad_hidden, grad_middle, grad_bias_two = dense_backward(second_saved, middle, grad_hidden)
    grad_current, grad_first, grad_bias_one = dense_backward(first_saved, first_matrix, grad_hidden)
    grad_anchor = jnp.zeros_like(anchor)
    grads_down = [None] * LAYERS
    grads_up = [None] * LAYERS
    grads_cross = [None] * LAYERS
    for depth in reversed(range(LAYERS)):
        grad_current, grad_part, grads_down[depth], grads_up[depth], grads_cross[depth] = (
            cross_backward(anchor, stored[depth], cross_down[depth], cross_up[depth], grad_current)
        )
        grad_anchor = grad_anchor + grad_part
    grad_anchor = grad_anchor + grad_current
    grad_pooled = grad_anchor[:, EMB:].astype(jnp.bfloat16).reshape(samples * F, EMB)
    sent_back = jnp.take(grad_pooled, segment, axis=0).reshape(devices, capacity, EMB)
    arrived = lax.all_to_all(sent_back, "row", split_axis=0, concat_axis=0, tiled=True)
    grad_table = table_gradient(arrived.reshape(-1, EMB), received.reshape(-1), table_rows)
    grad_proj_local = jnp.einsum(
        "sa,sb->ab",
        dense_feats,
        grad_anchor[:, :EMB],
        precision=highest,
        preferred_element_type=jnp.float32,
    )
    stacked = jnp.concatenate(
        [
            jnp.stack(grads_down).reshape(-1, RANK),
            jnp.stack(grads_up).reshape(-1, RANK),
            grad_first.reshape(-1, RANK),
            grad_middle.reshape(-1, RANK),
            grad_third,
            jnp.zeros((BR, RANK), jnp.float32),
        ],
        axis=0,
    ).reshape(block_count + 1, BR, RANK)
    matches = block_owners[None, :] == jnp.arange(devices * slot_count, dtype=jnp.int32)[:, None]
    inverse = jnp.sum(
        jnp.where(matches, jnp.arange(block_count, dtype=jnp.int32)[None, :], 0), axis=1
    )
    inverse = inverse + jnp.where(jnp.any(matches, axis=1), 0, block_count)
    grad_slots = lax.psum_scatter(
        jnp.take(stacked, inverse, axis=0), "row", scatter_dimension=0, tiled=True
    )
    bias_local = jnp.concatenate(
        [
            jnp.sum(grad_anchor[:, :EMB], axis=0),
            jnp.stack(grads_cross).reshape(-1),
            grad_bias_one,
            grad_bias_two,
            grad_bias_three,
            jnp.sum(grad_logits)[None],
        ]
    )
    loss_total, grad_proj, grad_head, grad_bias = lax.psum(
        (loss_local, grad_proj_local, grad_head_local, bias_local), "row"
    )
    local_squares = jnp.sum(grad_table * grad_table) + jnp.sum(grad_slots * grad_slots)
    squares = lax.psum(local_squares, "row")
    squares = (
        squares
        + jnp.sum(grad_proj * grad_proj)
        + jnp.sum(grad_head * grad_head)
        + jnp.sum(grad_bias * grad_bias)
    )
    grad_norm = jnp.sqrt(squares)
    clip_scale = clip_norm / jnp.maximum(grad_norm, clip_norm)
    table_new = adamw(embed_table, table_moment, table_square, clip_scale * grad_table, rate_table)
    dense_new = adamw(dense_slots, dense_moment, dense_square, clip_scale * grad_slots, rate_dense)
    proj_new = adamw(dense_proj, proj_moment, proj_square, clip_scale * grad_proj, rate_small)
    head_new = adamw(head_weight, head_moment, head_square, clip_scale * grad_head, rate_small)
    bias_new = adamw(biases, bias_moment, bias_square, clip_scale * grad_bias, rate_small)
    return (
        loss_total,
        grad_norm,
        table_new[0],
        table_new[1],
        table_new[2],
        dense_new[0],
        dense_new[1],
        dense_new[2],
        proj_new[0],
        proj_new[1],
        proj_new[2],
        head_new[0],
        head_new[1],
        head_new[2],
        bias_new[0],
        bias_new[1],
        bias_new[2],
    )


def body_counted(
    row_ids,
    hot_counts,
    dense_feats,
    click_labels,
    block_owners,
    embed_table,
    table_moment,
    table_square,
    dense_slots,
    dense_moment,
    dense_square,
    dense_proj,
    proj_moment,
    proj_square,
    head_weight,
    head_moment,
    head_square,
    biases,
    bias_moment,
    bias_square,
):
    devices = lax.axis_size("row")
    samples = row_ids.shape[0]
    slot_count = dense_slots.shape[0]
    table_rows = embed_table.shape[1]
    block_count = block_owners.shape[0]
    capacity = samples * TOTAL // devices
    live_total = samples * TOTAL
    bf16 = jnp.bfloat16
    slot_tiles = (
        dense_slots.astype(bf16)
        .reshape(slot_count, 8, 16, 4, 128)
        .transpose(1, 3, 0, 2, 4)
        .reshape(devices, slot_count * 16, 128)
    )
    slot_tiles = lax.all_to_all(slot_tiles, "row", split_axis=0, concat_axis=0, tiled=True)
    lanes = lax.broadcasted_iota(jnp.int32, row_ids.shape, 2)
    features = lax.broadcasted_iota(jnp.int32, row_ids.shape, 1)
    sample_of = lax.broadcasted_iota(jnp.int32, row_ids.shape, 0)
    key = (
        ((row_ids // table_rows) << 21)
        | (features << 16)
        | ((row_ids % table_rows) << 7)
        | sample_of
    )
    key = jnp.where(lanes < hot_counts[:, :, None], key, devices << 21)
    ordered = lax.sort(key.reshape(-1), is_stable=False)[:live_total]
    block_tiles = jnp.take(
        slot_tiles.reshape(devices * slot_count, 16, 128),
        block_owners + jnp.minimum(ordered[0], 0),
        axis=0,
        mode="clip",
    )
    early_count = 81
    early = lax.all_gather(
        block_tiles[:early_count].reshape(early_count * 16, 128), "row", axis=0, tiled=True
    ).reshape(devices, early_count, 16, 128)
    bias_dense, bias_cross, bias_one, bias_two, bias_three, bias_last = split_bias(biases)
    requests = (ordered & ((1 << 21) - 1)).reshape(devices, capacity)
    received = lax.all_to_all(requests, "row", split_axis=0, concat_axis=0, tiled=True)
    edges = jnp.arange(F + 1, dtype=jnp.int32) << 16
    offsets = jnp.sum((received[:, None, :] < edges[None, :, None]).astype(jnp.int32), axis=2)
    room = (capacity + samples - 1) // samples * samples + samples
    keys = jnp.pad(received, ((0, 0), (0, room - capacity)), constant_values=-1)
    counts, partial = count_tables(offsets, keys, embed_table, devices, samples)
    pooled, tiles = front_exchange(partial, block_tiles[early_count - 1 :], F * EMB, (2, 3) * 8, (2, 3, 4, 5, 8), 10, (1, 2, 3, 4, 5), 3, 0)
    dense_part = (
        jnp.dot(dense_feats, dense_proj, precision=highest, preferred_element_type=jnp.float32)
        + bias_dense
    )
    grad_tiles, grad_pooled, grad_small = dense_step(
        early,
        tiles,
        pooled,
        jnp.pad(dense_feats, ((0, 0), (0, 3))),
        dense_part,
        click_labels.astype(jnp.float32)[:, None],
        head_weight[None, :],
        jnp.broadcast_to(bias_last, (samples, 1)),
        bias_cross.reshape(LAYERS * CHUNKS, CW),
        bias_one.reshape(2, RANK),
        bias_two.reshape(2, RANK),
        bias_three[None, :],
        samples * devices,
    )
    grad_mine, grad_table, small_total, grad_norm, clip_scale = back_exchange(
        grad_tiles.reshape(devices, block_count * 16, 128),
        grad_pooled,
        counts,
        grad_small,
        (2, 3) * 8,
        (2, 3, 4, 5, 8),
        13,
        (1, 2, 3, 4, 5),
        6,
        3,
        1,
    )
    matches = block_owners[None, :] == jnp.arange(devices * slot_count, dtype=jnp.int32)[:, None]
    inverse = jnp.sum(
        jnp.where(matches, jnp.arange(block_count, dtype=jnp.int32)[None, :], 0), axis=1
    )
    named = jnp.any(matches, axis=1)
    returned = jnp.take(
        grad_mine.reshape(block_count, 16, 128), inverse, axis=0, mode="clip"
    )
    returned = jnp.where(named[:, None, None], returned, 0)
    returned = lax.all_to_all(
        returned.reshape(devices, slot_count * 16, 128), "row", split_axis=0, concat_axis=0, tiled=True
    )
    loss_total = small_total[0, 0]
    grad_proj = small_total[PROJ_ROW : PROJ_ROW + NDENSE]
    grad_head = small_total[HEAD_ROW : HEAD_ROW + 4].reshape(-1)
    grad_bias = small_total[DENSE_ROW : LAST_ROW + 1].reshape(-1)[:NBIAS]
    table_new = adamw(embed_table, table_moment, table_square, clip_scale * grad_table, rate_table)
    dense_new = slot_update(
        clip_scale,
        returned.reshape(devices, slot_count, 16, 128),
        dense_slots,
        dense_moment,
        dense_square,
    )
    proj_new = adamw(dense_proj, proj_moment, proj_square, clip_scale * grad_proj, rate_small)
    head_new = adamw(head_weight, head_moment, head_square, clip_scale * grad_head, rate_small)
    bias_new = adamw(biases, bias_moment, bias_square, clip_scale * grad_bias, rate_small)
    return (
        (loss_total, grad_norm) + table_new + dense_new + proj_new + head_new + bias_new
    )


def solution(mesh):
    in_specs = (
        P("row", None, None),
        P("row", None),
        P("row", None),
        P("row"),
        P(),
        P(None, "row", None),
        P(None, "row", None),
        P(None, "row", None),
        P("row", None, None),
        P("row", None, None),
        P("row", None, None),
        P(),
        P(),
        P(),
        P(),
        P(),
        P(),
        P(),
        P(),
        P(),
    )
    out_specs = (
        P(),
        P(),
        P(None, "row", None),
        P(None, "row", None),
        P(None, "row", None),
        P("row", None, None),
        P("row", None, None),
        P("row", None, None),
        P(),
        P(),
        P(),
        P(),
        P(),
        P(),
        P(),
        P(),
        P(),
    )
    fits = mesh.shape["row"] == 32
    chosen = body_counted if fits else body
    return jax.shard_map(chosen, mesh=mesh, in_specs=in_specs, out_specs=out_specs, check_vma=False)
```
